256 devices in a mesh: dp: 16 (over y, x), proto: 16 (over z, core).
Axes of the slice: x: 4, y: 4, z: 8, core: 2. Of those that a mesh axis runs over, the one named last changes fastest.
Arguments:
- teacher_feats: bfloat16 [4096, 256], P('dp', 'proto'), may hold values from -8 to 8
- student_feats: bfloat16 [4096, 256], P('dp', 'proto'), may hold values from -6 to 6
- prototypes: bfloat16 [256, 131072], P('dp', 'proto'), may hold values from -0.5 to 0.5
Outputs:
- loss: float32 [], replicated
- grad_proto: float32 [256, 131072], P('dp', 'proto')
- grad_student: float32 [4096, 256], P('dp', 'proto')
The draws below stay inside these ranges and needn't reach their ends.
All inputs are finite; a program needn't handle non-finite values.
Results may differ from the reference program's by a relative error of at most 0.00045.
The reference program's roundings to bfloat16 on the way (of `t_unit`, `s_unit`, `w_unit` and `grad_logits`) count: a program that leaves them out, or rounds other values in their place, can miss the bound.
Values may be sent and summed in bfloat16 or wider, within the bound.
A program may use at most 64 MiB of HBM per device.

```python
import math
import jax
import jax.numpy as jnp
from jax import lax

D = 256
PROTOS = 131072
ROW_DEV = 256
ITERS = 3
ROWS = 4096
LOSS_SCALE = 2097152


def cluster_centers(key):
    center_key = jax.random.fold_in(key, 101)
    return jnp.clip(jax.random.normal(center_key, (16, D), jnp.float32), -4.0, 4.0)


def draw_teacher_feats(key, part):
    centers = cluster_centers(key)
    key = jax.random.fold_in(key, 7)
    id_key, mate_key, jitter_key, scale_key = jax.random.split(key, 4)
    chosen = jnp.minimum(jax.random.randint(id_key, (ROWS,), 0, 16), jax.random.randint(mate_key, (ROWS,), 0, 16))
    jitter = jnp.clip(jax.random.normal(jitter_key, (ROWS, D), jnp.float32), -4.0, 4.0)
    strength = 0.62
    scales = jnp.exp(jax.random.uniform(scale_key, (ROWS, 1), jnp.float32, -1.15, 1.15))
    return jnp.clip((strength * centers[chosen] + jitter) * scales, -8.0, 8.0).astype(jnp.bfloat16)


def draw_prototypes(key, part):
    centers = cluster_centers(key)
    key = jax.random.fold_in(key, 11)
    id_key, jitter_key, scale_key = jax.random.split(key, 3)
    owners = jax.random.randint(id_key, (PROTOS,), 0, 16)
    jitter = jnp.clip(jax.random.normal(jitter_key, (D, PROTOS), jnp.float32), -4.0, 4.0)
    strength = 0.62
    scales = jnp.exp(jax.random.uniform(scale_key, (1, PROTOS), jnp.float32, -1.15, 1.15)) / math.sqrt(D)
    return jnp.clip((strength * centers[owners].T + jitter) * scales, -0.5, 0.5).astype(jnp.bfloat16)


def steps_of(stream_key, extent, cuts, smallest, top_value):
    factor_of = 1.0
    for dim, shards_of in cuts:
        draws = jax.random.uniform(jax.random.fold_in(jax.random.fold_in(stream_key, 6), dim), (shards_of,), jnp.float32, smallest / len(cuts), top_value / len(cuts))
        factor_of = factor_of * jnp.repeat(jnp.exp(draws), extent[dim] // shards_of).reshape((-1,) + (1,) * (len(extent) - 1 - dim))
    return factor_of


def bell_draw(key, shape, scale, limit, shards=(), held_as=jnp.bfloat16):
    drawn = jax.random.normal(key, shape, jnp.float32) * scale
    if len(shards) > 0:
        drawn = steps_of(key, shape, shards, -0.22, 0.18) * drawn
    return jnp.clip(drawn, min=-limit, max=limit).astype(held_as)


def setup_inputs(seed: int = 0) -> dict:
    key_of = jax.random.split(jax.random.key(seed), 4)
    teacher_feats = draw_teacher_feats(jax.random.fold_in(key_of[3], 71), 0)
    student_feats = bell_draw(key_of[1], (ROWS, D), 1.0, 6.0, ((0, 16), (1, 16)))
    prototypes = draw_prototypes(jax.random.fold_in(key_of[3], 71), 0)
    return dict(teacher_feats=teacher_feats, student_feats=student_feats, prototypes=prototypes)


eps = 1e-06
teacher_temp = 0.07
student_temp = 0.1

def reference(teacher_feats, student_feats, prototypes):
    t32 = teacher_feats.astype(jnp.float32)
    t_unit = (t32 * lax.rsqrt(lax.optimization_barrier(jnp.sum(t32 * t32, axis=1, keepdims=True)) + eps)).astype(jnp.bfloat16)
    s32 = student_feats.astype(jnp.float32)
    s_inv = lax.rsqrt(lax.optimization_barrier(jnp.sum(s32 * s32, axis=1, keepdims=True)) + eps)
    s_unit32 = s32 * s_inv
    s_unit = s_unit32.astype(jnp.bfloat16)
    w32 = prototypes.astype(jnp.float32)
    w_inv = lax.rsqrt(lax.optimization_barrier(jnp.sum(w32 * w32, axis=0, keepdims=True)) + eps)
    w_unit32 = w32 * w_inv
    w_unit = w_unit32.astype(jnp.bfloat16)
    blocks = ROWS // ROW_DEV
    t_blocks = t_unit.reshape(blocks, ROW_DEV, D)

    def teacher_block(rows_in):
        return jnp.exp(jnp.dot(rows_in, w_unit, preferred_element_type=jnp.float32) / teacher_temp)
    base = lax.map(teacher_block, t_blocks)
    row_scale = jnp.ones((blocks, ROW_DEV), jnp.float32)
    col_scale = jnp.ones((PROTOS,), jnp.float32)
    for step in range(ITERS):
        col_scale = 1.0 / jnp.einsum('abk,ab->k', base, row_scale, precision=lax.Precision.HIGHEST)
        row_scale = 1.0 / jnp.einsum('abk,k->ab', base, col_scale, precision=lax.Precision.HIGHEST)
    factor = float(LOSS_SCALE) / float(ROWS) / student_temp
    w_unit_t = w_unit.T

    def student_block(carry, inputs):
        grad_wunit, loss_sum = carry
        base_blk, scale_blk, s_blk, s32_blk, sinv_blk = inputs
        logits = jnp.dot(s_blk, w_unit, preferred_element_type=jnp.float32) / student_temp
        expo = jnp.exp(logits)
        totals = lax.optimization_barrier(jnp.sum(expo, axis=1, keepdims=True))
        targets = base_blk * scale_blk[:, None] * col_scale[None, :]
        loss_sum = loss_sum + jnp.sum(targets * (logits - jnp.log(totals)))
        grad_logits = ((expo / totals - targets) * factor).astype(jnp.bfloat16)
        grad_wunit = grad_wunit + jnp.dot(s_blk.T, grad_logits, preferred_element_type=jnp.float32)
        grad_sunit = jnp.dot(grad_logits, w_unit_t, preferred_element_type=jnp.float32)
        dots = lax.optimization_barrier(jnp.sum(s32_blk * grad_sunit, axis=1, keepdims=True))
        return ((grad_wunit, loss_sum), sinv_blk * (grad_sunit - s32_blk * dots))
    start = (jnp.zeros((D, PROTOS), jnp.float32), jnp.zeros((), jnp.float32))
    inputs = (base, row_scale, s_unit.reshape(blocks, ROW_DEV, D), s_unit32.reshape(blocks, ROW_DEV, D), s_inv.reshape(blocks, ROW_DEV, 1))
    (grad_wunit, loss_sum), grad_rows = lax.scan(student_block, start, inputs)
    loss = -loss_sum / float(ROWS)
    col_dots = lax.optimization_barrier(jnp.sum(w_unit32 * grad_wunit, axis=0, keepdims=True))
    grad_proto = w_inv * (grad_wunit - w_unit32 * col_dots)
    grad_student = grad_rows.reshape(ROWS, D)
    return (loss, grad_proto, grad_student)
```

```python
import functools

import jax
import jax.numpy as jnp
from jax import lax
from jax.experimental import pallas as pl
from jax.experimental.pallas import tpu as pltpu
from jax.sharding import PartitionSpec as P

ITERS = 3
EPS = 1e-06
TEACHER_TEMP = 0.07
STUDENT_TEMP = 0.1
MESH = pl.DeviceIdType.MESH
F32 = jnp.float32
BF16 = jnp.bfloat16


def rcopy(src, dst, send_sem, recv_sem, dev):
    return pltpu.make_async_remote_copy(
        src_ref=src, dst_ref=dst, send_sem=send_sem, recv_sem=recv_sem,
        device_id=dev, device_id_type=MESH,
    )


def each(lo, hi, fn):
    def step(k, carry):
        fn(k)
        return carry
    lax.fori_loop(lo, hi, step, 0)


def dot(a, b, dims=((1,), (0,))):
    return lax.dot_general(a, b, (dims, ((), ())), preferred_element_type=F32)


def kernel(
    cfg, x_ref, w_ref, loss_ref, gp_ref, gs_ref,
    feats, wraw, wn, wtn, sn, base, logit, acc, colb, rscale, tots, gbuf, lossv,
    core_col, plane_row, z_row, gw, gw_in, gp_all,
    part_a, part_b, in_a, in_b, sum_a, sum_b, in_a2, in_b2, msg, msg_in, plane_loss,
    f_send, f_recv, w_send, w_recv, wc_sem, t_send, t_recv, s_send, s_recv,
    cc_send, cc_recv, pr_send, pr_recv, zr_send, zr_recv, gw_sem, gp_send, gp_recv,
    a_send, a_recv, b_send, b_recv, a2_send, a2_recv, b2_send, b2_recv,
    m_send, m_recv, l_send, l_recv,
):
    NP, NJ, NY, NX, factor, inv_rows = cfg
    NZ = NJ // 2
    DB = x_ref.shape[1]
    SH = x_ref.shape[2] // 2
    CB = wraw.shape[2]
    D = DB * NJ
    DH = D // 2
    PC = 2 * CB
    CH = min(256, CB)
    HX = NX // 2
    p = lax.axis_index("dp")
    j = lax.axis_index("proto")
    y, x = p // NX, lax.rem(p, NX)
    z, c = j // 2, lax.rem(j, 2)
    oc = 1 - c
    peer = (p, 2 * z + oc)

    def dp_of(yy, xx):
        return yy * NX + xx

    def nxt(v, k, n):
        return lax.rem(v + k, n)

    barrier = pltpu.get_barrier_semaphore()

    def greet_dp(k):
        pl.semaphore_signal(barrier, inc=1, device_id=(nxt(p, k, NP), j), device_id_type=MESH)

    def greet_proto(k):
        pl.semaphore_signal(barrier, inc=1, device_id=(p, nxt(j, k, NJ)), device_id_type=MESH)

    each(1, NP, greet_dp)
    each(1, NJ, greet_proto)
    pl.semaphore_wait(barrier, NP + NJ - 2)

    def half(cc):
        return x_ref.at[:, :, pl.ds(pl.multiple_of(cc * SH, SH), SH)]

    my_rows = pl.ds(pl.multiple_of(j * DB, DB), DB)

    def feat_copy(k):
        q = nxt(j, k, NJ)
        return rcopy(half(lax.rem(q, 2)), feats.at[:, y, x, my_rows], f_send.at[q], f_recv.at[j], (p, q))

    each(1, NJ, lambda k: feat_copy(k).start())

    w_rows = pl.ds(pl.multiple_of(p * DB, DB), DB)

    def w_copy(k):
        q = nxt(p, k, NP)
        cols = pl.ds(pl.multiple_of(q * CB, CB), CB)
        return rcopy(w_ref.at[:, cols], wraw.at[c, w_rows], w_send.at[q], w_recv.at[p], (q, j))

    each(1, NP, lambda k: w_copy(k).start())
    feats[:, y, x, my_rows, :] = x_ref[:, :, pl.ds(pl.multiple_of(c * SH, SH), SH)]
    wraw[c, w_rows, :] = w_ref[:, pl.ds(pl.multiple_of(p * CB, CB), CB)]

    def feat_wait(k):
        q = nxt(j, k, NJ)
        rows = pl.ds(pl.multiple_of(q * DB, DB), DB)
        rcopy(half(0), feats.at[:, y, x, rows], f_send.at[q], f_recv.at[q], (p, q)).wait_recv()

    each(1, NJ, feat_wait)

    def t_copy(xs, n, dev):
        slot = feats.at[0, y, xs]
        return rcopy(slot, slot, t_send.at[n], t_recv.at[y, xs], dev)

    def s_copy(ys, n, dev):
        slot = feats.at[1, ys, x]
        return rcopy(slot, slot, s_send.at[n], s_recv.at[ys, x], dev)

    def t_wait(yy, xx):
        slot = feats.at[0, yy, xx]
        rcopy(slot, slot, t_send.at[0], t_recv.at[yy, xx], peer).wait_recv()

    def s_wait(yy, xx):
        slot = feats.at[1, yy, xx]
        rcopy(slot, slot, s_send.at[0], s_recv.at[yy, xx], peer).wait_recv()

    def own_out(k):
        xq, yq = nxt(x, k, NX), nxt(y, k, NY)
        t_copy(x, k - 1, (dp_of(y, xq), j)).start()
        s_copy(y, k - 1, (dp_of(yq, x), j)).start()
        t_copy(x, NX - 2 + k, (dp_of(yq, x), j)).start()
        s_copy(y, NY - 2 + k, (dp_of(y, xq), j)).start()

    each(1, NX, own_out)

    def w_wait(k):
        q = nxt(p, k, NP)
        rows = pl.ds(pl.multiple_of(q * DB, DB), DB)
        rcopy(w_ref.at[:, pl.ds(0, CB)], wraw.at[c, rows], w_send.at[q], w_recv.at[q], (q, j)).wait_recv()

    each(1, NP, w_wait)
    w_core = rcopy(wraw.at[c], wraw.at[c], wc_sem.at[0], wc_sem.at[1], peer)
    w_core.start()

    def forward(k):
        xs, ys = nxt(x, k, NX), nxt(y, k, NY)
        t_wait(y, xs)
        n0 = 2 * (NX - 1) + (k - 1) * (NX - 1) - 1

        def fwd_t(m):
            t_copy(xs, n0 + m, (dp_of(nxt(y, m, NY), x), j)).start()

        each(1, NY, fwd_t)
        s_wait(ys, x)

        def fwd_s(m):
            s_copy(ys, n0 + m, (dp_of(y, nxt(x, m, NX)), j)).start()

        each(1, NX, fwd_s)

    each(1, NX, forward)

    def unit_cols(v):
        v32 = v.astype(F32)
        inv = lax.rsqrt(jnp.sum(v32 * v32, axis=0, keepdims=True) + EPS)
        return v32 * inv, inv

    def w_norm(cc):
        for h in range(CB // CH):
            u, _ = unit_cols(wraw[cc, :, h * CH:(h + 1) * CH])
            wn[cc, :, h * CH:(h + 1) * CH] = u.astype(BF16)
            wtn[cc, h * CH:(h + 1) * CH, :] = u.T.astype(BF16)

    w_norm(c)
    w_core.wait_recv()
    w_norm(oc)

    chunks = [(cc, h) for cc in range(2) for h in range(CB // CH)]

    def two(a):
        return jnp.concatenate([a, a], axis=1)

    acc[...] = jnp.zeros_like(acc)

    def teacher_rows(k):
        yy = nxt(y, k, NY)

        @pl.when(k > 0)
        def _():
            each(0, NX, lambda xx: t_wait(yy, xx))

        def pair(xp):
            b = yy * HX + xp
            raw = jnp.concatenate([feats[0, yy, 2 * xp], feats[0, yy, 2 * xp + 1]], axis=1)
            u, _ = unit_cols(raw)
            tn = u.astype(BF16)
            for i, (cc, h) in enumerate(chunks):
                rows = slice(i * CH, (i + 1) * CH)
                e = jnp.exp(dot(wtn[cc, h * CH:(h + 1) * CH, :], tn) * (1.0 / TEACHER_TEMP))
                base[b, rows, :] = e
                acc[rows, :] += e[:, :SH] + e[:, SH:]

        each(0, HX, pair)

    each(0, NY, teacher_rows)

    def student_rows(k):
        yy = nxt(y, k, NY)

        def pair(xp):
            b = yy * HX + xp

            def arrive(xx):
                @pl.when(jnp.logical_and(k >= 0, xx != x))
                def _():
                    s_wait(yy, xx)

            arrive(2 * xp)
            arrive(2 * xp + 1)
            raw = jnp.concatenate([feats[1, yy, 2 * xp], feats[1, yy, 2 * xp + 1]], axis=1)
            u, _ = unit_cols(raw)
            un = u.astype(BF16)
            sn[b] = un
            part = jnp.zeros((8, 2 * SH), F32)
            for i, (cc, h) in enumerate(chunks):
                rows = slice(i * CH, (i + 1) * CH)
                v = dot(wtn[cc, h * CH:(h + 1) * CH, :], un) * (1.0 / STUDENT_TEMP)
                logit[b, rows, :] = v
                part = part + jnp.sum(jnp.exp(v).reshape(CH // 8, 8, 2 * SH), axis=0)
            tot = jnp.sum(part, axis=0, keepdims=True)
            q = yy * NX + 2 * xp
            tots[pl.ds(q, 1), :] = tot[:, :SH]
            tots[pl.ds(q + 1, 1), :] = tot[:, SH:]

        each(0, HX, pair)

    def col_exchange(r):
        for i in range(PC // 128):
            core_col[r, c, :, i * 128:(i + 1) * 128] = jnp.sum(
                acc[i * 128:(i + 1) * 128, :].T, axis=0, keepdims=True)
        cp = rcopy(core_col.at[r, c], core_col.at[r, c], cc_send.at[r], cc_recv.at[r], peer)
        cp.start()
        cp.wait_recv()
        for i in range(PC // 128):
            s = slice(i * 128, (i + 1) * 128)
            v = 1.0 / (core_col[r, 0, :, s] + core_col[r, 1, :, s])
            colb[s, :] = jnp.broadcast_to(v, (128, 128)).T

    def col_pass():
        scale = rscale[...]

        def block(i):
            rows = pl.ds(pl.multiple_of(i * 64, 64), 64)
            a = jnp.zeros((64, SH), F32)
            for b in range(NP // 2):
                for h in range(2):
                    a = a + base[b, rows, h * SH:(h + 1) * SH] * scale[2 * b + h:2 * b + h + 1, :]
            acc[rows, :] = a

        each(0, PC // 64, block)

    def row_pass(r):
        def pair(b):
            for h in range(2):
                a = jnp.zeros((8, SH), F32)
                for i in range(PC // 64):
                    rows = slice(i * 64, (i + 1) * 64)
                    v = base[b, rows, h * SH:(h + 1) * SH] * colb[rows, :]
                    a = a + jnp.sum(v.reshape(8, 8, SH), axis=0)
                plane_row[r, p, pl.ds(2 * b + h, 1), :] = jnp.sum(a, axis=0, keepdims=True)

        each(0, NP // 2, pair)

    def row_exchange(r, between=None):
        n = 2 * NP if r == 1 else NP
        if r == 1:
            plane_row[r, p, NP:, :] = tots[...]

        def plane_copy(q, src):
            slot = plane_row.at[r, src, pl.ds(0, n)]
            return rcopy(slot, slot, pr_send.at[r, q], pr_recv.at[r, src], (q, j))

        each(1, NP, lambda k: plane_copy(nxt(p, k, NP), p).start())
        if between is not None:
            between()

        def plane_wait(k):
            q = nxt(p, k, NP)
            plane_copy(q, q).wait_recv()

        each(1, NP, plane_wait)
        total = plane_row[r, 0, :n, :]
        for q in range(1, NP):
            total = total + plane_row[r, q, :n, :]
        z_row[r, z, :n, :] = total

        def z_copy(q, src):
            slot = z_row.at[r, src, pl.ds(0, n)]
            return rcopy(slot, slot, zr_send.at[r, q], zr_recv.at[r, src], (p, 2 * q + c))

        each(1, NZ, lambda k: z_copy(nxt(z, k, NZ), z).start())

        def z_wait(k):
            q = nxt(z, k, NZ)
            z_copy(q, q).wait_recv()

        each(1, NZ, z_wait)
        total = z_row[r, 0, :n, :]
        for q in range(1, NZ):
            total = total + z_row[r, q, :n, :]
        rscale[...] = 1.0 / total[:NP]
        if r == 1:
            tots[...] = total[NP:]

    for r in range(ITERS):
        if r > 0:
            col_pass()
        col_exchange(r)
        row_pass(r)
        row_exchange(r, (lambda: each(0, NY, student_rows)) if r == 0 else None)

    lossv[...] = jnp.zeros_like(lossv)
    gw[...] = jnp.zeros_like(gw)

    def row_of(ref, q):
        return jnp.concatenate([ref[pl.ds(q, 1), :], ref[pl.ds(q + 1, 1), :]], axis=1)

    def a_copy(yy, xp, src_y):
        xs = pl.ds(2 * xp, 2)
        n = yy * HX + xp
        m = src_y * HX + xp
        return rcopy(part_a.at[yy, xs], in_a.at[src_y, xs], a_send.at[n], a_recv.at[m], (dp_of(yy, x), j))

    def b_copy(xx, yy, src_x):
        return rcopy(part_b.at[xx, yy], in_b.at[src_x, yy], b_send.at[xx, yy], b_recv.at[src_x, yy], (dp_of(y, xx), j))

    def grad_rows(k):
        yy = nxt(y, k + 1, NY)

        def pair(xp):
            b = yy * HX + xp
            q = yy * NX + 2 * xp
            rs = row_of(rscale, q)
            tot = row_of(tots, q)
            inv_tot = 1.0 / tot
            log_tot = jnp.log(tot)
            lsum = jnp.zeros((8, 2 * SH), F32)
            for i in range(PC // CH):
                rows = slice(i * CH, (i + 1) * CH)
                lg = logit[b, rows, :]
                target = base[b, rows, :] * rs * two(colb[rows, :])
                lsum = lsum + jnp.sum((target * (lg - log_tot)).reshape(CH // 8, 8, 2 * SH), axis=0)
                gbuf[rows, :] = ((jnp.exp(lg) * inv_tot - target) * factor).astype(BF16)
            lossv[...] += lsum[:, :SH] + lsum[:, SH:]
            gs = dot(wn[0], gbuf[:CB, :]) + dot(wn[1], gbuf[CB:, :])
            part_a[yy, 2 * xp] = gs[:DH, :SH]
            part_a[yy, 2 * xp + 1] = gs[:DH, SH:]
            part_b[2 * xp, yy] = gs[DH:, :SH]
            part_b[2 * xp + 1, yy] = gs[DH:, SH:]

            @pl.when(k < NY - 1)
            def _():
                a_copy(yy, xp, y).start()

            for h in range(2):
                @pl.when(2 * xp + h != x)
                def _():
                    b_copy(2 * xp + h, yy, x).start()

            un = sn[b]
            for i, (cc, h) in enumerate(chunks):
                gw[cc, :, h * CH:(h + 1) * CH] += dot(un, gbuf[i * CH:(i + 1) * CH, :], ((1,), (1,)))

        each(0, HX, pair)

    each(0, NY, grad_rows)

    gw_copy = rcopy(gw.at[oc], gw_in, gw_sem.at[0], gw_sem.at[1], peer)
    gw_copy.start()

    plane_loss[p] = lossv[...]

    def l_copy(q, src):
        slot = plane_loss.at[src]
        return rcopy(slot, slot, l_send.at[q], l_recv.at[src], (q, j))

    each(1, NP, lambda k: l_copy(nxt(p, k, NP), p).start())

    gw_copy.wait_recv()
    for h in range(CB // CH):
        s = slice(h * CH, (h + 1) * CH)
        u, inv = unit_cols(wraw[c, :, s])
        g = gw[c, :, s] + gw_in[:, s]
        gp_all[:, s] = inv * (g - u * jnp.sum(u * g, axis=0, keepdims=True))

    my_cols = pl.ds(pl.multiple_of(p * CB, CB), CB)

    def gp_copy(k):
        q = nxt(p, k, NP)
        rows = pl.ds(pl.multiple_of(q * DB, DB), DB)
        return rcopy(gp_all.at[rows], gp_ref.at[:, my_cols], gp_send.at[q], gp_recv.at[p], (q, j))

    def a_wait(k):
        src = nxt(y, k, NY)
        each(0, HX, lambda xp: a_copy(src, xp, src).wait_recv())

    each(1, NY, a_wait)

    def a_sum(xx):
        t = part_a[y, xx]
        for k in range(1, NY):
            t = t + in_a[nxt(y, k, NY), xx]
        sum_a[xx] = t

    each(0, NX, a_sum)

    def a2_copy(xx, src):
        return rcopy(sum_a.at[xx], in_a2.at[src], a2_send.at[xx], a2_recv.at[src], (dp_of(y, xx), j))

    def a2_start(k):
        a2_copy(nxt(x, k, NX), x).start()

    each(1, NX, a2_start)

    def b_wait(k):
        src = nxt(x, k, NX)
        each(0, NY, lambda yy: b_copy(src, yy, src).wait_recv())

    each(1, NX, b_wait)

    def b_sum(yy):
        t = part_b[x, yy]
        for k in range(1, NX):
            t = t + in_b[nxt(x, k, NX), yy]
        sum_b[yy] = t

    each(0, NY, b_sum)

    def b2_copy(yy, src):
        return rcopy(sum_b.at[yy], in_b2.at[src], b2_send.at[yy], b2_recv.at[src], (dp_of(yy, x), j))

    def b2_start(k):
        b2_copy(nxt(y, k, NY), y).start()

    each(1, NY, b2_start)
    each(1, NP, lambda k: gp_copy(k).start())
    gp_ref[:, my_cols] = gp_all[w_rows, :]

    def l_wait(k):
        q = nxt(p, k, NP)
        l_copy(q, q).wait_recv()

    each(1, NP, l_wait)
    loss_part = plane_loss[0]
    for q in range(1, NP):
        loss_part = loss_part + plane_loss[q]

    def a2_wait(k):
        src = nxt(x, k, NX)
        a2_copy(src, src).wait_recv()

    def b2_wait(k):
        src = nxt(y, k, NY)
        b2_copy(src, src).wait_recv()

    each(1, NX, a2_wait)
    each(1, NY, b2_wait)
    su, sinv = unit_cols(feats[1, y, x])
    ga, gb = sum_a[x], sum_b[y]
    for k in range(1, NX):
        ga = ga + in_a2[nxt(x, k, NX)]
        gb = gb + in_b2[nxt(y, k, NY)]
    dots = jnp.sum(su[:DH] * ga, axis=0, keepdims=True) + jnp.sum(su[DH:] * gb, axis=0, keepdims=True)

    for q in range(NJ):
        lo = q * DB
        msg[q, :DB, :] = ga[lo:lo + DB] if lo < DH else gb[lo - DH:lo - DH + DB]
        msg[q, DB:DB + 8, :] = loss_part
        msg[q, DB + 8:DB + 16, :] = jnp.broadcast_to(dots, (8, SH))
        msg[q, DB + 16:, :] = jnp.broadcast_to(sinv, (8, SH))

    def m_copy(q, src):
        return rcopy(msg.at[q], msg_in.at[src], m_send.at[q], m_recv.at[src], (p, q))

    def m_start(k):
        m_copy(nxt(j, k, NJ), j).start()

    each(1, NJ, m_start)
    msg_in[j] = msg[j]

    def m_wait(k):
        src = nxt(j, k, NJ)
        m_copy(src, src).wait_recv()

    each(1, NJ, m_wait)
    loss_sum = jnp.zeros((8, SH), F32)
    for h in range(2):
        t = msg_in[h, :DB + 16, :]
        for q in range(1, NZ):
            t = t + msg_in[2 * q + h, :DB + 16, :]
        loss_sum = loss_sum + t[DB:DB + 8]
        dsum = t[DB + 8:DB + 9]
        inv = msg_in[h, DB + 16:DB + 17, :]
        own = x_ref[1, :, h * SH:(h + 1) * SH].astype(F32) * inv
        gs_ref[:, h * SH:(h + 1) * SH] = inv * (t[:DB] - own * dsum)
    loss_ref[...] = jnp.full((8, SH), -inv_rows, F32) * jnp.sum(loss_sum)

    def gp_wait(k):
        q = nxt(p, k, NP)
        cols = pl.ds(pl.multiple_of(q * CB, CB), CB)
        rcopy(gp_all.at[pl.ds(0, DB)], gp_ref.at[:, cols], gp_send.at[q], gp_recv.at[q], (q, j)).wait_recv()

    each(1, NP, gp_wait)

    w_core.wait_send()
    gw_copy.wait_send()
    for r in range(ITERS):
        rcopy(core_col.at[r, c], core_col.at[r, c], cc_send.at[r], cc_recv.at[r], peer).wait_send()
        n = 2 * NP if r == 1 else NP
        slot = plane_row.at[r, p, pl.ds(0, n)]
        each(1, NP, lambda k: rcopy(slot, slot, pr_send.at[r, nxt(p, k, NP)], pr_recv.at[r, p], peer).wait_send())
        zslot = z_row.at[r, z, pl.ds(0, n)]
        each(1, NZ, lambda k: rcopy(zslot, zslot, zr_send.at[r, nxt(z, k, NZ)], zr_recv.at[r, z], peer).wait_send())
    each(1, NJ, lambda k: feat_copy(k).wait_send())
    each(1, NP, lambda k: w_copy(k).wait_send())
    each(0, t_send.shape[0], lambda n: t_copy(x, n, peer).wait_send())
    each(0, s_send.shape[0], lambda n: s_copy(y, n, peer).wait_send())
    each(1, NP, lambda k: gp_copy(k).wait_send())
    each(1, NP, lambda k: l_copy(nxt(p, k, NP), p).wait_send())
    each(1, NJ, lambda k: m_copy(nxt(j, k, NJ), j).wait_send())
    each(1, NX, lambda k: a2_copy(nxt(x, k, NX), x).wait_send())
    each(1, NY, lambda k: b2_copy(nxt(y, k, NY), y).wait_send())
    each(1, NY, lambda k: each(0, HX, lambda xp: a_copy(nxt(y, k, NY), xp, y).wait_send()))
    each(1, NX, lambda k: each(0, NY, lambda yy: b_copy(nxt(x, k, NX), yy, x).wait_send()))


def body(cfg, teacher_feats, student_feats, prototypes):
    NP, NJ, NY, NX, _, _ = cfg
    NZ = NJ // 2
    xt = jnp.stack([teacher_feats.T, student_feats.T])
    DB, SB = xt.shape[1:]
    SH = SB // 2
    D = DB * NJ
    DH = D // 2
    WC = prototypes.shape[1]
    CB = WC // NP
    PC = 2 * CB
    NB = NP // 2
    V, S = pltpu.VMEM, pltpu.SemaphoreType.DMA
    scratch = [
        V((2, NY, NX, D, SH), BF16), V((2, D, CB), BF16), V((2, D, CB), BF16), V((2, CB, D), BF16),
        V((NB, D, SB), BF16), V((NB, PC, SB), F32), V((NB, PC, SB), F32), V((PC, SH), F32),
        V((PC, SH), F32), V((NP, SH), F32), V((NP, SH), F32), V((PC, SB), BF16), V((8, SH), F32),
        V((ITERS, 2, 1, PC), F32), V((ITERS, NP, 2 * NP, SH), F32), V((ITERS, NZ, 2 * NP, SH), F32),
        V((2, D, CB), F32), V((D, CB), F32), V((D, CB), F32),
        V((NY, NX, DH, SH), F32), V((NX, NY, DH, SH), F32), V((NY, NX, DH, SH), F32), V((NX, NY, DH, SH), F32),
        V((NX, DH, SH), F32), V((NY, DH, SH), F32), V((NX, DH, SH), F32), V((NY, DH, SH), F32),
        V((NJ, DB + 24, SH), F32), V((NJ, DB + 24, SH), F32), V((NP, 8, SH), F32),
        S((NJ,)), S((NJ,)), S((NP,)), S((NP,)), S((2,)),
        S((NP - 1,)), S((NY, NX)), S((NP - 1,)), S((NY, NX)),
        S((ITERS,)), S((ITERS,)), S((ITERS, NP)), S((ITERS, NP)), S((ITERS, NZ)), S((ITERS, NZ)),
        S((2,)), S((NP,)), S((NP,)),
        S((NB,)), S((NB,)), S((NX, NY)), S((NX, NY)), S((NX,)), S((NX,)), S((NY,)), S((NY,)),
        S((NJ,)), S((NJ,)), S((NP,)), S((NP,)),
    ]
    vmem = pl.BlockSpec(memory_space=pltpu.VMEM)
    loss, gp, gs = pl.pallas_call(
        functools.partial(kernel, cfg),
        out_shape=(
            jax.ShapeDtypeStruct((8, SH), F32),
            jax.ShapeDtypeStruct((DB, WC), F32),
            jax.ShapeDtypeStruct((DB, SB), F32),
        ),
        in_specs=[vmem, vmem],
        out_specs=(vmem, vmem, vmem),
        scratch_shapes=scratch,
        compiler_params=pltpu.CompilerParams(
            collective_id=0, has_side_effects=True, vmem_limit_bytes=56 * 1024 * 1024
        ),
    )(xt, prototypes)
    return loss[0, 0], gp, gs.T


def solution(mesh):
    NP, NJ = mesh.shape["dp"], mesh.shape["proto"]
    NY = NX = int(round(NP ** 0.5))

    def run(teacher_feats, student_feats, prototypes):
        rows, protos = teacher_feats.shape[0], prototypes.shape[1]
        loss_scale = rows * protos // 256
        factor = float(loss_scale) / float(rows) / STUDENT_TEMP
        cfg = (NP, NJ, NY, NX, factor, 1.0 / rows)
        spec = P("dp", "proto")
        return jax.shard_map(
            functools.partial(body, cfg), mesh=mesh, in_specs=(spec,) * 3,
            out_specs=(P(), spec, spec), check_vma=False,
        )(teacher_feats, student_feats, prototypes)

    return run
```

```python
import functools

import jax
import jax.numpy as jnp
from jax import lax
from jax.experimental import pallas as pl
from jax.experimental.pallas import tpu as pltpu
from jax.sharding import PartitionSpec as P

ITERS = 3
EPS = 1e-06
TEACHER_TEMP = 0.07
STUDENT_TEMP = 0.1
MESH = pl.DeviceIdType.MESH
F32 = jnp.float32
BF16 = jnp.bfloat16


def rcopy(src, dst, send_sem, recv_sem, dev):
    return pltpu.make_async_remote_copy(
        src_ref=src, dst_ref=dst, send_sem=send_sem, recv_sem=recv_sem,
        device_id=dev, device_id_type=MESH,
    )


def each(lo, hi, fn):
    def step(k, carry):
        fn(k)
        return carry
    lax.fori_loop(lo, hi, step, 0)


def dot(a, b, dims=((1,), (0,))):
    return lax.dot_general(a, b, (dims, ((), ())), preferred_element_type=F32)


def kernel(
    cfg, t_ref, s_ref, w_ref, loss_ref, gp_ref, gs_ref,
    feats, wraw, wn, wtn, sn, base, logit, acc, colb, rscale, tots, gbuf, lossv,
    core_col, plane_row, z_row, gw, gw_in, gp_all,
    part_a, part_b, in_a, in_b, sum_a, sum_b, in_a2, in_b2, msg, msg_in, plane_loss,
    f_send, f_recv, w_send, w_recv, wc_sem, ag_send, ag_recv, own_sem,
    cc_send, cc_recv, pr_send, pr_recv, zr_send, zr_recv, gw_sem, gp_send, gp_recv,
    a_send, a_recv, b_send, b_recv, a2_send, a2_recv, b2_send, b2_recv,
    m_send, m_recv, l_send, l_recv,
):
    NP, NJ, NY, NX, factor, inv_rows = cfg
    NZ = NJ // 2
    DB = t_ref.shape[0]
    SH = t_ref.shape[1] // 2
    CB = wraw.shape[2]
    D = DB * NJ
    DH = D // 2
    PC = 2 * CB
    CH = min(256, CB)
    HX = NX // 2
    p = lax.axis_index("dp")
    j = lax.axis_index("proto")
    y, x = p // NX, lax.rem(p, NX)
    z, c = j // 2, lax.rem(j, 2)
    oc = 1 - c
    peer = (p, 2 * z + oc)

    def dp_of(yy, xx):
        return yy * NX + xx

    def nxt(v, k, n):
        return lax.rem(v + k, n)

    barrier = pltpu.get_barrier_semaphore()

    def greet_dp(k):
        pl.semaphore_signal(barrier, inc=1, device_id=(nxt(p, k, NP), j), device_id_type=MESH)

    def greet_proto(k):
        pl.semaphore_signal(barrier, inc=1, device_id=(p, nxt(j, k, NJ)), device_id_type=MESH)

    each(1, NP, greet_dp)
    each(1, NJ, greet_proto)
    pl.semaphore_wait(barrier, NP + NJ - 2)

    my_rows = pl.ds(pl.multiple_of(j * DB, DB), DB)
    my_half = pl.ds(pl.multiple_of(c * SH, SH), SH)

    def feat_copy(arr, k):
        q = nxt(j, k, NJ)
        lanes = pl.ds(pl.multiple_of(lax.rem(q, 2) * SH, SH), SH)
        src = (t_ref, s_ref)[arr].at[:, lanes]
        return rcopy(src, feats.at[arr, y, x, my_rows], f_send.at[arr, q], f_recv.at[arr, j], (p, q))

    each(1, NJ, lambda k: feat_copy(0, k).start())

    w_rows = pl.ds(pl.multiple_of(p * DB, DB), DB)

    def w_copy(k):
        q = nxt(p, k, NP)
        cols = pl.ds(pl.multiple_of(q * CB, CB), CB)
        return rcopy(w_ref.at[:, cols], wraw.at[c, w_rows], w_send.at[q], w_recv.at[p], (q, j))

    each(1, NP, lambda k: w_copy(k).start())
    each(1, NJ, lambda k: feat_copy(1, k).start())
    feats[0, y, x, my_rows, :] = t_ref[:, my_half]
    feats[1, y, x, my_rows, :] = s_ref[:, my_half]
    w_own = pltpu.make_async_copy(
        w_ref.at[:, pl.ds(pl.multiple_of(p * CB, CB), CB)], wraw.at[c, w_rows], own_sem.at[0])
    w_own.start()

    def feat_wait(arr):
        def wait(k):
            q = nxt(j, k, NJ)
            rows = pl.ds(pl.multiple_of(q * DB, DB), DB)
            rcopy(t_ref.at[:, pl.ds(0, SH)], feats.at[arr, y, x, rows],
                  f_send.at[arr, q], f_recv.at[arr, q], (p, q)).wait_recv()
        each(1, NJ, wait)

    near = sorted(range(1, NX), key=lambda k: min(k, NX - k))

    def ag_copy(arr, h, ys, xs, n, dev):
        slot = feats.at[arr, ys, xs, pl.ds(h * DH, DH)]
        return rcopy(slot, slot, ag_send.at[2 * arr + h, n], ag_recv.at[2 * arr + h, ys, xs], dev)

    def ag_wait(arr, h, ys, xs):
        ag_copy(arr, h, ys, xs, 0, peer).wait_recv()

    def own_out(arr):
        for i, k in enumerate(near):
            ag_copy(arr, 0, y, x, i, (dp_of(y, nxt(x, k, NX)), j)).start()
            ag_copy(arr, 1, y, x, i, (dp_of(nxt(y, k, NY), x), j)).start()
        for i, k in enumerate(near):
            ag_copy(arr, 0, y, x, NX - 1 + i, (dp_of(nxt(y, k, NY), x), j)).start()
            ag_copy(arr, 1, y, x, NX - 1 + i, (dp_of(y, nxt(x, k, NX)), j)).start()

    def forward(arr):
        for i, k in enumerate(near):
            xs, ys = nxt(x, k, NX), nxt(y, k, NY)
            n0 = (2 + i) * (NX - 1) - 1
            ag_wait(arr, 0, y, xs)
            each(1, NY, lambda m: ag_copy(arr, 0, y, xs, n0 + m, (dp_of(nxt(y, m, NY), x), j)).start())
            ag_wait(arr, 1, ys, x)
            each(1, NX, lambda m: ag_copy(arr, 1, ys, x, n0 + m, (dp_of(y, nxt(x, m, NX)), j)).start())

    def pair_wait(arr, yy, xp):
        def one(xx):
            @pl.when(yy != y)
            def _():
                @pl.when(xx != x)
                def _():
                    ag_wait(arr, 0, yy, xx)
                    ag_wait(arr, 1, yy, xx)

                @pl.when(xx == x)
                def _():
                    ag_wait(arr, 0, yy, xx)

            @pl.when(jnp.logical_and(yy == y, xx != x))
            def _():
                ag_wait(arr, 1, yy, xx)

        one(2 * xp)
        one(2 * xp + 1)

    feat_wait(0)
    own_out(0)

    def w_wait(k):
        q = nxt(p, k, NP)
        rows = pl.ds(pl.multiple_of(q * DB, DB), DB)
        rcopy(w_ref.at[:, pl.ds(0, CB)], wraw.at[c, rows], w_send.at[q], w_recv.at[q], (q, j)).wait_recv()

    each(1, NP, w_wait)
    w_own.wait()
    w_core = rcopy(wraw.at[c], wraw.at[c], wc_sem.at[0], wc_sem.at[1], peer)
    w_core.start()
    forward(0)
    feat_wait(1)
    own_out(1)

    def unit_cols(v):
        v32 = v.astype(F32)
        inv = lax.rsqrt(jnp.sum(v32 * v32, axis=0, keepdims=True) + EPS)
        return v32 * inv, inv

    def w_norm(cc):
        for h in range(CB // CH):
            u, _ = unit_cols(wraw[cc, :, h * CH:(h + 1) * CH])
            wn[cc, :, h * CH:(h + 1) * CH] = u.astype(BF16)
            wtn[cc, h * CH:(h + 1) * CH, :] = u.T.astype(BF16)

    w_norm(c)
    w_core.wait_recv()
    w_norm(oc)

    chunks = [(cc, h) for cc in range(2) for h in range(CB // CH)]

    def two(a):
        return jnp.concatenate([a, a], axis=1)

    acc[...] = jnp.zeros_like(acc)

    def teacher_rows(k):
        yy = nxt(y, k + k // 2 - 2 * (k // 3), NY)

        def pair(xp):
            pair_wait(0, yy, xp)
            b = yy * HX + xp
            raw = jnp.concatenate([feats[0, yy, 2 * xp], feats[0, yy, 2 * xp + 1]], axis=1)
            u, _ = unit_cols(raw)
            tn = u.astype(BF16)
            for i, (cc, h) in enumerate(chunks):
                rows = slice(i * CH, (i + 1) * CH)
                e = jnp.exp(dot(wtn[cc, h * CH:(h + 1) * CH, :], tn) * (1.0 / TEACHER_TEMP))
                base[b, rows, :] = e
                acc[rows, :] += e[:, :SH] + e[:, SH:]

        each(0, HX, pair)

    each(0, NY, teacher_rows)

    def student_rows(k):
        yy = nxt(y, k, NY)

        def pair(xp):
            b = yy * HX + xp

            pair_wait(1, yy, xp)
            raw = jnp.concatenate([feats[1, yy, 2 * xp], feats[1, yy, 2 * xp + 1]], axis=1)
            u, _ = unit_cols(raw)
            un = u.astype(BF16)
            sn[b] = un
            part = jnp.zeros((8, 2 * SH), F32)
            for i, (cc, h) in enumerate(chunks):
                rows = slice(i * CH, (i + 1) * CH)
                v = dot(wtn[cc, h * CH:(h + 1) * CH, :], un) * (1.0 / STUDENT_TEMP)
                logit[b, rows, :] = v
                part = part + jnp.sum(jnp.exp(v).reshape(CH // 8, 8, 2 * SH), axis=0)
            tot = jnp.sum(part, axis=0, keepdims=True)
            q = yy * NX + 2 * xp
            tots[pl.ds(q, 1), :] = tot[:, :SH]
            tots[pl.ds(q + 1, 1), :] = tot[:, SH:]

        each(0, HX, pair)

    def col_exchange(r):
        for i in range(PC // 128):
            core_col[r, c, :, i * 128:(i + 1) * 128] = jnp.sum(
                acc[i * 128:(i + 1) * 128, :].T, axis=0, keepdims=True)
        cp = rcopy(core_col.at[r, c], core_col.at[r, c], cc_send.at[r], cc_recv.at[r], peer)
        cp.start()
        cp.wait_recv()
        for i in range(PC // 128):
            s = slice(i * 128, (i + 1) * 128)
            v = 1.0 / (core_col[r, 0, :, s] + core_col[r, 1, :, s])
            colb[s, :] = jnp.broadcast_to(v, (128, 128)).T

    def col_pass():
        scale = rscale[...]

        def block(i):
            rows = pl.ds(pl.multiple_of(i * 64, 64), 64)
            a = jnp.zeros((64, SH), F32)
            for b in range(NP // 2):
                for h in range(2):
                    a = a + base[b, rows, h * SH:(h + 1) * SH] * scale[2 * b + h:2 * b + h + 1, :]
            acc[rows, :] = a

        each(0, PC // 64, block)

    def row_pass(r):
        def pair(b):
            for h in range(2):
                a = jnp.zeros((8, SH), F32)
                for i in range(PC // 64):
                    rows = slice(i * 64, (i + 1) * 64)
                    v = base[b, rows, h * SH:(h + 1) * SH] * colb[rows, :]
                    a = a + jnp.sum(v.reshape(8, 8, SH), axis=0)
                plane_row[r, p, pl.ds(2 * b + h, 1), :] = jnp.sum(a, axis=0, keepdims=True)

        each(0, NP // 2, pair)

    def row_exchange(r, between=None):
        n = 2 * NP if r == 2 else NP
        if r == 2:
            plane_row[r, p, NP:, :] = tots[...]

        def plane_copy(q, src):
            slot = plane_row.at[r, src, pl.ds(0, n)]
            return rcopy(slot, slot, pr_send.at[r, q], pr_recv.at[r, src], (q, j))

        each(1, NP, lambda k: plane_copy(nxt(p, k, NP), p).start())
        if between is not None:
            between()

        def plane_wait(k):
            q = nxt(p, k, NP)
            plane_copy(q, q).wait_recv()

        each(1, NP, plane_wait)
        total = plane_row[r, 0, :n, :]
        for q in range(1, NP):
            total = total + plane_row[r, q, :n, :]
        z_row[r, z, :n, :] = total

        def z_copy(q, src):
            slot = z_row.at[r, src, pl.ds(0, n)]
            return rcopy(slot, slot, zr_send.at[r, q], zr_recv.at[r, src], (p, 2 * q + c))

        each(1, NZ, lambda k: z_copy(nxt(z, k, NZ), z).start())

        def z_wait(k):
            q = nxt(z, k, NZ)
            z_copy(q, q).wait_recv()

        each(1, NZ, z_wait)
        total = z_row[r, 0, :n, :]
        for q in range(1, NZ):
            total = total + z_row[r, q, :n, :]
        rscale[...] = 1.0 / total[:NP]
        if r == 2:
            tots[...] = total[NP:]

    for r in range(ITERS):
        if r > 0:
            col_pass()
        col_exchange(r)
        row_pass(r)
        row_exchange(r, (lambda: forward(1), lambda: each(0, NY, student_rows), None)[r])

    lossv[...] = jnp.zeros_like(lossv)
    gw[...] = jnp.zeros_like(gw)

    def row_of(ref, q):
        return jnp.concatenate([ref[pl.ds(q, 1), :], ref[pl.ds(q + 1, 1), :]], axis=1)

    def a_copy(yy, xp, src_y):
        xs = pl.ds(2 * xp, 2)
        n = yy * HX + xp
        m = src_y * HX + xp
        return rcopy(part_a.at[yy, xs], in_a.at[src_y, xs], a_send.at[n], a_recv.at[m], (dp_of(yy, x), j))

    def b_copy(xx, yy, src_x):
        return rcopy(part_b.at[xx, yy], in_b.at[src_x, yy], b_send.at[xx, yy], b_recv.at[src_x, yy], (dp_of(y, xx), j))

    def grad_rows(k):
        yy = nxt(y, k + 1, NY)

        def pair(xp):
            b = yy * HX + xp
            q = yy * NX + 2 * xp
            rs = row_of(rscale, q)
            tot = row_of(tots, q)
            inv_tot = 1.0 / tot
            log_tot = jnp.log(tot)
            lsum = jnp.zeros((8, 2 * SH), F32)
            for i in range(PC // CH):
                rows = slice(i * CH, (i + 1) * CH)
                lg = logit[b, rows, :]
                target = base[b, rows, :] * rs * two(colb[rows, :])
                lsum = lsum + jnp.sum((target * (lg - log_tot)).reshape(CH // 8, 8, 2 * SH), axis=0)
                gbuf[rows, :] = ((jnp.exp(lg) * inv_tot - target) * factor).astype(BF16)
            lossv[...] += lsum[:, :SH] + lsum[:, SH:]
            gs = dot(wn[0], gbuf[:CB, :]) + dot(wn[1], gbuf[CB:, :])
            part_a[yy, 2 * xp] = gs[:DH, :SH]
            part_a[yy, 2 * xp + 1] = gs[:DH, SH:]
            part_b[2 * xp, yy] = gs[DH:, :SH]
            part_b[2 * xp + 1, yy] = gs[DH:, SH:]

            @pl.when(k < NY - 1)
            def _():
                a_copy(yy, xp, y).start()

            for h in range(2):
                @pl.when(2 * xp + h != x)
                def _():
                    b_copy(2 * xp + h, yy, x).start()

            un = sn[b]
            for i, (cc, h) in enumerate(chunks):
                gw[cc, :, h * CH:(h + 1) * CH] += dot(un, gbuf[i * CH:(i + 1) * CH, :], ((1,), (1,)))

        each(0, HX, pair)

    each(0, NY, grad_rows)

    gw_copy = rcopy(gw.at[oc], gw_in, gw_sem.at[0], gw_sem.at[1], peer)
    gw_copy.start()

    plane_loss[p] = lossv[...]

    def l_copy(q, src):
        slot = plane_loss.at[src]
        return rcopy(slot, slot, l_send.at[q], l_recv.at[src], (q, j))

    each(1, NP, lambda k: l_copy(nxt(p, k, NP), p).start())

    gw_copy.wait_recv()
    for h in range(CB // CH):
        s = slice(h * CH, (h + 1) * CH)
        u, inv = unit_cols(wraw[c, :, s])
        g = gw[c, :, s] + gw_in[:, s]
        gp_all[:, s] = inv * (g - u * jnp.sum(u * g, axis=0, keepdims=True))

    my_cols = pl.ds(pl.multiple_of(p * CB, CB), CB)

    def gp_copy(k):
        q = nxt(p, k, NP)
        rows = pl.ds(pl.multiple_of(q * DB, DB), DB)
        return rcopy(gp_all.at[rows], gp_ref.at[:, my_cols], gp_send.at[q], gp_recv.at[p], (q, j))

    def a_sum(xp):
        for k in range(1, NY):
            src = nxt(y, k, NY)
            a_copy(src, xp, src).wait_recv()
        for h in range(2):
            xx = 2 * xp + h
            t = part_a[y, xx]
            for k in range(1, NY):
                t = t + in_a[nxt(y, k, NY), xx]
            sum_a[xx] = t

            @pl.when(xx != x)
            def _():
                a2_copy(xx, x).start()

    def a2_copy(xx, src):
        return rcopy(sum_a.at[xx], in_a2.at[src], a2_send.at[xx], a2_recv.at[src], (dp_of(y, xx), j))

    def b_sum(yy):
        for k in range(1, NX):
            src = nxt(x, k, NX)
            b_copy(src, yy, src).wait_recv()
        t = part_b[x, yy]
        for k in range(1, NX):
            t = t + in_b[nxt(x, k, NX), yy]
        sum_b[yy] = t

    def b2_copy(yy, src):
        return rcopy(sum_b.at[yy], in_b2.at[src], b2_send.at[yy], b2_recv.at[src], (dp_of(yy, x), j))

    def b_next(k):
        yy = nxt(y, k, NY)
        b_sum(yy)
        b2_copy(yy, y).start()

    each(1, NY, b_next)
    each(0, HX, a_sum)
    b_sum(y)
    each(1, NP, lambda k: gp_copy(k).start())
    gp_own = pltpu.make_async_copy(gp_all.at[w_rows], gp_ref.at[:, my_cols], own_sem.at[1])
    gp_own.start()

    def l_wait(k):
        q = nxt(p, k, NP)
        l_copy(q, q).wait_recv()

    each(1, NP, l_wait)
    loss_part = plane_loss[0]
    for q in range(1, NP):
        loss_part = loss_part + plane_loss[q]

    loss_row = jnp.sum(loss_part, axis=0, keepdims=True)

    def a2_wait(k):
        src = nxt(x, k, NX)
        a2_copy(src, src).wait_recv()

    def b2_wait(k):
        src = nxt(y, k, NY)
        b2_copy(src, src).wait_recv()

    each(1, NX, a2_wait)
    each(1, NY, b2_wait)
    su, sinv = unit_cols(feats[1, y, x])
    ga, gb = sum_a[x], sum_b[y]
    for k in range(1, NX):
        ga = ga + in_a2[nxt(x, k, NX)]
        gb = gb + in_b2[nxt(y, k, NY)]
    dots = jnp.sum(su[:DH] * ga, axis=0, keepdims=True) + jnp.sum(su[DH:] * gb, axis=0, keepdims=True)

    for q in range(NJ):
        lo = q * DB
        msg[q, :DB, :] = ga[lo:lo + DB] if lo < DH else gb[lo - DH:lo - DH + DB]
        msg[q, DB:DB + 1, :] = dots
        msg[q, DB + 1:DB + 2, :] = sinv
        msg[q, DB + 2:DB + 3, :] = loss_row
        msg[q, DB + 3:, :] = jnp.zeros((5, SH), F32)

    def m_copy(q, src):
        return rcopy(msg.at[q], msg_in.at[src], m_send.at[q], m_recv.at[src], (p, q))

    def m_start(k):
        m_copy(nxt(j, k, NJ), j).start()

    each(1, NJ, m_start)
    msg_in[j] = msg[j]

    def m_wait(k):
        src = nxt(j, k, NJ)
        m_copy(src, src).wait_recv()

    each(1, NJ, m_wait)
    loss_sum = jnp.zeros((1, SH), F32)
    for h in range(2):
        t = msg_in[h]
        for q in range(1, NZ):
            t = t + msg_in[2 * q + h]
        loss_sum = loss_sum + t[DB + 2:DB + 3]
        dsum = t[DB:DB + 1]
        inv = msg_in[h, DB + 1:DB + 2, :]
        own = s_ref[:, h * SH:(h + 1) * SH].astype(F32) * inv
        gs_ref[:, h * SH:(h + 1) * SH] = inv * (t[:DB] - own * dsum)
    loss_ref[0, 0] = -inv_rows * jnp.sum(loss_sum)

    def gp_wait(k):
        q = nxt(p, k, NP)
        cols = pl.ds(pl.multiple_of(q * CB, CB), CB)
        rcopy(gp_all.at[pl.ds(0, DB)], gp_ref.at[:, cols], gp_send.at[q], gp_recv.at[q], (q, j)).wait_recv()

    each(1, NP, gp_wait)
    gp_own.wait()

    w_core.wait_send()
    gw_copy.wait_send()
    for r in range(ITERS):
        rcopy(core_col.at[r, c], core_col.at[r, c], cc_send.at[r], cc_recv.at[r], peer).wait_send()
        n = 2 * NP if r == 2 else NP
        slot = plane_row.at[r, p, pl.ds(0, n)]
        each(1, NP, lambda k: rcopy(slot, slot, pr_send.at[r, nxt(p, k, NP)], pr_recv.at[r, p], peer).wait_send())
        zslot = z_row.at[r, z, pl.ds(0, n)]
        each(1, NZ, lambda k: rcopy(zslot, zslot, zr_send.at[r, nxt(z, k, NZ)], zr_recv.at[r, z], peer).wait_send())
    for arr in range(2):
        each(1, NJ, lambda k: feat_copy(arr, k).wait_send())
        for h in range(2):
            each(0, NP - 1, lambda n: ag_copy(arr, h, y, x, n, peer).wait_send())
    each(1, NP, lambda k: w_copy(k).wait_send())
    each(1, NP, lambda k: gp_copy(k).wait_send())
    each(1, NP, lambda k: l_copy(nxt(p, k, NP), p).wait_send())
    each(1, NJ, lambda k: m_copy(nxt(j, k, NJ), j).wait_send())
    each(1, NX, lambda k: a2_copy(nxt(x, k, NX), x).wait_send())
    each(1, NY, lambda k: b2_copy(nxt(y, k, NY), y).wait_send())
    each(1, NY, lambda k: each(0, HX, lambda xp: a_copy(nxt(y, k, NY), xp, y).wait_send()))
    each(1, NX, lambda k: each(0, NY, lambda yy: b_copy(nxt(x, k, NX), yy, x).wait_send()))


def body(cfg, teacher_feats, student_feats, prototypes):
    NP, NJ, NY, NX, _, _ = cfg
    NZ = NJ // 2
    SB, DB = teacher_feats.shape
    SH = SB // 2
    D = DB * NJ
    DH = D // 2
    WC = prototypes.shape[1]
    CB = WC // NP
    PC = 2 * CB
    NB = NP // 2
    V, S = pltpu.VMEM, pltpu.SemaphoreType.DMA
    scratch = [
        V((2, NY, NX, D, SH), BF16), V((2, D, CB), BF16), V((2, D, CB), BF16), V((2, CB, D), BF16),
        V((NB, D, SB), BF16), V((NB, PC, SB), F32), V((NB, PC, SB), F32), V((PC, SH), F32),
        V((PC, SH), F32), V((NP, SH), F32), V((NP, SH), F32), V((PC, SB), BF16), V((8, SH), F32),
        V((ITERS, 2, 1, PC), F32), V((ITERS, NP, 2 * NP, SH), F32), V((ITERS, NZ, 2 * NP, SH), F32),
        V((2, D, CB), F32), V((D, CB), F32), V((D, CB), F32),
        V((NY, NX, DH, SH), F32), V((NX, NY, DH, SH), F32), V((NY, NX, DH, SH), F32), V((NX, NY, DH, SH), F32),
        V((NX, DH, SH), F32), V((NY, DH, SH), F32), V((NX, DH, SH), F32), V((NY, DH, SH), F32),
        V((NJ, DB + 8, SH), F32), V((NJ, DB + 8, SH), F32), V((NP, 8, SH), F32),
        S((2, NJ)), S((2, NJ)), S((NP,)), S((NP,)), S((2,)),
        S((4, NP - 1)), S((4, NY, NX)), S((2,)),
        S((ITERS,)), S((ITERS,)), S((ITERS, NP)), S((ITERS, NP)), S((ITERS, NZ)), S((ITERS, NZ)),
        S((2,)), S((NP,)), S((NP,)),
        S((NB,)), S((NB,)), S((NX, NY)), S((NX, NY)), S((NX,)), S((NX,)), S((NY,)), S((NY,)),
        S((NJ,)), S((NJ,)), S((NP,)), S((NP,)),
    ]
    vmem = pl.BlockSpec(memory_space=pltpu.VMEM)
    hbm = pl.BlockSpec(memory_space=pl.ANY)
    loss, gp, gs = pl.pallas_call(
        functools.partial(kernel, cfg),
        out_shape=(
            jax.ShapeDtypeStruct((1, 1), F32),
            jax.ShapeDtypeStruct((DB, WC), F32),
            jax.ShapeDtypeStruct((DB, SB), F32),
        ),
        in_specs=[vmem, vmem, hbm],
        out_specs=(pl.BlockSpec(memory_space=pltpu.SMEM), hbm, vmem),
        scratch_shapes=scratch,
        compiler_params=pltpu.CompilerParams(
            collective_id=0, has_side_effects=True, vmem_limit_bytes=56 * 1024 * 1024
        ),
    )(teacher_feats.T, student_feats.T, prototypes)
    return loss[0, 0], gp, gs.T


def solution(mesh):
    NP, NJ = mesh.shape["dp"], mesh.shape["proto"]
    NY = NX = int(round(NP ** 0.5))

    def run(teacher_feats, student_feats, prototypes):
        rows, protos = teacher_feats.shape[0], prototypes.shape[1]
        loss_scale = rows * protos // 256
        factor = float(loss_scale) / float(rows) / STUDENT_TEMP
        cfg = (NP, NJ, NY, NX, factor, 1.0 / rows)
        spec = P("dp", "proto")
        return jax.shard_map(
            functools.partial(body, cfg), mesh=mesh, in_specs=(spec,) * 3,
            out_specs=(P(), spec, spec), check_vma=False,
        )(teacher_feats, student_feats, prototypes)

    return run
```

```python
import functools

import jax
import jax.numpy as jnp
from jax import lax
from jax.experimental import pallas as pl
from jax.experimental.pallas import tpu as pltpu
from jax.sharding import PartitionSpec as P

ITERS = 3
EPS = 1e-06
TEACHER_TEMP = 0.07
STUDENT_TEMP = 0.1
MESH = pl.DeviceIdType.MESH
F32 = jnp.float32
BF16 = jnp.bfloat16


def rcopy(src, dst, send_sem, recv_sem, dev):
    return pltpu.make_async_remote_copy(
        src_ref=src, dst_ref=dst, send_sem=send_sem, recv_sem=recv_sem,
        device_id=dev, device_id_type=MESH,
    )


def take(ref, sem):
    pltpu.make_async_copy(ref, ref, sem).wait()


def each(lo, hi, fn):
    def step(k, carry):
        fn(k)
        return carry
    lax.fori_loop(lo, hi, step, 0)


def dot(a, b, dims=((1,), (0,))):
    return lax.dot_general(a, b, (dims, ((), ())), preferred_element_type=F32)


def kernel(
    cfg, t_ref, s_ref, w_ref, loss_ref, gp_ref, gs_ref,
    feats, wraw, wn, wtn, sn, base, logit, acc, colb, rscale, tots, gbuf, lossv,
    core_col, plane_row, z_row, gw, gw_in, gp_all,
    part_a, part_b, in_a, in_b, sum_a, sum_b, in_a2, in_b2, msg, msg_in, plane_loss,
    f_send, f_recv, w_send, w_recv, wc_sem, ag_send, ag_recv, ag_recv_s, own_sem,
    cc_send, cc_recv, pr_send, pr_recv, zr_send, zr_recv, gw_sem, gp_send, gp_recv,
    a_send, a_recv, b_send, b_recv, a2_send, a2_recv, b2_send, b2_recv,
    m_send, m_recv, l_send, l_recv,
):
    NP, NJ, NY, NX, factor, inv_rows = cfg
    NZ = NJ // 2
    DB = t_ref.shape[0]
    SH = t_ref.shape[1] // 2
    CB = wraw.shape[2]
    D = DB * NJ
    DH = D // 2
    PC = 2 * CB
    CH = min(256, CB)
    HX = NX // 2
    ag_rows = (NP - 1) * DH * SH // 2 // (2 * SH)
    p = lax.axis_index("dp")
    j = lax.axis_index("proto")
    y, x = p // NX, lax.rem(p, NX)
    z, c = j // 2, lax.rem(j, 2)
    oc = 1 - c
    peer = (p, 2 * z + oc)

    def dp_of(yy, xx):
        return yy * NX + xx

    def nxt(v, k, n):
        return lax.rem(v + k, n)

    barrier = pltpu.get_barrier_semaphore()

    def greet_dp(k):
        pl.semaphore_signal(barrier, inc=1, device_id=(nxt(p, k, NP), j), device_id_type=MESH)

    def greet_proto(k):
        pl.semaphore_signal(barrier, inc=1, device_id=(p, nxt(j, k, NJ)), device_id_type=MESH)

    each(1, NP, greet_dp)
    each(1, NJ, greet_proto)
    pl.semaphore_wait(barrier, NP + NJ - 2)

    my_rows = pl.ds(pl.multiple_of(j * DB, DB), DB)
    my_half = pl.ds(pl.multiple_of(c * SH, SH), SH)

    def feat_copy(arr, k):
        q = nxt(j, k, NJ)
        lanes = pl.ds(pl.multiple_of(lax.rem(q, 2) * SH, SH), SH)
        src = (t_ref, s_ref)[arr].at[:, lanes]
        return rcopy(src, feats.at[arr, y, x, my_rows], f_send.at[arr], f_recv.at[arr], (p, q))

    each(1, NJ, lambda k: feat_copy(0, k).start())

    w_rows = pl.ds(pl.multiple_of(p * DB, DB), DB)

    def w_copy(k):
        q = nxt(p, k, NP)
        cols = pl.ds(pl.multiple_of(q * CB, CB), CB)
        return rcopy(w_ref.at[:, cols], wraw.at[c, w_rows], w_send.at[0], w_recv.at[0], (q, j))

    each(1, NP, lambda k: w_copy(k).start())
    each(1, NJ, lambda k: feat_copy(1, k).start())
    feats[0, y, x, my_rows, :] = t_ref[:, my_half]
    feats[1, y, x, my_rows, :] = s_ref[:, my_half]
    w_own = pltpu.make_async_copy(
        w_ref.at[:, pl.ds(pl.multiple_of(p * CB, CB), CB)], wraw.at[c, w_rows], own_sem.at[0])
    w_own.start()

    def feat_wait(arr):
        take(feats.at[arr, y, x, pl.ds(0, D - DB)], f_recv.at[arr])

    near = sorted(range(1, NX), key=lambda k: min(k, NX - k))

    def ag_copy(arr, h, ys, xs, stage, dev):
        slot = feats.at[arr, ys, xs, pl.ds(h * DH, DH)]
        sem = ag_recv.at[h, ys, xs] if arr == 0 else ag_recv_s.at[h, stage]
        return rcopy(slot, slot, ag_send.at[arr, h], sem, dev)

    def ag_wait(arr, h, ys, xs):
        take(feats.at[arr, ys, xs, pl.ds(h * DH, DH)], ag_recv.at[h, ys, xs])

    def own_out(arr):
        for k in near:
            ag_copy(arr, 0, y, x, 0, (dp_of(y, nxt(x, k, NX)), j)).start()
            ag_copy(arr, 1, y, x, 0, (dp_of(nxt(y, k, NY), x), j)).start()
        for k in near:
            ag_copy(arr, 0, y, x, 1, (dp_of(nxt(y, k, NY), x), j)).start()
            ag_copy(arr, 1, y, x, 1, (dp_of(y, nxt(x, k, NX)), j)).start()

    def forward(arr):
        if arr == 1:
            for h in range(2):
                take(feats.at[1, 0, pl.ds(0, NX - 1), pl.ds(0, DH)], ag_recv_s.at[h, 0])
        for k in near:
            xs, ys = nxt(x, k, NX), nxt(y, k, NY)
            if arr == 0:
                ag_wait(0, 0, y, xs)
            each(1, NY, lambda m: ag_copy(arr, 0, y, xs, 1, (dp_of(nxt(y, m, NY), x), j)).start())
            if arr == 0:
                ag_wait(0, 1, ys, x)
            each(1, NX, lambda m: ag_copy(arr, 1, ys, x, 1, (dp_of(y, nxt(x, m, NX)), j)).start())

    def pair_wait(arr, yy, xp):
        def one(xx):
            @pl.when(yy != y)
            def _():
                @pl.when(xx != x)
                def _():
                    ag_wait(arr, 0, yy, xx)
                    ag_wait(arr, 1, yy, xx)

                @pl.when(xx == x)
                def _():
                    ag_wait(arr, 0, yy, xx)

            @pl.when(jnp.logical_and(yy == y, xx != x))
            def _():
                ag_wait(arr, 1, yy, xx)

        one(2 * xp)
        one(2 * xp + 1)

    feat_wait(0)
    own_out(0)

    take(wraw.at[c, pl.ds(0, D - DB)], w_recv.at[0])
    w_own.wait()
    w_core = rcopy(wraw.at[c], wraw.at[c], wc_sem.at[0], wc_sem.at[1], peer)
    w_core.start()
    forward(0)
    feat_wait(1)
    own_out(1)

    def unit_cols(v):
        v32 = v.astype(F32)
        inv = lax.rsqrt(jnp.sum(v32 * v32, axis=0, keepdims=True) + EPS)
        return v32 * inv, inv

    def w_norm(cc):
        for h in range(CB // CH):
            u, _ = unit_cols(wraw[cc, :, h * CH:(h + 1) * CH])
            wn[cc, :, h * CH:(h + 1) * CH] = u.astype(BF16)
            wtn[cc, h * CH:(h + 1) * CH, :] = u.T.astype(BF16)

    w_norm(c)
    w_core.wait_recv()
    w_norm(oc)

    chunks = [(cc, h) for cc in range(2) for h in range(CB // CH)]

    def two(a):
        return jnp.concatenate([a, a], axis=1)

    acc[...] = jnp.zeros_like(acc)

    def teacher_rows(k):
        yy = nxt(y, k + k // 2 - 2 * (k // 3), NY)

        def pair(xp):
            pair_wait(0, yy, xp)
            b = yy * HX + xp
            raw = jnp.concatenate([feats[0, yy, 2 * xp], feats[0, yy, 2 * xp + 1]], axis=1)
            u, _ = unit_cols(raw)
            tn = u.astype(BF16)
            for i, (cc, h) in enumerate(chunks):
                rows = slice(i * CH, (i + 1) * CH)
                e = jnp.exp(dot(wtn[cc, h * CH:(h + 1) * CH, :], tn) * (1.0 / TEACHER_TEMP))
                base[b, rows, :] = e
                acc[rows, :] += e[:, :SH] + e[:, SH:]

        each(0, HX, pair)

    each(0, NY, teacher_rows)

    def student_rows(yy):

        def pair(xp):
            b = yy * HX + xp

            raw = jnp.concatenate([feats[1, yy, 2 * xp], feats[1, yy, 2 * xp + 1]], axis=1)
            u, _ = unit_cols(raw)
            un = u.astype(BF16)
            sn[b] = un
            part = jnp.zeros((8, 2 * SH), F32)
            for i, (cc, h) in enumerate(chunks):
                rows = slice(i * CH, (i + 1) * CH)
                v = dot(wtn[cc, h * CH:(h + 1) * CH, :], un) * (1.0 / STUDENT_TEMP)
                logit[b, rows, :] = v
                part = part + jnp.sum(jnp.exp(v).reshape(CH // 8, 8, 2 * SH), axis=0)
            tot = jnp.sum(part, axis=0, keepdims=True)
            q = yy * NX + 2 * xp
            plane_row[ITERS, p, pl.ds(q, 1), :] = tot[:, :SH]
            plane_row[ITERS, p, pl.ds(q + 1, 1), :] = tot[:, SH:]

        each(0, HX, pair)

    def col_exchange(r):
        for i in range(PC // 128):
            core_col[r, c, :, i * 128:(i + 1) * 128] = jnp.sum(
                acc[i * 128:(i + 1) * 128, :].T, axis=0, keepdims=True)
        cp = rcopy(core_col.at[r, c], core_col.at[r, c], cc_send.at[r], cc_recv.at[r], peer)
        cp.start()
        cp.wait_recv()
        for i in range(PC // 128):
            s = slice(i * 128, (i + 1) * 128)
            v = 1.0 / (core_col[r, 0, :, s] + core_col[r, 1, :, s])
            colb[s, :] = jnp.broadcast_to(v, (128, 128)).T

    def col_pass():
        scale = rscale[...]

        def block(i):
            rows = pl.ds(pl.multiple_of(i * 64, 64), 64)
            a = jnp.zeros((64, SH), F32)
            for b in range(NP // 2):
                for h in range(2):
                    a = a + base[b, rows, h * SH:(h + 1) * SH] * scale[2 * b + h:2 * b + h + 1, :]
            acc[rows, :] = a

        each(0, PC // 64, block)

    def row_pass(r):
        def pair(b):
            for h in range(2):
                a = jnp.zeros((8, SH), F32)
                for i in range(PC // 64):
                    rows = slice(i * 64, (i + 1) * 64)
                    v = base[b, rows, h * SH:(h + 1) * SH] * colb[rows, :]
                    a = a + jnp.sum(v.reshape(8, 8, SH), axis=0)
                plane_row[r, p, pl.ds(2 * b + h, 1), :] = jnp.sum(a, axis=0, keepdims=True)

        each(0, NP // 2, pair)

    def plane_start(r):
        slot = plane_row.at[r, p]
        each(1, NP, lambda k: rcopy(slot, slot, pr_send.at[r], pr_recv.at[r], (nxt(p, k, NP), j)).start())

    def plane_end(r):
        take(plane_row.at[r, pl.ds(0, NP - 1)], pr_recv.at[r])
        total = plane_row[r, 0]
        for q in range(1, NP):
            total = total + plane_row[r, q]
        z_row[r, z] = total

    def z_start(r):
        slot = z_row.at[r, z]
        each(1, NZ, lambda k: rcopy(slot, slot, zr_send.at[r], zr_recv.at[r], (p, 2 * nxt(z, k, NZ) + c)).start())

    def z_end(r):
        take(z_row.at[r, pl.ds(0, NZ - 1)], zr_recv.at[r])
        total = z_row[r, 0]
        for q in range(1, NZ):
            total = total + z_row[r, q]
        return total

    for r in range(ITERS):
        if r == 2:
            plane_end(ITERS)
            z_start(ITERS)
        if r > 0:
            col_pass()
        col_exchange(r)
        row_pass(r)
        plane_start(r)
        if r == 0:
            forward(1)
        if r == 1:
            for h in range(2):
                take(feats.at[1, pl.ds(0, NY - 1), :, pl.ds(0, DH)], ag_recv_s.at[h, 1])
            each(0, NY, student_rows)
            plane_start(ITERS)
        plane_end(r)
        z_start(r)
        rscale[...] = 1.0 / z_end(r)
    tots[...] = z_end(ITERS)

    lossv[...] = jnp.zeros_like(lossv)
    gw[...] = jnp.zeros_like(gw)

    def row_of(ref, q):
        return jnp.concatenate([ref[pl.ds(q, 1), :], ref[pl.ds(q + 1, 1), :]], axis=1)

    def a_copy(yy, xp):
        xs = pl.ds(2 * xp, 2)
        return rcopy(part_a.at[yy, xs], in_a.at[y, xs], a_send.at[0], a_recv.at[xp], (dp_of(yy, x), j))

    def b_copy(xx, yy):
        return rcopy(part_b.at[xx, yy], in_b.at[x, yy], b_send.at[0], b_recv.at[yy], (dp_of(y, xx), j))

    def grad_rows(k):
        yy = nxt(y, k + 1, NY)

        def pair(xp):
            b = yy * HX + xp
            q = yy * NX + 2 * xp
            rs = row_of(rscale, q)
            tot = row_of(tots, q)
            inv_tot = 1.0 / tot
            log_tot = jnp.log(tot)
            lsum = jnp.zeros((8, 2 * SH), F32)
            for i in range(PC // CH):
                rows = slice(i * CH, (i + 1) * CH)
                lg = logit[b, rows, :]
                target = base[b, rows, :] * rs * two(colb[rows, :])
                lsum = lsum + jnp.sum((target * (lg - log_tot)).reshape(CH // 8, 8, 2 * SH), axis=0)
                gbuf[rows, :] = ((jnp.exp(lg) * inv_tot - target) * factor).astype(BF16)
            lossv[...] += lsum[:, :SH] + lsum[:, SH:]
            gs = dot(wn[0], gbuf[:CB, :]) + dot(wn[1], gbuf[CB:, :])
            part_a[yy, 2 * xp] = gs[:DH, :SH]
            part_a[yy, 2 * xp + 1] = gs[:DH, SH:]
            part_b[2 * xp, yy] = gs[DH:, :SH]
            part_b[2 * xp + 1, yy] = gs[DH:, SH:]

            @pl.when(k < NY - 1)
            def _():
                a_copy(yy, xp).start()

            for h in range(2):
                @pl.when(2 * xp + h != x)
                def _():
                    b_copy(2 * xp + h, yy).start()

            un = sn[b]
            for i, (cc, h) in enumerate(chunks):
                gw[cc, :, h * CH:(h + 1) * CH] += dot(un, gbuf[i * CH:(i + 1) * CH, :], ((1,), (1,)))

        each(0, HX, pair)

    each(0, NY, grad_rows)

    gw_copy = rcopy(gw.at[oc], gw_in, gw_sem.at[0], gw_sem.at[1], peer)
    gw_copy.start()

    plane_loss[p] = lossv[...]

    def l_start(k):
        slot = plane_loss.at[p]
        rcopy(slot, slot, l_send.at[0], l_recv.at[0], (nxt(p, k, NP), j)).start()

    each(1, NP, l_start)

    gw_copy.wait_recv()
    for h in range(CB // CH):
        s = slice(h * CH, (h + 1) * CH)
        u, inv = unit_cols(wraw[c, :, s])
        g = gw[c, :, s] + gw_in[:, s]
        gp_all[:, s] = inv * (g - u * jnp.sum(u * g, axis=0, keepdims=True))

    my_cols = pl.ds(pl.multiple_of(p * CB, CB), CB)

    def gp_copy(k):
        q = nxt(p, k, NP)
        rows = pl.ds(pl.multiple_of(q * DB, DB), DB)
        return rcopy(gp_all.at[rows], gp_ref.at[:, my_cols], gp_send.at[0], gp_recv.at[0], (q, j))

    def a_sum(xp):
        take(in_a.at[pl.ds(0, NY - 1), pl.ds(2 * xp, 2)], a_recv.at[xp])
        for h in range(2):
            xx = 2 * xp + h
            t = part_a[y, xx]
            for k in range(1, NY):
                t = t + in_a[nxt(y, k, NY), xx]
            sum_a[xx] = t

            @pl.when(xx != x)
            def _():
                a2_copy(xx, x).start()

    def a2_copy(xx, src):
        return rcopy(sum_a.at[xx], in_a2.at[src], a2_send.at[0], a2_recv.at[0], (dp_of(y, xx), j))

    def b_sum(yy):
        take(in_b.at[pl.ds(0, NX - 1), yy], b_recv.at[yy])
        t = part_b[x, yy]
        for k in range(1, NX):
            t = t + in_b[nxt(x, k, NX), yy]
        sum_b[yy] = t

    def b2_copy(yy, src):
        return rcopy(sum_b.at[yy], in_b2.at[src], b2_send.at[0], b2_recv.at[0], (dp_of(yy, x), j))

    def b_next(k):
        yy = nxt(y, k, NY)
        b_sum(yy)
        b2_copy(yy, y).start()

    each(1, NY, b_next)
    each(0, HX, a_sum)
    b_sum(y)
    each(1, NP, lambda k: gp_copy(k).start())
    gp_own = pltpu.make_async_copy(gp_all.at[w_rows], gp_ref.at[:, my_cols], own_sem.at[1])
    gp_own.start()

    take(plane_loss.at[pl.ds(0, NP - 1)], l_recv.at[0])
    loss_part = plane_loss[0]
    for q in range(1, NP):
        loss_part = loss_part + plane_loss[q]

    loss_row = jnp.sum(loss_part, axis=0, keepdims=True)

    take(in_a2.at[pl.ds(0, NX - 1)], a2_recv.at[0])
    take(in_b2.at[pl.ds(0, NY - 1)], b2_recv.at[0])
    su, sinv = unit_cols(feats[1, y, x])
    ga, gb = sum_a[x], sum_b[y]
    for k in range(1, NX):
        ga = ga + in_a2[nxt(x, k, NX)]
        gb = gb + in_b2[nxt(y, k, NY)]
    dots = jnp.sum(su[:DH] * ga, axis=0, keepdims=True) + jnp.sum(su[DH:] * gb, axis=0, keepdims=True)

    for q in range(NJ):
        lo = q * DB
        msg[q, :DB, :] = ga[lo:lo + DB] if lo < DH else gb[lo - DH:lo - DH + DB]
        msg[q, DB:DB + 1, :] = dots
        msg[q, DB + 1:DB + 2, :] = sinv
        msg[q, DB + 2:DB + 3, :] = loss_row
        msg[q, DB + 3:, :] = jnp.zeros((5, SH), F32)

    def m_copy(q, src):
        return rcopy(msg.at[q], msg_in.at[src], m_send.at[0], m_recv.at[0], (p, q))

    def m_start(k):
        m_copy(nxt(j, k, NJ), j).start()

    each(1, NJ, m_start)
    msg_in[j] = msg[j]

    take(msg_in.at[pl.ds(0, NJ - 1)], m_recv.at[0])
    loss_sum = jnp.zeros((1, SH), F32)
    for h in range(2):
        t = msg_in[h]
        for q in range(1, NZ):
            t = t + msg_in[2 * q + h]
        loss_sum = loss_sum + t[DB + 2:DB + 3]
        dsum = t[DB:DB + 1]
        inv = msg_in[h, DB + 1:DB + 2, :]
        own = s_ref[:, h * SH:(h + 1) * SH].astype(F32) * inv
        gs_ref[:, h * SH:(h + 1) * SH] = inv * (t[:DB] - own * dsum)
    loss_ref[0, 0] = -inv_rows * jnp.sum(loss_sum)

    take(gp_all.at[pl.ds(0, D - DB)], gp_recv.at[0])
    gp_own.wait()

    w_core.wait_send()
    gw_copy.wait_send()
    for r in range(ITERS + 1):
        if r < ITERS:
            take(core_col.at[r, 0], cc_send.at[r])
        take(plane_row.at[r, pl.ds(0, NP - 1)], pr_send.at[r])
        take(z_row.at[r, pl.ds(0, NZ - 1)], zr_send.at[r])
    for arr in range(2):
        take(feats.at[arr, 0, 0, pl.ds(0, D - DB)], f_send.at[arr])
        for h in range(2):
            take(base.at[0, pl.ds(0, ag_rows)], ag_send.at[arr, h])
    take(wraw.at[0, pl.ds(0, D - DB)], w_send.at[0])
    take(gp_all.at[pl.ds(0, D - DB)], gp_send.at[0])
    take(plane_loss.at[pl.ds(0, NP - 1)], l_send.at[0])
    take(msg_in.at[pl.ds(0, NJ - 1)], m_send.at[0])
    take(in_a2.at[pl.ds(0, NX - 1)], a2_send.at[0])
    take(in_b2.at[pl.ds(0, NY - 1)], b2_send.at[0])
    take(in_a.at[pl.ds(0, NY - 1)], a_send.at[0])
    take(in_b.at[pl.ds(0, NX - 1)], b_send.at[0])

def body(cfg, teacher_feats, student_feats, prototypes):
    NP, NJ, NY, NX, _, _ = cfg
    NZ = NJ // 2
    SB, DB = teacher_feats.shape
    SH = SB // 2
    D = DB * NJ
    DH = D // 2
    WC = prototypes.shape[1]
    CB = WC // NP
    PC = 2 * CB
    NB = NP // 2
    V, S = pltpu.VMEM, pltpu.SemaphoreType.DMA
    scratch = [
        V((2, NY, NX, D, SH), BF16), V((2, D, CB), BF16), V((2, D, CB), BF16), V((2, CB, D), BF16),
        V((NB, D, SB), BF16), V((NB, PC, SB), F32), V((NB, PC, SB), F32), V((PC, SH), F32),
        V((PC, SH), F32), V((NP, SH), F32), V((NP, SH), F32), V((PC, SB), BF16), V((8, SH), F32),
        V((ITERS, 2, 1, PC), F32), V((ITERS + 1, NP, NP, SH), F32), V((ITERS + 1, NZ, NP, SH), F32),
        V((2, D, CB), F32), V((D, CB), F32), V((D, CB), F32),
        V((NY, NX, DH, SH), F32), V((NX, NY, DH, SH), F32), V((NY, NX, DH, SH), F32), V((NX, NY, DH, SH), F32),
        V((NX, DH, SH), F32), V((NY, DH, SH), F32), V((NX, DH, SH), F32), V((NY, DH, SH), F32),
        V((NJ, DB + 8, SH), F32), V((NJ, DB + 8, SH), F32), V((NP, 8, SH), F32),
        S((2,)), S((2,)), S((1,)), S((1,)), S((2,)), S((2, 2)), S((2, NY, NX)), S((2, 2)), S((2,)),
        S((ITERS,)), S((ITERS,)), S((ITERS + 1,)), S((ITERS + 1,)), S((ITERS + 1,)), S((ITERS + 1,)),
        S((2,)), S((1,)), S((1,)),
        S((1,)), S((NX // 2,)), S((1,)), S((NY,)), S((1,)), S((1,)), S((1,)), S((1,)),
        S((1,)), S((1,)), S((1,)), S((1,)),
    ]
    vmem = pl.BlockSpec(memory_space=pltpu.VMEM)
    hbm = pl.BlockSpec(memory_space=pl.ANY)
    loss, gp, gs = pl.pallas_call(
        functools.partial(kernel, cfg),
        out_shape=(
            jax.ShapeDtypeStruct((1, 1), F32),
            jax.ShapeDtypeStruct((DB, WC), F32),
            jax.ShapeDtypeStruct((DB, SB), F32),
        ),
        in_specs=[vmem, vmem, hbm],
        out_specs=(pl.BlockSpec(memory_space=pltpu.SMEM), hbm, vmem),
        scratch_shapes=scratch,
        compiler_params=pltpu.CompilerParams(
            collective_id=0, has_side_effects=True, vmem_limit_bytes=56 * 1024 * 1024
        ),
    )(teacher_feats.T, student_feats.T, prototypes)
    return loss[0, 0], gp, gs.T


def solution(mesh):
    NP, NJ = mesh.shape["dp"], mesh.shape["proto"]
    NY = NX = int(round(NP ** 0.5))

    def run(teacher_feats, student_feats, prototypes):
        rows, protos = teacher_feats.shape[0], prototypes.shape[1]
        loss_scale = rows * protos // 256
        factor = float(loss_scale) / float(rows) / STUDENT_TEMP
        cfg = (NP, NJ, NY, NX, factor, 1.0 / rows)
        spec = P("dp", "proto")
        return jax.shard_map(
            functools.partial(body, cfg), mesh=mesh, in_specs=(spec,) * 3,
            out_specs=(P(), spec, spec), check_vma=False,
        )(teacher_feats, student_feats, prototypes)

    return run
```

```python
import functools

import jax
import jax.numpy as jnp
from jax import lax
from jax.experimental import pallas as pl
from jax.experimental.pallas import tpu as pltpu
from jax.sharding import PartitionSpec as P

ITERS = 3
EPS = 1e-06
TEACHER_TEMP = 0.07
STUDENT_TEMP = 0.1
MESH = pl.DeviceIdType.MESH
F32 = jnp.float32
BF16 = jnp.bfloat16


def rcopy(src, dst, send_sem, recv_sem, dev):
    return pltpu.make_async_remote_copy(
        src_ref=src, dst_ref=dst, send_sem=send_sem, recv_sem=recv_sem,
        device_id=dev, device_id_type=MESH,
    )


def take(ref, sem):
    pltpu.make_async_copy(ref, ref, sem).wait()


def each(lo, hi, fn):
    def step(k, carry):
        fn(k)
        return carry
    lax.fori_loop(lo, hi, step, 0)


def dot(a, b, dims=((1,), (0,))):
    return lax.dot_general(a, b, (dims, ((), ())), preferred_element_type=F32)


def kernel(
    cfg, t_ref, s_ref, w_ref, loss_ref, gp_ref, gs_ref,
    feats, wraw, wn, wtn, sn, base, logit, acc, colb, rscale, tots, gbuf, lossv,
    core_col, plane_row, z_row, gw, gw_in, gp_all,
    part_a, part_b, in_a, in_b, sum_a, sum_b, in_a2, in_b2, msg, msg_in, plane_loss,
    f_send, f_recv, w_send, w_recv, wc_sem, ag_send, ag_recv, ag_recv_s, own_sem,
    cc_send, cc_recv, pr_send, pr_recv, zr_send, zr_recv, gw_sem, gp_send, gp_recv,
    a_send, a_recv, b_send, b_recv, a2_send, a2_recv, b2_send, b2_recv,
    m_send, m_recv, l_send, l_recv,
):
    NP, NJ, NY, NX, factor, inv_rows = cfg
    NZ = NJ // 2
    DB = t_ref.shape[0]
    SH = t_ref.shape[1] // 2
    CB = wraw.shape[2]
    D = DB * NJ
    DH = D // 2
    PC = 2 * CB
    CH = min(256, CB)
    HX = NX // 2
    ag_rows = (NP - 1) * DH * SH // 2 // (2 * SH)
    p = lax.axis_index("dp")
    j = lax.axis_index("proto")
    y, x = p // NX, lax.rem(p, NX)
    z, c = j // 2, lax.rem(j, 2)
    oc = 1 - c
    peer = (p, 2 * z + oc)

    def dp_of(yy, xx):
        return yy * NX + xx

    def nxt(v, k, n):
        return lax.rem(v + k, n)

    barrier = pltpu.get_barrier_semaphore()

    def greet_dp(k):
        pl.semaphore_signal(barrier, inc=1, device_id=(nxt(p, k, NP), j), device_id_type=MESH)

    def greet_proto(k):
        pl.semaphore_signal(barrier, inc=1, device_id=(p, nxt(j, k, NJ)), device_id_type=MESH)

    each(1, NP, greet_dp)
    each(1, NJ, greet_proto)
    pl.semaphore_wait(barrier, NP + NJ - 2)

    my_rows = pl.ds(pl.multiple_of(j * DB, DB), DB)
    my_half = pl.ds(pl.multiple_of(c * SH, SH), SH)

    def feat_copy(arr, k):
        q = nxt(j, k, NJ)
        lanes = pl.ds(pl.multiple_of(lax.rem(q, 2) * SH, SH), SH)
        src = (t_ref, s_ref)[arr].at[:, lanes]
        return rcopy(src, feats.at[arr, y, x, my_rows], f_send.at[arr], f_recv.at[arr], (p, q))

    each(1, NJ, lambda k: feat_copy(0, k).start())

    w_rows = pl.ds(pl.multiple_of(p * DB, DB), DB)

    def w_copy(k):
        q = nxt(p, k, NP)
        cols = pl.ds(pl.multiple_of(q * CB, CB), CB)
        return rcopy(w_ref.at[:, cols], wraw.at[c, w_rows], w_send.at[0], w_recv.at[0], (q, j))

    each(1, NP, lambda k: w_copy(k).start())
    each(1, NJ, lambda k: feat_copy(1, k).start())
    feats[0, y, x, my_rows, :] = t_ref[:, my_half]
    feats[1, y, x, my_rows, :] = s_ref[:, my_half]
    w_own = pltpu.make_async_copy(
        w_ref.at[:, pl.ds(pl.multiple_of(p * CB, CB), CB)], wraw.at[c, w_rows], own_sem.at[0])
    w_own.start()

    def feat_wait(arr):
        take(feats.at[arr, y, x, pl.ds(0, D - DB)], f_recv.at[arr])

    near = sorted(range(1, NX), key=lambda k: min(k, NX - k))

    def ag_copy(arr, h, ys, xs, stage, dev):
        slot = feats.at[arr, ys, xs, pl.ds(h * DH, DH)]
        sem = ag_recv.at[h, ys, xs] if arr == 0 else ag_recv_s.at[h, stage]
        return rcopy(slot, slot, ag_send.at[arr, h], sem, dev)

    def ag_wait(arr, h, ys, xs):
        take(feats.at[arr, ys, xs, pl.ds(h * DH, DH)], ag_recv.at[h, ys, xs])

    def own_out(arr):
        for k in near:
            ag_copy(arr, 0, y, x, 0, (dp_of(y, nxt(x, k, NX)), j)).start()
            ag_copy(arr, 1, y, x, 0, (dp_of(nxt(y, k, NY), x), j)).start()
        for k in near:
            ag_copy(arr, 0, y, x, 1, (dp_of(nxt(y, k, NY), x), j)).start()
            ag_copy(arr, 1, y, x, 1, (dp_of(y, nxt(x, k, NX)), j)).start()

    def forward(arr):
        if arr == 1:
            for h in range(2):
                take(feats.at[1, 0, pl.ds(0, NX - 1), pl.ds(0, DH)], ag_recv_s.at[h, 0])
        for k in near:
            xs, ys = nxt(x, k, NX), nxt(y, k, NY)
            if arr == 0:
                ag_wait(0, 0, y, xs)
            each(1, NY, lambda m: ag_copy(arr, 0, y, xs, 1, (dp_of(nxt(y, m, NY), x), j)).start())
            if arr == 0:
                ag_wait(0, 1, ys, x)
            each(1, NX, lambda m: ag_copy(arr, 1, ys, x, 1, (dp_of(y, nxt(x, m, NX)), j)).start())

    def pair_wait(arr, yy, xp):
        def one(xx):
            @pl.when(yy != y)
            def _():
                @pl.when(xx != x)
                def _():
                    ag_wait(arr, 0, yy, xx)
                    ag_wait(arr, 1, yy, xx)

                @pl.when(xx == x)
                def _():
                    ag_wait(arr, 0, yy, xx)

            @pl.when(jnp.logical_and(yy == y, xx != x))
            def _():
                ag_wait(arr, 1, yy, xx)

        one(2 * xp)
        one(2 * xp + 1)

    feat_wait(0)
    own_out(0)

    take(wraw.at[c, pl.ds(0, D - DB)], w_recv.at[0])
    w_own.wait()
    w_core = rcopy(wraw.at[c], wraw.at[c], wc_sem.at[0], wc_sem.at[1], peer)
    w_core.start()
    forward(0)
    feat_wait(1)
    own_out(1)

    def unit_cols(v):
        v32 = v.astype(F32)
        inv = lax.rsqrt(jnp.sum(v32 * v32, axis=0, keepdims=True) + EPS)
        return v32 * inv, inv

    def w_norm(cc):
        for h in range(CB // CH):
            u, _ = unit_cols(wraw[cc, :, h * CH:(h + 1) * CH])
            wn[cc, :, h * CH:(h + 1) * CH] = u.astype(BF16)
            wtn[cc, h * CH:(h + 1) * CH, :] = u.T.astype(BF16)

    w_norm(c)
    w_core.wait_recv()
    w_norm(oc)

    chunks = [(cc, h) for cc in range(2) for h in range(CB // CH)]

    def two(a):
        return jnp.concatenate([a, a], axis=1)

    acc[...] = jnp.zeros_like(acc)

    def teacher_rows(k):
        yy = nxt(y, k + k // 2 - 2 * (k // 3), NY)

        def pair(xp):
            pair_wait(0, yy, xp)
            b = yy * HX + xp
            raw = jnp.concatenate([feats[0, yy, 2 * xp], feats[0, yy, 2 * xp + 1]], axis=1)
            u, _ = unit_cols(raw)
            tn = u.astype(BF16)
            for i, (cc, h) in enumerate(chunks):
                rows = slice(i * CH, (i + 1) * CH)
                e = jnp.exp(dot(wtn[cc, h * CH:(h + 1) * CH, :], tn) * (1.0 / TEACHER_TEMP))
                base[b, rows, :] = e
                acc[rows, :] += e[:, :SH] + e[:, SH:]

        each(0, HX, pair)

    each(0, NY, teacher_rows)

    def student_rows(yy):

        def pair(xp):
            b = yy * HX + xp

            raw = jnp.concatenate([feats[1, yy, 2 * xp], feats[1, yy, 2 * xp + 1]], axis=1)
            u, _ = unit_cols(raw)
            un = u.astype(BF16)
            sn[b] = un
            part = jnp.zeros((8, 2 * SH), F32)
            for i, (cc, h) in enumerate(chunks):
                rows = slice(i * CH, (i + 1) * CH)
                v = dot(wtn[cc, h * CH:(h + 1) * CH, :], un) * (1.0 / STUDENT_TEMP)
                logit[b, rows, :] = v
                part = part + jnp.sum(jnp.exp(v).reshape(CH // 8, 8, 2 * SH), axis=0)
            tot = jnp.sum(part, axis=0, keepdims=True)
            q = yy * NX + 2 * xp
            plane_row[ITERS, p, pl.ds(q, 1), :] = tot[:, :SH]
            plane_row[ITERS, p, pl.ds(q + 1, 1), :] = tot[:, SH:]

        each(0, HX, pair)

    def col_exchange(r):
        for i in range(PC // 128):
            core_col[r, c, :, i * 128:(i + 1) * 128] = jnp.sum(
                acc[i * 128:(i + 1) * 128, :].T, axis=0, keepdims=True)
        cp = rcopy(core_col.at[r, c], core_col.at[r, c], cc_send.at[r], cc_recv.at[r], peer)
        cp.start()
        cp.wait_recv()
        for i in range(PC // 128):
            s = slice(i * 128, (i + 1) * 128)
            v = 1.0 / (core_col[r, 0, :, s] + core_col[r, 1, :, s])
            colb[s, :] = jnp.broadcast_to(v, (128, 128)).T

    def col_pass():
        scale = rscale[...]

        def block(i):
            rows = pl.ds(pl.multiple_of(i * 64, 64), 64)
            a = jnp.zeros((64, SH), F32)
            for b in range(NP // 2):
                for h in range(2):
                    a = a + base[b, rows, h * SH:(h + 1) * SH] * scale[2 * b + h:2 * b + h + 1, :]
            acc[rows, :] = a

        each(0, PC // 64, block)

    def row_pass(r):
        def pair(b):
            for h in range(2):
                a = jnp.zeros((8, SH), F32)
                for i in range(PC // 64):
                    rows = slice(i * 64, (i + 1) * 64)
                    v = base[b, rows, h * SH:(h + 1) * SH] * colb[rows, :]
                    a = a + jnp.sum(v.reshape(8, 8, SH), axis=0)
                plane_row[r, p, pl.ds(2 * b + h, 1), :] = jnp.sum(a, axis=0, keepdims=True)

        each(0, NP // 2, pair)

    def plane_start(r):
        slot = plane_row.at[r, p]
        each(1, NP, lambda k: rcopy(slot, slot, pr_send.at[r], pr_recv.at[r], (nxt(p, k, NP), j)).start())

    def plane_end(r):
        take(plane_row.at[r, pl.ds(0, NP - 1)], pr_recv.at[r])
        total = plane_row[r, 0]
        for q in range(1, NP):
            total = total + plane_row[r, q]
        z_row[r, z] = total

    def z_start(r):
        slot = z_row.at[r, z]
        each(1, NZ, lambda k: rcopy(slot, slot, zr_send.at[r], zr_recv.at[r], (p, 2 * nxt(z, k, NZ) + c)).start())

    def z_end(r):
        take(z_row.at[r, pl.ds(0, NZ - 1)], zr_recv.at[r])
        total = z_row[r, 0]
        for q in range(1, NZ):
            total = total + z_row[r, q]
        return total

    for r in range(ITERS):
        if r == 2:
            plane_end(ITERS)
            z_start(ITERS)
        if r > 0:
            col_pass()
        col_exchange(r)
        row_pass(r)
        plane_start(r)
        if r == 0:
            forward(1)
        if r == 1:
            for h in range(2):
                take(feats.at[1, pl.ds(0, NY - 1), :, pl.ds(0, DH)], ag_recv_s.at[h, 1])
            each(0, NY, student_rows)
            plane_start(ITERS)
        plane_end(r)
        z_start(r)
        rscale[...] = 1.0 / z_end(r)
    tots[...] = z_end(ITERS)

    lossv[...] = jnp.zeros_like(lossv)
    gw[...] = jnp.zeros_like(gw)

    def row_of(ref, q):
        return jnp.concatenate([ref[pl.ds(q, 1), :], ref[pl.ds(q + 1, 1), :]], axis=1)

    def a_copy(yy, xp):
        xs = pl.ds(2 * xp, 2)
        return rcopy(part_a.at[yy, xs], in_a.at[y, xs], a_send.at[0], a_recv.at[xp], (dp_of(yy, x), j))

    def b_copy(xx, yy):
        return rcopy(part_b.at[xx, yy], in_b.at[x, yy], b_send.at[0], b_recv.at[yy], (dp_of(y, xx), j))

    def grad_rows(k):
        yy = nxt(y, k + 1, NY)

        def pair(xp):
            b = yy * HX + xp
            q = yy * NX + 2 * xp
            rs = row_of(rscale, q)
            tot = row_of(tots, q)
            inv_tot = 1.0 / tot
            log_tot = jnp.log(tot)
            lsum = jnp.zeros((8, 2 * SH), F32)
            for i in range(PC // CH):
                rows = slice(i * CH, (i + 1) * CH)
                lg = logit[b, rows, :]
                target = base[b, rows, :] * rs * two(colb[rows, :])
                lsum = lsum + jnp.sum((target * (lg - log_tot)).reshape(CH // 8, 8, 2 * SH), axis=0)
                gbuf[rows, :] = ((jnp.exp(lg) * inv_tot - target) * factor).astype(BF16)
            lossv[...] += lsum[:, :SH] + lsum[:, SH:]
            gs = dot(wn[0], gbuf[:CB, :]) + dot(wn[1], gbuf[CB:, :])
            part_a[yy, 2 * xp] = gs[:DH, :SH]
            part_a[yy, 2 * xp + 1] = gs[:DH, SH:]
            part_b[2 * xp, yy] = gs[DH:, :SH]
            part_b[2 * xp + 1, yy] = gs[DH:, SH:]

            @pl.when(k < NY - 1)
            def _():
                a_copy(yy, xp).start()

            for h in range(2):
                @pl.when(2 * xp + h != x)
                def _():
                    b_copy(2 * xp + h, yy).start()

            un = sn[b]
            for i, (cc, h) in enumerate(chunks):
                gw[cc, :, h * CH:(h + 1) * CH] += dot(un, gbuf[i * CH:(i + 1) * CH, :], ((1,), (1,)))

        each(0, HX, pair)

    each(0, NY, grad_rows)

    gw_copy = rcopy(gw.at[oc], gw_in, gw_sem.at[0], gw_sem.at[1], peer)
    gw_copy.start()

    plane_loss[p] = lossv[...]

    def l_start(k):
        slot = plane_loss.at[p]
        rcopy(slot, slot, l_send.at[0], l_recv.at[0], (nxt(p, k, NP), j)).start()

    each(1, NP, l_start)

    gw_copy.wait_recv()
    for h in range(CB // CH):
        s = slice(h * CH, (h + 1) * CH)
        u, inv = unit_cols(wraw[c, :, s])
        g = gw[c, :, s] + gw_in[:, s]
        gp_all[:, s] = inv * (g - u * jnp.sum(u * g, axis=0, keepdims=True))

    my_cols = pl.ds(pl.multiple_of(p * CB, CB), CB)

    def gp_copy(k):
        q = nxt(p, k, NP)
        rows = pl.ds(pl.multiple_of(q * DB, DB), DB)
        return rcopy(gp_all.at[rows], gp_ref.at[:, my_cols], gp_send.at[0], gp_recv.at[0], (q, j))

    def a_sum(xp):
        take(in_a.at[pl.ds(0, NY - 1), pl.ds(2 * xp, 2)], a_recv.at[xp])
        for h in range(2):
            xx = 2 * xp + h
            t = part_a[y, xx]
            for k in range(1, NY):
                t = t + in_a[nxt(y, k, NY), xx]
            sum_a[xx] = t

            @pl.when(xx != x)
            def _():
                a2_copy(xx, x).start()

    def a2_copy(xx, src):
        return rcopy(sum_a.at[xx], in_a2.at[src], a2_send.at[0], a2_recv.at[0], (dp_of(y, xx), j))

    def b_sum(yy):
        take(in_b.at[pl.ds(0, NX - 1), yy], b_recv.at[yy])
        t = part_b[x, yy]
        for k in range(1, NX):
            t = t + in_b[nxt(x, k, NX), yy]
        sum_b[yy] = t

    def b2_copy(yy, src):
        return rcopy(sum_b.at[yy], in_b2.at[src], b2_send.at[0], b2_recv.at[0], (dp_of(yy, x), j))

    def b_next(k):
        yy = nxt(y, k, NY)
        b_sum(yy)
        b2_copy(yy, y).start()

    each(1, NY, b_next)
    each(0, HX, a_sum)
    b_sum(y)
    gp_own = pltpu.make_async_copy(gp_all.at[w_rows], gp_ref.at[:, my_cols], own_sem.at[1])
    gp_own.start()

    take(plane_loss.at[pl.ds(0, NP - 1)], l_recv.at[0])
    loss_part = plane_loss[0]
    for q in range(1, NP):
        loss_part = loss_part + plane_loss[q]

    loss_row = jnp.sum(loss_part, axis=0, keepdims=True)

    take(in_a2.at[pl.ds(0, NX - 1)], a2_recv.at[0])
    take(in_b2.at[pl.ds(0, NY - 1)], b2_recv.at[0])
    su, sinv = unit_cols(feats[1, y, x])
    ga, gb = sum_a[x], sum_b[y]
    for k in range(1, NX):
        ga = ga + in_a2[nxt(x, k, NX)]
        gb = gb + in_b2[nxt(y, k, NY)]
    dots = jnp.sum(su[:DH] * ga, axis=0, keepdims=True) + jnp.sum(su[DH:] * gb, axis=0, keepdims=True)

    for q in range(NJ):
        lo = q * DB
        msg[q, :DB, :] = ga[lo:lo + DB] if lo < DH else gb[lo - DH:lo - DH + DB]
        msg[q, DB:DB + 1, :] = dots
        msg[q, DB + 1:DB + 2, :] = sinv
        msg[q, DB + 2:DB + 3, :] = loss_row
        msg[q, DB + 3:, :] = jnp.zeros((5, SH), F32)

    def m_copy(q, src):
        return rcopy(msg.at[q], msg_in.at[src], m_send.at[0], m_recv.at[0], (p, q))

    def m_start(k):
        m_copy(nxt(j, k, NJ), j).start()

    each(1, NJ, m_start)
    each(1, NP, lambda k: gp_copy(k).start())
    msg_in[j] = msg[j]

    take(msg_in.at[pl.ds(0, NJ - 1)], m_recv.at[0])
    loss_sum = jnp.zeros((1, SH), F32)
    for h in range(2):
        t = msg_in[h]
        for q in range(1, NZ):
            t = t + msg_in[2 * q + h]
        loss_sum = loss_sum + t[DB + 2:DB + 3]
        dsum = t[DB:DB + 1]
        inv = msg_in[h, DB + 1:DB + 2, :]
        own = s_ref[:, h * SH:(h + 1) * SH].astype(F32) * inv
        gs_ref[:, h * SH:(h + 1) * SH] = inv * (t[:DB] - own * dsum)
    loss_ref[0, 0] = -inv_rows * jnp.sum(loss_sum)

    take(gp_all.at[pl.ds(0, D - DB)], gp_recv.at[0])
    gp_own.wait()

    w_core.wait_send()
    gw_copy.wait_send()
    for r in range(ITERS + 1):
        if r < ITERS:
            take(core_col.at[r, 0], cc_send.at[r])
        take(plane_row.at[r, pl.ds(0, NP - 1)], pr_send.at[r])
        take(z_row.at[r, pl.ds(0, NZ - 1)], zr_send.at[r])
    for arr in range(2):
        take(feats.at[arr, 0, 0, pl.ds(0, D - DB)], f_send.at[arr])
        for h in range(2):
            take(base.at[0, pl.ds(0, ag_rows)], ag_send.at[arr, h])
    take(wraw.at[0, pl.ds(0, D - DB)], w_send.at[0])
    take(gp_all.at[pl.ds(0, D - DB)], gp_send.at[0])
    take(plane_loss.at[pl.ds(0, NP - 1)], l_send.at[0])
    take(msg_in.at[pl.ds(0, NJ - 1)], m_send.at[0])
    take(in_a2.at[pl.ds(0, NX - 1)], a2_send.at[0])
    take(in_b2.at[pl.ds(0, NY - 1)], b2_send.at[0])
    take(in_a.at[pl.ds(0, NY - 1)], a_send.at[0])
    take(in_b.at[pl.ds(0, NX - 1)], b_send.at[0])

def body(cfg, teacher_feats, student_feats, prototypes):
    NP, NJ, NY, NX, _, _ = cfg
    NZ = NJ // 2
    SB, DB = teacher_feats.shape
    SH = SB // 2
    D = DB * NJ
    DH = D // 2
    WC = prototypes.shape[1]
    CB = WC // NP
    PC = 2 * CB
    NB = NP // 2
    V, S = pltpu.VMEM, pltpu.SemaphoreType.DMA
    scratch = [
        V((2, NY, NX, D, SH), BF16), V((2, D, CB), BF16), V((2, D, CB), BF16), V((2, CB, D), BF16),
        V((NB, D, SB), BF16), V((NB, PC, SB), F32), V((NB, PC, SB), F32), V((PC, SH), F32),
        V((PC, SH), F32), V((NP, SH), F32), V((NP, SH), F32), V((PC, SB), BF16), V((8, SH), F32),
        V((ITERS, 2, 1, PC), F32), V((ITERS + 1, NP, NP, SH), F32), V((ITERS + 1, NZ, NP, SH), F32),
        V((2, D, CB), F32), V((D, CB), F32), V((D, CB), F32),
        V((NY, NX, DH, SH), F32), V((NX, NY, DH, SH), F32), V((NY, NX, DH, SH), F32), V((NX, NY, DH, SH), F32),
        V((NX, DH, SH), F32), V((NY, DH, SH), F32), V((NX, DH, SH), F32), V((NY, DH, SH), F32),
        V((NJ, DB + 8, SH), F32), V((NJ, DB + 8, SH), F32), V((NP, 8, SH), F32),
        S((2,)), S((2,)), S((1,)), S((1,)), S((2,)), S((2, 2)), S((2, NY, NX)), S((2, 2)), S((2,)),
        S((ITERS,)), S((ITERS,)), S((ITERS + 1,)), S((ITERS + 1,)), S((ITERS + 1,)), S((ITERS + 1,)),
        S((2,)), S((1,)), S((1,)),
        S((1,)), S((NX // 2,)), S((1,)), S((NY,)), S((1,)), S((1,)), S((1,)), S((1,)),
        S((1,)), S((1,)), S((1,)), S((1,)),
    ]
    vmem = pl.BlockSpec(memory_space=pltpu.VMEM)
    hbm = pl.BlockSpec(memory_space=pl.ANY)
    loss, gp, gs = pl.pallas_call(
        functools.partial(kernel, cfg),
        out_shape=(
            jax.ShapeDtypeStruct((1, 1), F32),
            pltpu.VMEM((DB, WC), F32),
            pltpu.VMEM((DB, SB), F32),
        ),
        in_specs=[vmem, vmem, hbm],
        out_specs=(pl.BlockSpec(memory_space=pltpu.SMEM), vmem, vmem),
        scratch_shapes=scratch,
        compiler_params=pltpu.CompilerParams(
            collective_id=0, has_side_effects=True, vmem_limit_bytes=56 * 1024 * 1024
        ),
    )(teacher_feats.T, student_feats.T, prototypes)
    return loss[0, 0], gp, gs.T


def solution(mesh):
    NP, NJ = mesh.shape["dp"], mesh.shape["proto"]
    NY = NX = int(round(NP ** 0.5))

    def run(teacher_feats, student_feats, prototypes):
        rows, protos = teacher_feats.shape[0], prototypes.shape[1]
        loss_scale = rows * protos // 256
        factor = float(loss_scale) / float(rows) / STUDENT_TEMP
        cfg = (NP, NJ, NY, NX, factor, 1.0 / rows)
        spec = P("dp", "proto")
        return jax.shard_map(
            functools.partial(body, cfg), mesh=mesh, in_specs=(spec,) * 3,
            out_specs=(P(), spec, spec), check_vma=False,
        )(teacher_feats, student_feats, prototypes)

    return run
```

```python
import functools

import jax
import jax.numpy as jnp
from jax import lax
from jax.experimental import pallas as pl
from jax.experimental.pallas import tpu as pltpu
from jax.sharding import PartitionSpec as P

ITERS = 3
EPS = 1e-06
TEACHER_TEMP = 0.07
STUDENT_TEMP = 0.1
MESH = pl.DeviceIdType.MESH
F32 = jnp.float32
BF16 = jnp.bfloat16


def rcopy(src, dst, send_sem, recv_sem, dev):
    return pltpu.make_async_remote_copy(
        src_ref=src, dst_ref=dst, send_sem=send_sem, recv_sem=recv_sem,
        device_id=dev, device_id_type=MESH,
    )


def take(ref, sem):
    pltpu.make_async_copy(ref, ref, sem).wait()


def each(lo, hi, fn):
    def step(k, carry):
        fn(k)
        return carry
    lax.fori_loop(lo, hi, step, 0)


def dot(a, b, dims=((1,), (0,))):
    return lax.dot_general(a, b, (dims, ((), ())), preferred_element_type=F32)


def kernel(
    cfg, t_ref, s_ref, w_ref, loss_ref, gp_ref, gs_ref,
    feats, wraw, wn, wtn, sn, base, logit, acc, colb, rscale, tots, gbuf, lossv,
    core_col, plane_row, z_row, gw, gw_in, gp_all,
    part_a, part_b, in_a, in_b, sum_a, sum_b, in_a2, in_b2, msg, msg_in, plane_loss,
    f_send, f_recv, w_send, w_recv, wc_sem, ag_send, ag_recv, ag_recv_s, own_sem,
    cc_send, cc_recv, pr_send, pr_recv, zr_send, zr_recv, gw_sem, gp_send, gp_recv,
    a_send, a_recv, b_send, b_recv, a2_send, a2_recv, b2_send, b2_recv,
    m_send, m_recv, l_send, l_recv,
):
    NP, NJ, NY, NX, factor, inv_rows = cfg
    NZ = NJ // 2
    DB = t_ref.shape[0]
    SH = t_ref.shape[1] // 2
    CB = wraw.shape[2]
    D = DB * NJ
    DH = D // 2
    PC = 2 * CB
    CH = min(256, CB)
    HX = NX // 2
    ag_rows = (NP - 1) * DH * SH // 2 // (2 * SH)
    p = lax.axis_index("dp")
    j = lax.axis_index("proto")
    y, x = p // NX, lax.rem(p, NX)
    z, c = j // 2, lax.rem(j, 2)
    oc = 1 - c
    peer = (p, 2 * z + oc)

    def dp_of(yy, xx):
        return yy * NX + xx

    def nxt(v, k, n):
        return lax.rem(v + k, n)

    def hops(k, n):
        return min(k, n - k)

    plane_off = sorted(
        ((dy, dx) for dy in range(NY) for dx in range(NX) if dy + dx > 0),
        key=lambda o: -hops(o[0], NY) - hops(o[1], NX))
    z_off = sorted(range(1, NZ), key=lambda k: -hops(k, NZ))

    def plane_peers():
        return [dp_of(nxt(y, dy, NY), nxt(x, dx, NX)) for dy, dx in plane_off]

    def proto_peers():
        return [2 * nxt(z, k, NZ) + cc for k in z_off for cc in (c, oc)] + [2 * z + oc]

    barrier = pltpu.get_barrier_semaphore()

    def greet_dp(k):
        pl.semaphore_signal(barrier, inc=1, device_id=(nxt(p, k, NP), j), device_id_type=MESH)

    def greet_proto(k):
        pl.semaphore_signal(barrier, inc=1, device_id=(p, nxt(j, k, NJ)), device_id_type=MESH)

    each(1, NP, greet_dp)
    each(1, NJ, greet_proto)
    pl.semaphore_wait(barrier, NP + NJ - 2)

    my_rows = pl.ds(pl.multiple_of(j * DB, DB), DB)
    my_half = pl.ds(pl.multiple_of(c * SH, SH), SH)

    def feat_copy(arr, q):
        lanes = pl.ds(pl.multiple_of(lax.rem(q, 2) * SH, SH), SH)
        src = (t_ref, s_ref)[arr].at[:, lanes]
        return rcopy(src, feats.at[arr, y, x, my_rows], f_send.at[arr], f_recv.at[arr], (p, q))

    for q in proto_peers():
        feat_copy(0, q).start()

    w_rows = pl.ds(pl.multiple_of(p * DB, DB), DB)

    def w_copy(k):
        q = nxt(p, k, NP)
        cols = pl.ds(pl.multiple_of(q * CB, CB), CB)
        return rcopy(w_ref.at[:, cols], wraw.at[c, w_rows], w_send.at[0], w_recv.at[0], (q, j))

    each(1, NP, lambda k: w_copy(k).start())
    each(1, NJ, lambda k: feat_copy(1, nxt(j, k, NJ)).start())
    feats[0, y, x, my_rows, :] = t_ref[:, my_half]
    feats[1, y, x, my_rows, :] = s_ref[:, my_half]
    w_own = pltpu.make_async_copy(
        w_ref.at[:, pl.ds(pl.multiple_of(p * CB, CB), CB)], wraw.at[c, w_rows], own_sem.at[0])
    w_own.start()

    def feat_wait(arr):
        take(feats.at[arr, y, x, pl.ds(0, D - DB)], f_recv.at[arr])

    near = sorted(range(1, NX), key=lambda k: min(k, NX - k))

    def ag_copy(arr, h, ys, xs, stage, dev):
        slot = feats.at[arr, ys, xs, pl.ds(h * DH, DH)]
        sem = ag_recv.at[h, ys, xs] if arr == 0 else ag_recv_s.at[h, stage]
        return rcopy(slot, slot, ag_send.at[arr, h], sem, dev)

    def ag_wait(arr, h, ys, xs):
        take(feats.at[arr, ys, xs, pl.ds(h * DH, DH)], ag_recv.at[h, ys, xs])

    def own_out(arr):
        for k in near:
            ag_copy(arr, 0, y, x, 0, (dp_of(y, nxt(x, k, NX)), j)).start()
            ag_copy(arr, 1, y, x, 0, (dp_of(nxt(y, k, NY), x), j)).start()
        for k in near:
            ag_copy(arr, 0, y, x, 1, (dp_of(nxt(y, k, NY), x), j)).start()
            ag_copy(arr, 1, y, x, 1, (dp_of(y, nxt(x, k, NX)), j)).start()

    def forward(arr):
        if arr == 1:
            for h in range(2):
                take(feats.at[1, 0, pl.ds(0, NX - 1), pl.ds(0, DH)], ag_recv_s.at[h, 0])
        for k in near:
            xs, ys = nxt(x, k, NX), nxt(y, k, NY)
            if arr == 0:
                ag_wait(0, 0, y, xs)
            each(1, NY, lambda m: ag_copy(arr, 0, y, xs, 1, (dp_of(nxt(y, m, NY), x), j)).start())
            if arr == 0:
                ag_wait(0, 1, ys, x)
            each(1, NX, lambda m: ag_copy(arr, 1, ys, x, 1, (dp_of(y, nxt(x, m, NX)), j)).start())

    def pair_wait(arr, yy, xp):
        def one(xx):
            @pl.when(yy != y)
            def _():
                @pl.when(xx != x)
                def _():
                    ag_wait(arr, 0, yy, xx)
                    ag_wait(arr, 1, yy, xx)

                @pl.when(xx == x)
                def _():
                    ag_wait(arr, 0, yy, xx)

            @pl.when(jnp.logical_and(yy == y, xx != x))
            def _():
                ag_wait(arr, 1, yy, xx)

        one(2 * xp)
        one(2 * xp + 1)

    feat_wait(0)
    own_out(0)

    take(wraw.at[c, pl.ds(0, D - DB)], w_recv.at[0])
    w_own.wait()
    w_core = rcopy(wraw.at[c], wraw.at[c], wc_sem.at[0], wc_sem.at[1], peer)
    w_core.start()
    forward(0)
    feat_wait(1)
    own_out(1)

    def unit_cols(v):
        v32 = v.astype(F32)
        inv = lax.rsqrt(jnp.sum(v32 * v32, axis=0, keepdims=True) + EPS)
        return v32 * inv, inv

    def w_norm(cc):
        for h in range(CB // CH):
            u, _ = unit_cols(wraw[cc, :, h * CH:(h + 1) * CH])
            wn[cc, :, h * CH:(h + 1) * CH] = u.astype(BF16)
            wtn[cc, h * CH:(h + 1) * CH, :] = u.T.astype(BF16)

    w_norm(c)
    w_core.wait_recv()
    w_norm(oc)

    chunks = [(cc, h) for cc in range(2) for h in range(CB // CH)]

    def two(a):
        return jnp.concatenate([a, a], axis=1)

    acc[...] = jnp.zeros_like(acc)

    def teacher_rows(k):
        yy = nxt(y, k + k // 2 - 2 * (k // 3), NY)

        def pair(xp):
            pair_wait(0, yy, xp)
            b = yy * HX + xp
            raw = jnp.concatenate([feats[0, yy, 2 * xp], feats[0, yy, 2 * xp + 1]], axis=1)
            u, _ = unit_cols(raw)
            tn = u.astype(BF16)
            for i, (cc, h) in enumerate(chunks):
                rows = slice(i * CH, (i + 1) * CH)
                e = jnp.exp(dot(wtn[cc, h * CH:(h + 1) * CH, :], tn) * (1.0 / TEACHER_TEMP))
                base[b, rows, :] = e
                acc[rows, :] += e[:, :SH] + e[:, SH:]

        each(0, HX, pair)

    each(0, NY, teacher_rows)

    def student_rows(yy):

        def pair(xp):
            b = yy * HX + xp

            raw = jnp.concatenate([feats[1, yy, 2 * xp], feats[1, yy, 2 * xp + 1]], axis=1)
            u, _ = unit_cols(raw)
            un = u.astype(BF16)
            sn[b] = un
            part = jnp.zeros((8, 2 * SH), F32)
            for i, (cc, h) in enumerate(chunks):
                rows = slice(i * CH, (i + 1) * CH)
                v = dot(wtn[cc, h * CH:(h + 1) * CH, :], un) * (1.0 / STUDENT_TEMP)
                logit[b, rows, :] = v
                part = part + jnp.sum(jnp.exp(v).reshape(CH // 8, 8, 2 * SH), axis=0)
            tot = jnp.sum(part, axis=0, keepdims=True)
            q = yy * NX + 2 * xp
            plane_row[ITERS, p, pl.ds(q, 1), :] = tot[:, :SH]
            plane_row[ITERS, p, pl.ds(q + 1, 1), :] = tot[:, SH:]

        each(0, HX, pair)

    def col_exchange(r):
        for i in range(PC // 128):
            core_col[r, c, :, i * 128:(i + 1) * 128] = jnp.sum(
                acc[i * 128:(i + 1) * 128, :].T, axis=0, keepdims=True)
        cp = rcopy(core_col.at[r, c], core_col.at[r, c], cc_send.at[r], cc_recv.at[r], peer)
        cp.start()
        cp.wait_recv()
        for i in range(PC // 128):
            s = slice(i * 128, (i + 1) * 128)
            v = 1.0 / (core_col[r, 0, :, s] + core_col[r, 1, :, s])
            colb[s, :] = jnp.broadcast_to(v, (128, 128)).T

    def col_pass():
        scale = rscale[...]

        def block(i):
            rows = pl.ds(pl.multiple_of(i * 64, 64), 64)
            a = jnp.zeros((64, SH), F32)
            for b in range(NP // 2):
                for h in range(2):
                    a = a + base[b, rows, h * SH:(h + 1) * SH] * scale[2 * b + h:2 * b + h + 1, :]
            acc[rows, :] = a

        each(0, PC // 64, block)

    def row_pass(r):
        def pair(b):
            for h in range(2):
                a = jnp.zeros((8, SH), F32)
                for i in range(PC // 64):
                    rows = slice(i * 64, (i + 1) * 64)
                    v = base[b, rows, h * SH:(h + 1) * SH] * colb[rows, :]
                    a = a + jnp.sum(v.reshape(8, 8, SH), axis=0)
                plane_row[r, p, pl.ds(2 * b + h, 1), :] = jnp.sum(a, axis=0, keepdims=True)

        each(0, NP // 2, pair)

    def plane_start(r):
        slot = plane_row.at[r, p]
        for q in plane_peers():
            rcopy(slot, slot, pr_send.at[r], pr_recv.at[r], (q, j)).start()

    def plane_end(r):
        take(plane_row.at[r, pl.ds(0, NP - 1)], pr_recv.at[r])
        total = plane_row[r, 0]
        for q in range(1, NP):
            total = total + plane_row[r, q]
        z_row[r, z] = total

    def z_start(r):
        slot = z_row.at[r, z]
        for k in z_off:
            rcopy(slot, slot, zr_send.at[r], zr_recv.at[r], (p, 2 * nxt(z, k, NZ) + c)).start()

    def z_end(r):
        take(z_row.at[r, pl.ds(0, NZ - 1)], zr_recv.at[r])
        total = z_row[r, 0]
        for q in range(1, NZ):
            total = total + z_row[r, q]
        return total

    for r in range(ITERS):
        if r == 2:
            plane_end(ITERS)
            z_start(ITERS)
        if r > 0:
            col_pass()
        col_exchange(r)
        row_pass(r)
        plane_start(r)
        if r == 0:
            forward(1)
        if r == 1:
            for h in range(2):
                take(feats.at[1, pl.ds(0, NY - 1), :, pl.ds(0, DH)], ag_recv_s.at[h, 1])
            each(0, NY, student_rows)
            plane_start(ITERS)
        plane_end(r)
        z_start(r)
        rscale[...] = 1.0 / z_end(r)
    tots[...] = z_end(ITERS)

    lossv[...] = jnp.zeros_like(lossv)
    gw[...] = jnp.zeros_like(gw)

    def row_of(ref, q):
        return jnp.concatenate([ref[pl.ds(q, 1), :], ref[pl.ds(q + 1, 1), :]], axis=1)

    def a_copy(yy, xp):
        xs = pl.ds(2 * xp, 2)
        return rcopy(part_a.at[yy, xs], in_a.at[y, xs], a_send.at[0], a_recv.at[xp], (dp_of(yy, x), j))

    def b_copy(xx, yy):
        return rcopy(part_b.at[xx, yy], in_b.at[x, yy], b_send.at[0], b_recv.at[yy], (dp_of(y, xx), j))

    def grad_rows(k):
        yy = nxt(y, k + 1, NY)

        def pair(xp):
            b = yy * HX + xp
            q = yy * NX + 2 * xp
            rs = row_of(rscale, q)
            tot = row_of(tots, q)
            inv_tot = 1.0 / tot
            log_tot = jnp.log(tot)
            lsum = jnp.zeros((8, 2 * SH), F32)
            for i in range(PC // CH):
                rows = slice(i * CH, (i + 1) * CH)
                lg = logit[b, rows, :]
                target = base[b, rows, :] * rs * two(colb[rows, :])
                lsum = lsum + jnp.sum((target * (lg - log_tot)).reshape(CH // 8, 8, 2 * SH), axis=0)
                gbuf[rows, :] = ((jnp.exp(lg) * inv_tot - target) * factor).astype(BF16)
            lossv[...] += lsum[:, :SH] + lsum[:, SH:]
            gs = dot(wn[0], gbuf[:CB, :]) + dot(wn[1], gbuf[CB:, :])
            part_a[yy, 2 * xp] = gs[:DH, :SH]
            part_a[yy, 2 * xp + 1] = gs[:DH, SH:]
            part_b[2 * xp, yy] = gs[DH:, :SH]
            part_b[2 * xp + 1, yy] = gs[DH:, SH:]

            @pl.when(k < NY - 1)
            def _():
                a_copy(yy, xp).start()

            for h in range(2):
                @pl.when(2 * xp + h != x)
                def _():
                    b_copy(2 * xp + h, yy).start()

            un = sn[b]
            for i, (cc, h) in enumerate(chunks):
                gw[cc, :, h * CH:(h + 1) * CH] += dot(un, gbuf[i * CH:(i + 1) * CH, :], ((1,), (1,)))

        each(0, HX, pair)

    each(0, NY, grad_rows)

    gw_copy = rcopy(gw.at[oc], gw_in, gw_sem.at[0], gw_sem.at[1], peer)
    gw_copy.start()

    plane_loss[p] = lossv[...]

    def l_start(k):
        slot = plane_loss.at[p]
        rcopy(slot, slot, l_send.at[0], l_recv.at[0], (nxt(p, k, NP), j)).start()

    each(1, NP, l_start)

    gw_copy.wait_recv()
    for h in range(CB // CH):
        s = slice(h * CH, (h + 1) * CH)
        u, inv = unit_cols(wraw[c, :, s])
        g = gw[c, :, s] + gw_in[:, s]
        gp_all[:, s] = inv * (g - u * jnp.sum(u * g, axis=0, keepdims=True))

    my_cols = pl.ds(pl.multiple_of(p * CB, CB), CB)

    def gp_copy(k):
        q = nxt(p, k, NP)
        rows = pl.ds(pl.multiple_of(q * DB, DB), DB)
        return rcopy(gp_all.at[rows], gp_ref.at[:, my_cols], gp_send.at[0], gp_recv.at[0], (q, j))

    def a_sum(xp):
        take(in_a.at[pl.ds(0, NY - 1), pl.ds(2 * xp, 2)], a_recv.at[xp])
        for h in range(2):
            xx = 2 * xp + h
            t = part_a[y, xx]
            for k in range(1, NY):
                t = t + in_a[nxt(y, k, NY), xx]
            sum_a[xx] = t

            @pl.when(xx != x)
            def _():
                a2_copy(xx, x).start()

    def a2_copy(xx, src):
        return rcopy(sum_a.at[xx], in_a2.at[src], a2_send.at[0], a2_recv.at[0], (dp_of(y, xx), j))

    def b_sum(yy):
        take(in_b.at[pl.ds(0, NX - 1), yy], b_recv.at[yy])
        t = part_b[x, yy]
        for k in range(1, NX):
            t = t + in_b[nxt(x, k, NX), yy]
        sum_b[yy] = t

    def b2_copy(yy, src):
        return rcopy(sum_b.at[yy], in_b2.at[src], b2_send.at[0], b2_recv.at[0], (dp_of(yy, x), j))

    def b_next(k):
        yy = nxt(y, k, NY)
        b_sum(yy)
        b2_copy(yy, y).start()

    each(1, NY, b_next)
    each(0, HX, a_sum)
    b_sum(y)
    gp_own = pltpu.make_async_copy(gp_all.at[w_rows], gp_ref.at[:, my_cols], own_sem.at[1])
    gp_own.start()

    take(plane_loss.at[pl.ds(0, NP - 1)], l_recv.at[0])
    loss_part = plane_loss[0]
    for q in range(1, NP):
        loss_part = loss_part + plane_loss[q]

    loss_row = jnp.sum(loss_part, axis=0, keepdims=True)

    take(in_a2.at[pl.ds(0, NX - 1)], a2_recv.at[0])
    take(in_b2.at[pl.ds(0, NY - 1)], b2_recv.at[0])
    su, sinv = unit_cols(feats[1, y, x])
    ga, gb = sum_a[x], sum_b[y]
    for k in range(1, NX):
        ga = ga + in_a2[nxt(x, k, NX)]
        gb = gb + in_b2[nxt(y, k, NY)]
    dots = jnp.sum(su[:DH] * ga, axis=0, keepdims=True) + jnp.sum(su[DH:] * gb, axis=0, keepdims=True)

    for q in range(NJ):
        lo = q * DB
        msg[q, :DB, :] = ga[lo:lo + DB] if lo < DH else gb[lo - DH:lo - DH + DB]
        msg[q, DB:DB + 1, :] = dots
        msg[q, DB + 1:DB + 2, :] = sinv
        msg[q, DB + 2:DB + 3, :] = loss_row
        msg[q, DB + 3:, :] = jnp.zeros((5, SH), F32)

    def m_copy(q, src):
        return rcopy(msg.at[q], msg_in.at[src], m_send.at[0], m_recv.at[0], (p, q))

    for q in proto_peers():
        m_copy(q, j).start()
    each(1, NP, lambda k: gp_copy(k).start())
    msg_in[j] = msg[j]

    take(msg_in.at[pl.ds(0, NJ - 1)], m_recv.at[0])
    loss_sum = jnp.zeros((1, SH), F32)
    for h in range(2):
        t = msg_in[h]
        for q in range(1, NZ):
            t = t + msg_in[2 * q + h]
        loss_sum = loss_sum + t[DB + 2:DB + 3]
        dsum = t[DB:DB + 1]
        inv = msg_in[h, DB + 1:DB + 2, :]
        own = s_ref[:, h * SH:(h + 1) * SH].astype(F32) * inv
        gs_ref[:, h * SH:(h + 1) * SH] = inv * (t[:DB] - own * dsum)
    loss_ref[0, 0] = -inv_rows * jnp.sum(loss_sum)

    take(gp_all.at[pl.ds(0, D - DB)], gp_recv.at[0])
    gp_own.wait()

    w_core.wait_send()
    gw_copy.wait_send()
    for r in range(ITERS + 1):
        if r < ITERS:
            take(core_col.at[r, 0], cc_send.at[r])
        take(plane_row.at[r, pl.ds(0, NP - 1)], pr_send.at[r])
        take(z_row.at[r, pl.ds(0, NZ - 1)], zr_send.at[r])
    for arr in range(2):
        take(feats.at[arr, 0, 0, pl.ds(0, D - DB)], f_send.at[arr])
        for h in range(2):
            take(base.at[0, pl.ds(0, ag_rows)], ag_send.at[arr, h])
    take(wraw.at[0, pl.ds(0, D - DB)], w_send.at[0])
    take(gp_all.at[pl.ds(0, D - DB)], gp_send.at[0])
    take(plane_loss.at[pl.ds(0, NP - 1)], l_send.at[0])
    take(msg_in.at[pl.ds(0, NJ - 1)], m_send.at[0])
    take(in_a2.at[pl.ds(0, NX - 1)], a2_send.at[0])
    take(in_b2.at[pl.ds(0, NY - 1)], b2_send.at[0])
    take(in_a.at[pl.ds(0, NY - 1)], a_send.at[0])
    take(in_b.at[pl.ds(0, NX - 1)], b_send.at[0])

def body(cfg, teacher_feats, student_feats, prototypes):
    NP, NJ, NY, NX, _, _ = cfg
    NZ = NJ // 2
    SB, DB = teacher_feats.shape
    SH = SB // 2
    D = DB * NJ
    DH = D // 2
    WC = prototypes.shape[1]
    CB = WC // NP
    PC = 2 * CB
    NB = NP // 2
    V, S = pltpu.VMEM, pltpu.SemaphoreType.DMA
    scratch = [
        V((2, NY, NX, D, SH), BF16), V((2, D, CB), BF16), V((2, D, CB), BF16), V((2, CB, D), BF16),
        V((NB, D, SB), BF16), V((NB, PC, SB), F32), V((NB, PC, SB), F32), V((PC, SH), F32),
        V((PC, SH), F32), V((NP, SH), F32), V((NP, SH), F32), V((PC, SB), BF16), V((8, SH), F32),
        V((ITERS, 2, 1, PC), F32), V((ITERS + 1, NP, NP, SH), F32), V((ITERS + 1, NZ, NP, SH), F32),
        V((2, D, CB), F32), V((D, CB), F32), V((D, CB), F32),
        V((NY, NX, DH, SH), F32), V((NX, NY, DH, SH), F32), V((NY, NX, DH, SH), F32), V((NX, NY, DH, SH), F32),
        V((NX, DH, SH), F32), V((NY, DH, SH), F32), V((NX, DH, SH), F32), V((NY, DH, SH), F32),
        V((NJ, DB + 8, SH), F32), V((NJ, DB + 8, SH), F32), V((NP, 8, SH), F32),
        S((2,)), S((2,)), S((1,)), S((1,)), S((2,)), S((2, 2)), S((2, NY, NX)), S((2, 2)), S((2,)),
        S((ITERS,)), S((ITERS,)), S((ITERS + 1,)), S((ITERS + 1,)), S((ITERS + 1,)), S((ITERS + 1,)),
        S((2,)), S((1,)), S((1,)),
        S((1,)), S((NX // 2,)), S((1,)), S((NY,)), S((1,)), S((1,)), S((1,)), S((1,)),
        S((1,)), S((1,)), S((1,)), S((1,)),
    ]
    vmem = pl.BlockSpec(memory_space=pltpu.VMEM)
    hbm = pl.BlockSpec(memory_space=pl.ANY)
    loss, gp, gs = pl.pallas_call(
        functools.partial(kernel, cfg),
        out_shape=(
            jax.ShapeDtypeStruct((1, 1), F32),
            pltpu.VMEM((DB, WC), F32),
            pltpu.VMEM((DB, SB), F32),
        ),
        in_specs=[vmem, vmem, hbm],
        out_specs=(pl.BlockSpec(memory_space=pltpu.SMEM), vmem, vmem),
        scratch_shapes=scratch,
        compiler_params=pltpu.CompilerParams(
            collective_id=0, has_side_effects=True, vmem_limit_bytes=56 * 1024 * 1024
        ),
    )(teacher_feats.T, student_feats.T, prototypes)
    return loss[0, 0], gp, gs.T


def solution(mesh):
    NP, NJ = mesh.shape["dp"], mesh.shape["proto"]
    NY = NX = int(round(NP ** 0.5))

    def run(teacher_feats, student_feats, prototypes):
        rows, protos = teacher_feats.shape[0], prototypes.shape[1]
        loss_scale = rows * protos // 256
        factor = float(loss_scale) / float(rows) / STUDENT_TEMP
        cfg = (NP, NJ, NY, NX, factor, 1.0 / rows)
        spec = P("dp", "proto")
        return jax.shard_map(
            functools.partial(body, cfg), mesh=mesh, in_specs=(spec,) * 3,
            out_specs=(P(), spec, spec), check_vma=False,
        )(teacher_feats, student_feats, prototypes)

    return run
```

```python
import functools

import jax
import jax.numpy as jnp
from jax import lax
from jax.experimental import pallas as pl
from jax.experimental.pallas import tpu as pltpu
from jax.sharding import PartitionSpec as P

ITERS = 3
EPS = 1e-06
TEACHER_TEMP = 0.07
STUDENT_TEMP = 0.1
MESH = pl.DeviceIdType.MESH
F32 = jnp.float32
BF16 = jnp.bfloat16


def rcopy(src, dst, send_sem, recv_sem, dev):
    return pltpu.make_async_remote_copy(
        src_ref=src, dst_ref=dst, send_sem=send_sem, recv_sem=recv_sem,
        device_id=dev, device_id_type=MESH,
    )


def take(ref, sem):
    pltpu.make_async_copy(ref, ref, sem).wait()


def each(lo, hi, fn):
    def step(k, carry):
        fn(k)
        return carry
    lax.fori_loop(lo, hi, step, 0)


def dot(a, b, dims=((1,), (0,))):
    return lax.dot_general(a, b, (dims, ((), ())), preferred_element_type=F32)


def kernel(
    cfg, t_ref, s_ref, w_ref, loss_ref, gp_ref, gs_ref,
    feats, wraw, wn, wtn, sn, base, logit, acc, colb, rscale, tots, gbuf, lossv,
    core_col, plane_row, z_row, gw, gw_in, gp_all,
    part_a, part_b, rel_a, rel_b, in_a, in_b, sum_a, sum_b, in_a2, in_b2, msg, msg_in, plane_loss,
    f_send, f_recv, w_send, w_recv, wc_sem, ag_send, ag_recv, ag_recv_s, own_sem,
    cc_send, cc_recv, pr_send, pr_recv, zr_send, zr_recv, gw_sem, gp_send, gp_recv,
    ra_recv, rb_recv, a_send, a_recv, b_send, b_recv, a2_send, a2_recv, b2_send, b2_recv,
    m_send, m_recv, l_send, l_recv,
):
    NP, NJ, NY, NX, factor, inv_rows = cfg
    NZ = NJ // 2
    DB = t_ref.shape[0]
    SH = t_ref.shape[1] // 2
    CB = wraw.shape[2]
    D = DB * NJ
    DH = D // 2
    PC = 2 * CB
    CH = min(256, CB)
    HX = NX // 2
    ag_rows = (NP - 1) * DH * SH // 2 // (2 * SH)
    p = lax.axis_index("dp")
    j = lax.axis_index("proto")
    y, x = p // NX, lax.rem(p, NX)
    z, c = j // 2, lax.rem(j, 2)
    oc = 1 - c
    peer = (p, 2 * z + oc)

    def dp_of(yy, xx):
        return yy * NX + xx

    def nxt(v, k, n):
        return lax.rem(v + k, n)

    def hops(k, n):
        return min(k, n - k)

    plane_off = sorted(
        ((dy, dx) for dy in range(NY) for dx in range(NX) if dy + dx > 0),
        key=lambda o: -hops(o[0], NY) - hops(o[1], NX))
    z_off = sorted(range(1, NZ), key=lambda k: -hops(k, NZ))

    def plane_peers():
        return [dp_of(nxt(y, dy, NY), nxt(x, dx, NX)) for dy, dx in plane_off]

    def proto_peers():
        return [2 * nxt(z, k, NZ) + cc for k in z_off for cc in (c, oc)] + [2 * z + oc]

    barrier = pltpu.get_barrier_semaphore()

    def greet_dp(k):
        pl.semaphore_signal(barrier, inc=1, device_id=(nxt(p, k, NP), j), device_id_type=MESH)

    def greet_proto(k):
        pl.semaphore_signal(barrier, inc=1, device_id=(p, nxt(j, k, NJ)), device_id_type=MESH)

    each(1, NP, greet_dp)
    each(1, NJ, greet_proto)
    pl.semaphore_wait(barrier, NP + NJ - 2)

    my_rows = pl.ds(pl.multiple_of(j * DB, DB), DB)
    my_half = pl.ds(pl.multiple_of(c * SH, SH), SH)

    def feat_copy(arr, q):
        lanes = pl.ds(pl.multiple_of(lax.rem(q, 2) * SH, SH), SH)
        src = (t_ref, s_ref)[arr].at[:, lanes]
        return rcopy(src, feats.at[arr, y, x, my_rows], f_send.at[arr], f_recv.at[arr], (p, q))

    for q in proto_peers():
        feat_copy(0, q).start()

    w_rows = pl.ds(pl.multiple_of(p * DB, DB), DB)

    def w_copy(k):
        q = nxt(p, k, NP)
        cols = pl.ds(pl.multiple_of(q * CB, CB), CB)
        return rcopy(w_ref.at[:, cols], wraw.at[c, w_rows], w_send.at[0], w_recv.at[0], (q, j))

    each(1, NP, lambda k: w_copy(k).start())
    each(1, NJ, lambda k: feat_copy(1, nxt(j, k, NJ)).start())
    feats[0, y, x, my_rows, :] = t_ref[:, my_half]
    feats[1, y, x, my_rows, :] = s_ref[:, my_half]
    w_own = pltpu.make_async_copy(
        w_ref.at[:, pl.ds(pl.multiple_of(p * CB, CB), CB)], wraw.at[c, w_rows], own_sem.at[0])
    w_own.start()

    def feat_wait(arr):
        take(feats.at[arr, y, x, pl.ds(0, D - DB)], f_recv.at[arr])

    near = sorted(range(1, NX), key=lambda k: min(k, NX - k))

    def ag_copy(arr, h, ys, xs, stage, dev):
        slot = feats.at[arr, ys, xs, pl.ds(h * DH, DH)]
        sem = ag_recv.at[h, ys, xs] if arr == 0 else ag_recv_s.at[h, stage]
        return rcopy(slot, slot, ag_send.at[arr, h], sem, dev)

    def ag_wait(arr, h, ys, xs):
        take(feats.at[arr, ys, xs, pl.ds(h * DH, DH)], ag_recv.at[h, ys, xs])

    def own_out(arr):
        for k in near:
            ag_copy(arr, 0, y, x, 0, (dp_of(y, nxt(x, k, NX)), j)).start()
            ag_copy(arr, 1, y, x, 0, (dp_of(nxt(y, k, NY), x), j)).start()
        for k in near:
            ag_copy(arr, 0, y, x, 1, (dp_of(nxt(y, k, NY), x), j)).start()
            ag_copy(arr, 1, y, x, 1, (dp_of(y, nxt(x, k, NX)), j)).start()

    def forward(arr):
        if arr == 1:
            for h in range(2):
                take(feats.at[1, 0, pl.ds(0, NX - 1), pl.ds(0, DH)], ag_recv_s.at[h, 0])
        for k in near:
            xs, ys = nxt(x, k, NX), nxt(y, k, NY)
            if arr == 0:
                ag_wait(0, 0, y, xs)
            each(1, NY, lambda m: ag_copy(arr, 0, y, xs, 1, (dp_of(nxt(y, m, NY), x), j)).start())
            if arr == 0:
                ag_wait(0, 1, ys, x)
            each(1, NX, lambda m: ag_copy(arr, 1, ys, x, 1, (dp_of(y, nxt(x, m, NX)), j)).start())

    def pair_wait(arr, yy, xp):
        def one(xx):
            @pl.when(yy != y)
            def _():
                @pl.when(xx != x)
                def _():
                    ag_wait(arr, 0, yy, xx)
                    ag_wait(arr, 1, yy, xx)

                @pl.when(xx == x)
                def _():
                    ag_wait(arr, 0, yy, xx)

            @pl.when(jnp.logical_and(yy == y, xx != x))
            def _():
                ag_wait(arr, 1, yy, xx)

        one(2 * xp)
        one(2 * xp + 1)

    feat_wait(0)
    own_out(0)

    take(wraw.at[c, pl.ds(0, D - DB)], w_recv.at[0])
    w_own.wait()
    w_core = rcopy(wraw.at[c], wraw.at[c], wc_sem.at[0], wc_sem.at[1], peer)
    w_core.start()
    forward(0)
    feat_wait(1)
    own_out(1)

    def unit_cols(v):
        v32 = v.astype(F32)
        inv = lax.rsqrt(jnp.sum(v32 * v32, axis=0, keepdims=True) + EPS)
        return v32 * inv, inv

    def w_norm(cc):
        for h in range(CB // CH):
            u, _ = unit_cols(wraw[cc, :, h * CH:(h + 1) * CH])
            wn[cc, :, h * CH:(h + 1) * CH] = u.astype(BF16)
            wtn[cc, h * CH:(h + 1) * CH, :] = u.T.astype(BF16)

    w_norm(c)
    w_core.wait_recv()
    w_norm(oc)

    chunks = [(cc, h) for cc in range(2) for h in range(CB // CH)]

    def two(a):
        return jnp.concatenate([a, a], axis=1)

    acc[...] = jnp.zeros_like(acc)

    def teacher_rows(k):
        yy = nxt(y, k + k // 2 - 2 * (k // 3), NY)

        def pair(xp):
            pair_wait(0, yy, xp)
            b = yy * HX + xp
            raw = jnp.concatenate([feats[0, yy, 2 * xp], feats[0, yy, 2 * xp + 1]], axis=1)
            u, _ = unit_cols(raw)
            tn = u.astype(BF16)
            for i, (cc, h) in enumerate(chunks):
                rows = slice(i * CH, (i + 1) * CH)
                e = jnp.exp(dot(wtn[cc, h * CH:(h + 1) * CH, :], tn) * (1.0 / TEACHER_TEMP))
                base[b, rows, :] = e
                acc[rows, :] += e[:, :SH] + e[:, SH:]

        each(0, HX, pair)

    each(0, NY, teacher_rows)

    def student_rows(yy):

        def pair(xp):
            b = yy * HX + xp

            raw = jnp.concatenate([feats[1, yy, 2 * xp], feats[1, yy, 2 * xp + 1]], axis=1)
            u, _ = unit_cols(raw)
            un = u.astype(BF16)
            sn[b] = un
            part = jnp.zeros((8, 2 * SH), F32)
            for i, (cc, h) in enumerate(chunks):
                rows = slice(i * CH, (i + 1) * CH)
                v = dot(wtn[cc, h * CH:(h + 1) * CH, :], un) * (1.0 / STUDENT_TEMP)
                logit[b, rows, :] = v
                part = part + jnp.sum(jnp.exp(v).reshape(CH // 8, 8, 2 * SH), axis=0)
            tot = jnp.sum(part, axis=0, keepdims=True)
            q = yy * NX + 2 * xp
            plane_row[ITERS, p, pl.ds(q, 1), :] = tot[:, :SH]
            plane_row[ITERS, p, pl.ds(q + 1, 1), :] = tot[:, SH:]

        each(0, HX, pair)

    def col_exchange(r):
        for i in range(PC // 128):
            core_col[r, c, :, i * 128:(i + 1) * 128] = jnp.sum(
                acc[i * 128:(i + 1) * 128, :].T, axis=0, keepdims=True)
        cp = rcopy(core_col.at[r, c], core_col.at[r, c], cc_send.at[r], cc_recv.at[r], peer)
        cp.start()
        cp.wait_recv()
        for i in range(PC // 128):
            s = slice(i * 128, (i + 1) * 128)
            v = 1.0 / (core_col[r, 0, :, s] + core_col[r, 1, :, s])
            colb[s, :] = jnp.broadcast_to(v, (128, 128)).T

    def col_pass():
        scale = rscale[...]

        def block(i):
            rows = pl.ds(pl.multiple_of(i * 64, 64), 64)
            a = jnp.zeros((64, SH), F32)
            for b in range(NP // 2):
                for h in range(2):
                    a = a + base[b, rows, h * SH:(h + 1) * SH] * scale[2 * b + h:2 * b + h + 1, :]
            acc[rows, :] = a

        each(0, PC // 64, block)

    def row_pass(r):
        def pair(b):
            for h in range(2):
                a = jnp.zeros((8, SH), F32)
                for i in range(PC // 64):
                    rows = slice(i * 64, (i + 1) * 64)
                    v = base[b, rows, h * SH:(h + 1) * SH] * colb[rows, :]
                    a = a + jnp.sum(v.reshape(8, 8, SH), axis=0)
                plane_row[r, p, pl.ds(2 * b + h, 1), :] = jnp.sum(a, axis=0, keepdims=True)

        each(0, NP // 2, pair)

    def plane_start(r):
        slot = plane_row.at[r, p]
        for q in plane_peers():
            rcopy(slot, slot, pr_send.at[r], pr_recv.at[r], (q, j)).start()

    def plane_end(r):
        take(plane_row.at[r, pl.ds(0, NP - 1)], pr_recv.at[r])
        total = plane_row[r, 0]
        for q in range(1, NP):
            total = total + plane_row[r, q]
        z_row[r, z] = total

    def z_start(r):
        slot = z_row.at[r, z]
        for k in z_off:
            rcopy(slot, slot, zr_send.at[r], zr_recv.at[r], (p, 2 * nxt(z, k, NZ) + c)).start()

    def z_end(r):
        take(z_row.at[r, pl.ds(0, NZ - 1)], zr_recv.at[r])
        total = z_row[r, 0]
        for q in range(1, NZ):
            total = total + z_row[r, q]
        return total

    for r in range(ITERS):
        if r == 2:
            plane_end(ITERS)
            z_start(ITERS)
        if r > 0:
            col_pass()
        col_exchange(r)
        row_pass(r)
        plane_start(r)
        if r == 0:
            forward(1)
        if r == 1:
            for h in range(2):
                take(feats.at[1, pl.ds(0, NY - 1), :, pl.ds(0, DH)], ag_recv_s.at[h, 1])
            each(0, NY, student_rows)
            plane_start(ITERS)
        plane_end(r)
        z_start(r)
        rscale[...] = 1.0 / z_end(r)
    tots[...] = z_end(ITERS)

    lossv[...] = jnp.zeros_like(lossv)
    gw[...] = jnp.zeros_like(gw)

    def row_of(ref, q):
        return jnp.concatenate([ref[pl.ds(q, 1), :], ref[pl.ds(q + 1, 1), :]], axis=1)

    def a_copy(yy, xp, slot):
        xs = pl.ds(2 * xp, 2)
        return rcopy(part_a.at[yy, xs], in_a.at[slot, xs], a_send.at[0], a_recv.at[xp], (dp_of(yy, x), j))

    def a_relay(yy, xp):
        dev = (dp_of(nxt(y, 1 + 2 * xp, NY), x), j)
        return rcopy(part_a.at[yy, pl.ds(2 * xp, 2)], rel_a.at[xp], a_send.at[0], ra_recv.at[xp], dev)

    def b_copy(xx, yy, slot):
        return rcopy(part_b.at[xx, yy], in_b.at[slot, yy], b_send.at[0], b_recv.at[yy], (dp_of(y, xx), j))

    def b_relay(xx, yy, e):
        dev = (dp_of(y, nxt(x, 1 + 2 * e, NX)), j)
        return rcopy(part_b.at[xx, yy], rel_b.at[yy], b_send.at[0], rb_recv.at[yy], dev)

    def row_at(k):
        n = NY - 1 - k
        return nxt(y, n + n // 2 - 2 * (n // 3), NY)

    def grad_rows(k):
        yy = row_at(k)
        e = lax.rem(yy, 2)

        def pair(xp):
            b = yy * HX + xp
            q = yy * NX + 2 * xp
            rs = row_of(rscale, q)
            tot = row_of(tots, q)
            inv_tot = 1.0 / tot
            log_tot = jnp.log(tot)
            lsum = jnp.zeros((8, 2 * SH), F32)
            for i in range(PC // CH):
                rows = slice(i * CH, (i + 1) * CH)
                lg = logit[b, rows, :]
                target = base[b, rows, :] * rs * two(colb[rows, :])
                lsum = lsum + jnp.sum((target * (lg - log_tot)).reshape(CH // 8, 8, 2 * SH), axis=0)
                gbuf[rows, :] = ((jnp.exp(lg) * inv_tot - target) * factor).astype(BF16)
            lossv[...] += lsum[:, :SH] + lsum[:, SH:]
            gs = dot(wn[0], gbuf[:CB, :]) + dot(wn[1], gbuf[CB:, :])
            part_a[yy, 2 * xp] = gs[:DH, :SH]
            part_a[yy, 2 * xp + 1] = gs[:DH, SH:]
            part_b[2 * xp, yy] = gs[DH:, :SH]
            part_b[2 * xp + 1, yy] = gs[DH:, SH:]

            @pl.when(k == 0)
            def _():
                a_relay(yy, xp).start()

            @pl.when(k == xp + 1)
            def _():
                a_copy(yy, xp, 1 - xp).start()

            for h in range(2):
                xx = 2 * xp + h
                d = lax.rem(xx - x + NX, NX)

                @pl.when(jnp.logical_and(k < NY - 1, d == 2))
                def _():
                    b_relay(xx, yy, e).start()

                @pl.when(jnp.logical_and(k == NY - 1, d == 2))
                def _():
                    b_copy(xx, yy, 2).start()

                @pl.when(d == 3 - 2 * e)
                def _():
                    b_copy(xx, yy, 1 - e).start()

                @pl.when(jnp.logical_and(k == NY - 1, d == 1 + 2 * e))
                def _():
                    b_copy(xx, yy, e).start()

            un = sn[b]
            for i, (cc, h) in enumerate(chunks):
                gw[cc, :, h * CH:(h + 1) * CH] += dot(un, gbuf[i * CH:(i + 1) * CH, :], ((1,), (1,)))

        each(0, HX, pair)

    each(0, NY, grad_rows)

    gw_copy = rcopy(gw.at[oc], gw_in, gw_sem.at[0], gw_sem.at[1], peer)
    gw_copy.start()
    for h in range(2):
        take(rel_a.at[h], ra_recv.at[h])
        dest = nxt(y, 1 + 2 * h, NY)
        for i in range(2):
            part_a[dest, 2 * h + i] += rel_a[h, i]
        a_copy(dest, h, h).start()

    def b_later(k):
        yy = row_at(k)
        e = lax.rem(yy, 2)
        xx = nxt(x, 1 + 2 * e, NX)
        take(rel_b.at[yy], rb_recv.at[yy])
        part_b[xx, yy] += rel_b[yy]
        b_copy(xx, yy, e).start()

    each(0, NY - 1, b_later)

    plane_loss[p] = lossv[...]

    def l_start(k):
        slot = plane_loss.at[p]
        rcopy(slot, slot, l_send.at[0], l_recv.at[0], (nxt(p, k, NP), j)).start()

    each(1, NP, l_start)

    gw_copy.wait_recv()
    for h in range(CB // CH):
        s = slice(h * CH, (h + 1) * CH)
        u, inv = unit_cols(wraw[c, :, s])
        g = gw[c, :, s] + gw_in[:, s]
        gp_all[:, s] = inv * (g - u * jnp.sum(u * g, axis=0, keepdims=True))

    my_cols = pl.ds(pl.multiple_of(p * CB, CB), CB)

    def gp_copy(k):
        q = nxt(p, k, NP)
        rows = pl.ds(pl.multiple_of(q * DB, DB), DB)
        return rcopy(gp_all.at[rows], gp_ref.at[:, my_cols], gp_send.at[0], gp_recv.at[0], (q, j))

    def a_sum(xp):
        take(in_a.at[pl.ds(0, 2), pl.ds(2 * xp, 2)], a_recv.at[xp])
        for h in range(2):
            xx = 2 * xp + h
            sum_a[xx] = part_a[y, xx] + in_a[0, xx] + in_a[1, xx]

            @pl.when(xx != x)
            def _():
                a2_copy(xx, x).start()

    def a2_copy(xx, src):
        return rcopy(sum_a.at[xx], in_a2.at[src], a2_send.at[0], a2_recv.at[0], (dp_of(y, xx), j))

    def b_sum(yy, n):
        take(in_b.at[pl.ds(0, n), yy], b_recv.at[yy])
        t = part_b[x, yy]
        for k in range(n):
            t = t + in_b[k, yy]
        sum_b[yy] = t

    def b2_copy(yy, src):
        return rcopy(sum_b.at[yy], in_b2.at[src], b2_send.at[0], b2_recv.at[0], (dp_of(yy, x), j))

    def b_next(k):
        yy = row_at(k)
        b_sum(yy, 2)
        b2_copy(yy, y).start()

    each(0, NY - 1, b_next)
    each(0, HX, a_sum)
    b_sum(y, 3)
    gp_own = pltpu.make_async_copy(gp_all.at[w_rows], gp_ref.at[:, my_cols], own_sem.at[1])
    gp_own.start()

    take(plane_loss.at[pl.ds(0, NP - 1)], l_recv.at[0])
    loss_part = plane_loss[0]
    for q in range(1, NP):
        loss_part = loss_part + plane_loss[q]

    loss_row = jnp.sum(loss_part, axis=0, keepdims=True)

    take(in_a2.at[pl.ds(0, NX - 1)], a2_recv.at[0])
    take(in_b2.at[pl.ds(0, NY - 1)], b2_recv.at[0])
    su, sinv = unit_cols(feats[1, y, x])
    ga, gb = sum_a[x], sum_b[y]
    for k in range(1, NX):
        ga = ga + in_a2[nxt(x, k, NX)]
        gb = gb + in_b2[nxt(y, k, NY)]
    dots = jnp.sum(su[:DH] * ga, axis=0, keepdims=True) + jnp.sum(su[DH:] * gb, axis=0, keepdims=True)

    for q in range(NJ):
        lo = q * DB
        msg[q, :DB, :] = ga[lo:lo + DB] if lo < DH else gb[lo - DH:lo - DH + DB]
        msg[q, DB:DB + 1, :] = dots
        msg[q, DB + 1:DB + 2, :] = sinv
        msg[q, DB + 2:DB + 3, :] = loss_row
        msg[q, DB + 3:, :] = jnp.zeros((5, SH), F32)

    def m_copy(q, src):
        return rcopy(msg.at[q], msg_in.at[src], m_send.at[0], m_recv.at[0], (p, q))

    for q in proto_peers():
        m_copy(q, j).start()
    each(1, NP, lambda k: gp_copy(k).start())
    msg_in[j] = msg[j]

    take(msg_in.at[pl.ds(0, NJ - 1)], m_recv.at[0])
    loss_sum = jnp.zeros((1, SH), F32)
    for h in range(2):
        t = msg_in[h]
        for q in range(1, NZ):
            t = t + msg_in[2 * q + h]
        loss_sum = loss_sum + t[DB + 2:DB + 3]
        dsum = t[DB:DB + 1]
        inv = msg_in[h, DB + 1:DB + 2, :]
        own = s_ref[:, h * SH:(h + 1) * SH].astype(F32) * inv
        gs_ref[:, h * SH:(h + 1) * SH] = inv * (t[:DB] - own * dsum)
    loss_ref[0, 0] = -inv_rows * jnp.sum(loss_sum)

    take(gp_all.at[pl.ds(0, D - DB)], gp_recv.at[0])
    gp_own.wait()

    w_core.wait_send()
    gw_copy.wait_send()
    for r in range(ITERS + 1):
        if r < ITERS:
            take(core_col.at[r, 0], cc_send.at[r])
        take(plane_row.at[r, pl.ds(0, NP - 1)], pr_send.at[r])
        take(z_row.at[r, pl.ds(0, NZ - 1)], zr_send.at[r])
    for arr in range(2):
        take(feats.at[arr, 0, 0, pl.ds(0, D - DB)], f_send.at[arr])
        for h in range(2):
            take(base.at[0, pl.ds(0, ag_rows)], ag_send.at[arr, h])
    take(wraw.at[0, pl.ds(0, D - DB)], w_send.at[0])
    take(gp_all.at[pl.ds(0, D - DB)], gp_send.at[0])
    take(plane_loss.at[pl.ds(0, NP - 1)], l_send.at[0])
    take(msg_in.at[pl.ds(0, NJ - 1)], m_send.at[0])
    take(in_a2.at[pl.ds(0, NX - 1)], a2_send.at[0])
    take(in_b2.at[pl.ds(0, NY - 1)], b2_send.at[0])
    take(in_a.at[pl.ds(0, NY - 1)], a_send.at[0])
    take(in_b.at[pl.ds(0, NX - 1)], b_send.at[0])

def body(cfg, teacher_feats, student_feats, prototypes):
    NP, NJ, NY, NX, _, _ = cfg
    NZ = NJ // 2
    SB, DB = teacher_feats.shape
    SH = SB // 2
    D = DB * NJ
    DH = D // 2
    WC = prototypes.shape[1]
    CB = WC // NP
    PC = 2 * CB
    NB = NP // 2
    V, S = pltpu.VMEM, pltpu.SemaphoreType.DMA
    scratch = [
        V((2, NY, NX, D, SH), BF16), V((2, D, CB), BF16), V((2, D, CB), BF16), V((2, CB, D), BF16),
        V((NB, D, SB), BF16), V((NB, PC, SB), F32), V((NB, PC, SB), F32), V((PC, SH), F32),
        V((PC, SH), F32), V((NP, SH), F32), V((NP, SH), F32), V((PC, SB), BF16), V((8, SH), F32),
        V((ITERS, 2, 1, PC), F32), V((ITERS + 1, NP, NP, SH), F32), V((ITERS + 1, NZ, NP, SH), F32),
        V((2, D, CB), F32), V((D, CB), F32), V((D, CB), F32),
        V((NY, NX, DH, SH), F32), V((NX, NY, DH, SH), F32), V((2, 2, DH, SH), F32), V((NY, DH, SH), F32),
        V((NY, NX, DH, SH), F32), V((NX, NY, DH, SH), F32),
        V((NX, DH, SH), F32), V((NY, DH, SH), F32), V((NX, DH, SH), F32), V((NY, DH, SH), F32),
        V((NJ, DB + 8, SH), F32), V((NJ, DB + 8, SH), F32), V((NP, 8, SH), F32),
        S((2,)), S((2,)), S((1,)), S((1,)), S((2,)), S((2, 2)), S((2, NY, NX)), S((2, 2)), S((2,)),
        S((ITERS,)), S((ITERS,)), S((ITERS + 1,)), S((ITERS + 1,)), S((ITERS + 1,)), S((ITERS + 1,)),
        S((2,)), S((1,)), S((1,)),
        S((2,)), S((NY,)), S((1,)), S((NX // 2,)), S((1,)), S((NY,)), S((1,)), S((1,)), S((1,)), S((1,)),
        S((1,)), S((1,)), S((1,)), S((1,)),
    ]
    vmem = pl.BlockSpec(memory_space=pltpu.VMEM)
    hbm = pl.BlockSpec(memory_space=pl.ANY)
    loss, gp, gs = pl.pallas_call(
        functools.partial(kernel, cfg),
        out_shape=(
            jax.ShapeDtypeStruct((1, 1), F32),
            pltpu.VMEM((DB, WC), F32),
            pltpu.VMEM((DB, SB), F32),
        ),
        in_specs=[vmem, vmem, hbm],
        out_specs=(pl.BlockSpec(memory_space=pltpu.SMEM), vmem, vmem),
        scratch_shapes=scratch,
        compiler_params=pltpu.CompilerParams(
            collective_id=0, has_side_effects=True, vmem_limit_bytes=56 * 1024 * 1024
        ),
    )(teacher_feats.T, student_feats.T, prototypes)
    return loss[0, 0], gp, gs.T


def solution(mesh):
    NP, NJ = mesh.shape["dp"], mesh.shape["proto"]
    NY = NX = int(round(NP ** 0.5))

    def run(teacher_feats, student_feats, prototypes):
        rows, protos = teacher_feats.shape[0], prototypes.shape[1]
        loss_scale = rows * protos // 256
        factor = float(loss_scale) / float(rows) / STUDENT_TEMP
        cfg = (NP, NJ, NY, NX, factor, 1.0 / rows)
        spec = P("dp", "proto")
        return jax.shard_map(
            functools.partial(body, cfg), mesh=mesh, in_specs=(spec,) * 3,
            out_specs=(P(), spec, spec), check_vma=False,
        )(teacher_feats, student_feats, prototypes)

    return run
```

```python
import functools

import jax
import jax.numpy as jnp
from jax import lax
from jax.experimental import pallas as pl
from jax.experimental.pallas import tpu as pltpu
from jax.sharding import PartitionSpec as P

ITERS = 3
EPS = 1e-06
TEACHER_TEMP = 0.07
STUDENT_TEMP = 0.1
MESH = pl.DeviceIdType.MESH
F32 = jnp.float32
BF16 = jnp.bfloat16


def rcopy(src, dst, send_sem, recv_sem, dev):
    return pltpu.make_async_remote_copy(
        src_ref=src, dst_ref=dst, send_sem=send_sem, recv_sem=recv_sem,
        device_id=dev, device_id_type=MESH,
    )


def take(ref, sem):
    pltpu.make_async_copy(ref, ref, sem).wait()


def each(lo, hi, fn):
    def step(k, carry):
        fn(k)
        return carry
    lax.fori_loop(lo, hi, step, 0)


def dot(a, b, dims=((1,), (0,))):
    return lax.dot_general(a, b, (dims, ((), ())), preferred_element_type=F32)


def kernel(
    cfg, t_hbm, s_hbm, w_ref, loss_ref, gp_ref, gs_ref,
    t_ref, s_ref,
    feats, wraw, wn, wtn, sn, base, logit, acc, colb, rscale, tots, gbuf, lossv,
    core_col, plane_row, z_row, gw, gw_in, gp_all,
    part_a, part_b, rel_a, rel_b, in_a, in_b, sum_a, sum_b, in_a2, in_b2, msg, msg_in, plane_loss,
    f_send, f_recv, w_send, w_recv, wc_sem, ag_send, ag_recv, ag_recv_s, own_sem,
    cc_send, cc_recv, pr_send, pr_recv, zr_send, zr_recv, gw_sem, gp_send, gp_recv,
    ra_recv, rb_recv, a_send, a_recv, b_send, b_recv, a2_send, a2_recv, b2_send, b2_recv,
    m_send, m_recv, l_send, l_recv,
):
    NP, NJ, NY, NX, factor, inv_rows = cfg
    NZ = NJ // 2
    DB = t_ref.shape[0]
    SH = t_ref.shape[1] // 2
    CB = wraw.shape[2]
    D = DB * NJ
    DH = D // 2
    PC = 2 * CB
    CH = min(256, CB)
    HX = NX // 2
    ag_rows = (NP - 1) * DH * SH // 2 // (2 * SH)
    p = lax.axis_index("dp")
    j = lax.axis_index("proto")
    y, x = p // NX, lax.rem(p, NX)
    z, c = j // 2, lax.rem(j, 2)
    oc = 1 - c
    peer = (p, 2 * z + oc)

    def dp_of(yy, xx):
        return yy * NX + xx

    def nxt(v, k, n):
        return lax.rem(v + k, n)

    def hops(k, n):
        return min(k, n - k)

    plane_off = sorted(
        ((dy, dx) for dy in range(NY) for dx in range(NX) if dy + dx > 0),
        key=lambda o: -hops(o[0], NY) - hops(o[1], NX))
    z_off = sorted(range(1, NZ), key=lambda k: -hops(k, NZ))

    def plane_peers():
        return [dp_of(nxt(y, dy, NY), nxt(x, dx, NX)) for dy, dx in plane_off]

    def proto_peers():
        return [2 * nxt(z, k, NZ) + cc for k in z_off for cc in (c, oc)] + [2 * z + oc]

    barrier = pltpu.get_barrier_semaphore()

    def greet_dp(k):
        pl.semaphore_signal(barrier, inc=1, device_id=(nxt(p, k, NP), j), device_id_type=MESH)

    def greet_proto(k):
        pl.semaphore_signal(barrier, inc=1, device_id=(p, nxt(j, k, NJ)), device_id_type=MESH)

    each(1, NP, greet_dp)
    each(1, NJ, greet_proto)
    t_in = pltpu.make_async_copy(t_hbm, t_ref, own_sem.at[2])
    s_in = pltpu.make_async_copy(s_hbm, s_ref, own_sem.at[3])
    t_in.start()
    s_in.start()
    pl.semaphore_wait(barrier, NP + NJ - 2)
    t_in.wait()
    s_in.wait()

    my_rows = pl.ds(pl.multiple_of(j * DB, DB), DB)
    my_half = pl.ds(pl.multiple_of(c * SH, SH), SH)

    def feat_copy(arr, q):
        lanes = pl.ds(pl.multiple_of(lax.rem(q, 2) * SH, SH), SH)
        src = (t_ref, s_ref)[arr].at[:, lanes]
        return rcopy(src, feats.at[arr, y, x, my_rows], f_send.at[arr], f_recv.at[arr], (p, q))

    for q in proto_peers():
        feat_copy(0, q).start()

    w_rows = pl.ds(pl.multiple_of(p * DB, DB), DB)

    def w_copy(k):
        q = nxt(p, k, NP)
        cols = pl.ds(pl.multiple_of(q * CB, CB), CB)
        return rcopy(w_ref.at[:, cols], wraw.at[c, w_rows], w_send.at[0], w_recv.at[0], (q, j))

    each(1, NP, lambda k: w_copy(k).start())
    each(1, NJ, lambda k: feat_copy(1, nxt(j, k, NJ)).start())
    feats[0, y, x, my_rows, :] = t_ref[:, my_half]
    feats[1, y, x, my_rows, :] = s_ref[:, my_half]
    w_own = pltpu.make_async_copy(
        w_ref.at[:, pl.ds(pl.multiple_of(p * CB, CB), CB)], wraw.at[c, w_rows], own_sem.at[0])
    w_own.start()

    def feat_wait(arr):
        take(feats.at[arr, y, x, pl.ds(0, D - DB)], f_recv.at[arr])

    near = sorted(range(1, NX), key=lambda k: min(k, NX - k))

    def ag_copy(arr, h, ys, xs, stage, dev):
        slot = feats.at[arr, ys, xs, pl.ds(h * DH, DH)]
        sem = ag_recv.at[h, ys, xs] if arr == 0 else ag_recv_s.at[h, stage]
        return rcopy(slot, slot, ag_send.at[arr, h], sem, dev)

    def ag_wait(arr, h, ys, xs):
        take(feats.at[arr, ys, xs, pl.ds(h * DH, DH)], ag_recv.at[h, ys, xs])

    def own_out(arr):
        for k in near:
            ag_copy(arr, 0, y, x, 0, (dp_of(y, nxt(x, k, NX)), j)).start()
            ag_copy(arr, 1, y, x, 0, (dp_of(nxt(y, k, NY), x), j)).start()
        for k in near:
            ag_copy(arr, 0, y, x, 1, (dp_of(nxt(y, k, NY), x), j)).start()
            ag_copy(arr, 1, y, x, 1, (dp_of(y, nxt(x, k, NX)), j)).start()

    def forward(arr):
        if arr == 1:
            for h in range(2):
                take(feats.at[1, 0, pl.ds(0, NX - 1), pl.ds(0, DH)], ag_recv_s.at[h, 0])
        for k in near:
            xs, ys = nxt(x, k, NX), nxt(y, k, NY)
            if arr == 0:
                ag_wait(0, 0, y, xs)
            each(1, NY, lambda m: ag_copy(arr, 0, y, xs, 1, (dp_of(nxt(y, m, NY), x), j)).start())
            if arr == 0:
                ag_wait(0, 1, ys, x)
            each(1, NX, lambda m: ag_copy(arr, 1, ys, x, 1, (dp_of(y, nxt(x, m, NX)), j)).start())

    def pair_wait(arr, yy, xp):
        def one(xx):
            @pl.when(yy != y)
            def _():
                @pl.when(xx != x)
                def _():
                    ag_wait(arr, 0, yy, xx)
                    ag_wait(arr, 1, yy, xx)

                @pl.when(xx == x)
                def _():
                    ag_wait(arr, 0, yy, xx)

            @pl.when(jnp.logical_and(yy == y, xx != x))
            def _():
                ag_wait(arr, 1, yy, xx)

        one(2 * xp)
        one(2 * xp + 1)

    feat_wait(0)
    own_out(0)

    take(wraw.at[c, pl.ds(0, D - DB)], w_recv.at[0])
    w_own.wait()
    w_core = rcopy(wraw.at[c], wraw.at[c], wc_sem.at[0], wc_sem.at[1], peer)
    w_core.start()
    forward(0)
    feat_wait(1)
    own_out(1)

    def unit_cols(v):
        v32 = v.astype(F32)
        inv = lax.rsqrt(jnp.sum(v32 * v32, axis=0, keepdims=True) + EPS)
        return v32 * inv, inv

    def w_norm(cc):
        for h in range(CB // CH):
            u, _ = unit_cols(wraw[cc, :, h * CH:(h + 1) * CH])
            wn[cc, :, h * CH:(h + 1) * CH] = u.astype(BF16)
            wtn[cc, h * CH:(h + 1) * CH, :] = u.T.astype(BF16)

    w_norm(c)
    w_core.wait_recv()
    w_norm(oc)

    chunks = [(cc, h) for cc in range(2) for h in range(CB // CH)]

    def two(a):
        return jnp.concatenate([a, a], axis=1)

    acc[...] = jnp.zeros_like(acc)

    def teacher_rows(k):
        yy = nxt(y, k + k // 2 - 2 * (k // 3), NY)

        def pair(xp):
            pair_wait(0, yy, xp)
            b = yy * HX + xp
            raw = jnp.concatenate([feats[0, yy, 2 * xp], feats[0, yy, 2 * xp + 1]], axis=1)
            u, _ = unit_cols(raw)
            tn = u.astype(BF16)
            for i, (cc, h) in enumerate(chunks):
                rows = slice(i * CH, (i + 1) * CH)
                e = jnp.exp(dot(wtn[cc, h * CH:(h + 1) * CH, :], tn) * (1.0 / TEACHER_TEMP))
                base[b, rows, :] = e
                acc[rows, :] += e[:, :SH] + e[:, SH:]

        each(0, HX, pair)

    each(0, NY, teacher_rows)

    def student_rows(yy):

        def pair(xp):
            b = yy * HX + xp

            raw = jnp.concatenate([feats[1, yy, 2 * xp], feats[1, yy, 2 * xp + 1]], axis=1)
            u, _ = unit_cols(raw)
            un = u.astype(BF16)
            sn[b] = un
            part = jnp.zeros((8, 2 * SH), F32)
            for i, (cc, h) in enumerate(chunks):
                rows = slice(i * CH, (i + 1) * CH)
                v = dot(wtn[cc, h * CH:(h + 1) * CH, :], un) * (1.0 / STUDENT_TEMP)
                logit[b, rows, :] = v
                part = part + jnp.sum(jnp.exp(v).reshape(CH // 8, 8, 2 * SH), axis=0)
            tot = jnp.sum(part, axis=0, keepdims=True)
            q = yy * NX + 2 * xp
            plane_row[ITERS, p, pl.ds(q, 1), :] = tot[:, :SH]
            plane_row[ITERS, p, pl.ds(q + 1, 1), :] = tot[:, SH:]

        each(0, HX, pair)

    def col_exchange(r):
        for i in range(PC // 128):
            core_col[r, c, :, i * 128:(i + 1) * 128] = jnp.sum(
                acc[i * 128:(i + 1) * 128, :].T, axis=0, keepdims=True)
        cp = rcopy(core_col.at[r, c], core_col.at[r, c], cc_send.at[r], cc_recv.at[r], peer)
        cp.start()
        cp.wait_recv()
        for i in range(PC // 128):
            s = slice(i * 128, (i + 1) * 128)
            v = 1.0 / (core_col[r, 0, :, s] + core_col[r, 1, :, s])
            colb[s, :] = jnp.broadcast_to(v, (128, 128)).T

    def col_pass():
        scale = rscale[...]

        def block(i):
            rows = pl.ds(pl.multiple_of(i * 64, 64), 64)
            a = jnp.zeros((64, SH), F32)
            for b in range(NP // 2):
                for h in range(2):
                    a = a + base[b, rows, h * SH:(h + 1) * SH] * scale[2 * b + h:2 * b + h + 1, :]
            acc[rows, :] = a

        each(0, PC // 64, block)

    def row_pass(r):
        def pair(b):
            for h in range(2):
                a = jnp.zeros((8, SH), F32)
                for i in range(PC // 64):
                    rows = slice(i * 64, (i + 1) * 64)
                    v = base[b, rows, h * SH:(h + 1) * SH] * colb[rows, :]
                    a = a + jnp.sum(v.reshape(8, 8, SH), axis=0)
                plane_row[r, p, pl.ds(2 * b + h, 1), :] = jnp.sum(a, axis=0, keepdims=True)

        each(0, NP // 2, pair)

    def plane_start(r):
        slot = plane_row.at[r, p]
        for q in plane_peers():
            rcopy(slot, slot, pr_send.at[r], pr_recv.at[r], (q, j)).start()

    def plane_end(r):
        take(plane_row.at[r, pl.ds(0, NP - 1)], pr_recv.at[r])
        total = plane_row[r, 0]
        for q in range(1, NP):
            total = total + plane_row[r, q]
        z_row[r, z] = total

    def z_start(r):
        slot = z_row.at[r, z]
        for k in z_off:
            rcopy(slot, slot, zr_send.at[r], zr_recv.at[r], (p, 2 * nxt(z, k, NZ) + c)).start()

    def z_end(r):
        take(z_row.at[r, pl.ds(0, NZ - 1)], zr_recv.at[r])
        total = z_row[r, 0]
        for q in range(1, NZ):
            total = total + z_row[r, q]
        return total

    for r in range(ITERS):
        if r > 0:
            col_pass()
        col_exchange(r)
        row_pass(r)
        plane_start(r)
        if r == 0:
            forward(1)
        if r == 1:
            for h in range(2):
                take(feats.at[1, pl.ds(0, NY - 1), :, pl.ds(0, DH)], ag_recv_s.at[h, 1])
            each(0, NY, student_rows)
        if r == 2:
            plane_end(ITERS)
            z_start(ITERS)
        plane_end(r)
        z_start(r)
        if r == 1:
            plane_start(ITERS)
        rscale[...] = 1.0 / z_end(r)
    tots[...] = z_end(ITERS)

    lossv[...] = jnp.zeros_like(lossv)
    gw[...] = jnp.zeros_like(gw)

    def row_of(ref, q):
        return jnp.concatenate([ref[pl.ds(q, 1), :], ref[pl.ds(q + 1, 1), :]], axis=1)

    def a_copy(yy, xp, slot):
        xs = pl.ds(2 * xp, 2)
        return rcopy(part_a.at[yy, xs], in_a.at[slot, xs], a_send.at[0], a_recv.at[xp], (dp_of(yy, x), j))

    def a_relay(yy, xp):
        dev = (dp_of(nxt(y, 1 + 2 * xp, NY), x), j)
        return rcopy(part_a.at[yy, pl.ds(2 * xp, 2)], rel_a.at[xp], a_send.at[0], ra_recv.at[xp], dev)

    def b_copy(xx, yy, slot):
        return rcopy(part_b.at[xx, yy], in_b.at[slot, yy], b_send.at[0], b_recv.at[yy], (dp_of(y, xx), j))

    def b_relay(xx, yy, e):
        dev = (dp_of(y, nxt(x, 1 + 2 * e, NX)), j)
        return rcopy(part_b.at[xx, yy], rel_b.at[yy], b_send.at[0], rb_recv.at[yy], dev)

    def row_at(k):
        n = NY - 1 - k
        return nxt(y, n + n // 2 - 2 * (n // 3), NY)

    def grad_rows(k):
        yy = row_at(k)
        e = lax.rem(yy, 2)

        def pair(xp):
            b = yy * HX + xp
            q = yy * NX + 2 * xp
            rs = row_of(rscale, q)
            tot = row_of(tots, q)
            inv_tot = 1.0 / tot
            log_tot = jnp.log(tot)
            lsum = jnp.zeros((8, 2 * SH), F32)
            for i in range(PC // CH):
                rows = slice(i * CH, (i + 1) * CH)
                lg = logit[b, rows, :]
                target = base[b, rows, :] * rs * two(colb[rows, :])
                lsum = lsum + jnp.sum((target * (lg - log_tot)).reshape(CH // 8, 8, 2 * SH), axis=0)
                gbuf[rows, :] = ((jnp.exp(lg) * inv_tot - target) * factor).astype(BF16)
            lossv[...] += lsum[:, :SH] + lsum[:, SH:]
            gs = dot(wn[0], gbuf[:CB, :]) + dot(wn[1], gbuf[CB:, :])
            part_a[yy, 2 * xp] = gs[:DH, :SH]
            part_a[yy, 2 * xp + 1] = gs[:DH, SH:]
            part_b[2 * xp, yy] = gs[DH:, :SH]
            part_b[2 * xp + 1, yy] = gs[DH:, SH:]

            @pl.when(k == 0)
            def _():
                a_relay(yy, xp).start()

            @pl.when(k == xp + 1)
            def _():
                a_copy(yy, xp, 1 - xp).start()

            for h in range(2):
                xx = 2 * xp + h
                d = lax.rem(xx - x + NX, NX)

                @pl.when(jnp.logical_and(k < NY - 1, d == 2))
                def _():
                    b_relay(xx, yy, e).start()

                @pl.when(jnp.logical_and(k == NY - 1, d == 2))
                def _():
                    b_copy(xx, yy, 2).start()

                @pl.when(d == 3 - 2 * e)
                def _():
                    b_copy(xx, yy, 1 - e).start()

                @pl.when(jnp.logical_and(k == NY - 1, d == 1 + 2 * e))
                def _():
                    b_copy(xx, yy, e).start()

            un = sn[b]
            for i, (cc, h) in enumerate(chunks):
                gw[cc, :, h * CH:(h + 1) * CH] += dot(un, gbuf[i * CH:(i + 1) * CH, :], ((1,), (1,)))

        each(0, HX, pair)

    each(0, NY, grad_rows)

    gw_copy = rcopy(gw.at[oc], gw_in, gw_sem.at[0], gw_sem.at[1], peer)
    gw_copy.start()
    for h in range(2):
        take(rel_a.at[h], ra_recv.at[h])
        dest = nxt(y, 1 + 2 * h, NY)
        for i in range(2):
            part_a[dest, 2 * h + i] += rel_a[h, i]
        a_copy(dest, h, h).start()

    def b_later(k):
        yy = row_at(k)
        e = lax.rem(yy, 2)
        xx = nxt(x, 1 + 2 * e, NX)
        take(rel_b.at[yy], rb_recv.at[yy])
        part_b[xx, yy] += rel_b[yy]
        b_copy(xx, yy, e).start()

    each(0, NY - 1, b_later)

    plane_loss[p] = lossv[...]

    def l_start(k):
        slot = plane_loss.at[p]
        rcopy(slot, slot, l_send.at[0], l_recv.at[0], (nxt(p, k, NP), j)).start()

    each(1, NP, l_start)

    gw_copy.wait_recv()
    for h in range(CB // CH):
        s = slice(h * CH, (h + 1) * CH)
        u, inv = unit_cols(wraw[c, :, s])
        g = gw[c, :, s] + gw_in[:, s]
        gp_all[:, s] = inv * (g - u * jnp.sum(u * g, axis=0, keepdims=True))

    my_cols = pl.ds(pl.multiple_of(p * CB, CB), CB)

    def gp_copy(k):
        q = nxt(p, k, NP)
        rows = pl.ds(pl.multiple_of(q * DB, DB), DB)
        return rcopy(gp_all.at[rows], gp_ref.at[:, my_cols], gp_send.at[0], gp_recv.at[0], (q, j))

    def a_sum(xp):
        take(in_a.at[pl.ds(0, 2), pl.ds(2 * xp, 2)], a_recv.at[xp])
        for h in range(2):
            xx = 2 * xp + h
            sum_a[xx] = part_a[y, xx] + in_a[0, xx] + in_a[1, xx]

            @pl.when(xx != x)
            def _():
                a2_copy(xx, x).start()

    def a2_copy(xx, src):
        return rcopy(sum_a.at[xx], in_a2.at[src], a2_send.at[0], a2_recv.at[0], (dp_of(y, xx), j))

    def b_sum(yy, n):
        take(in_b.at[pl.ds(0, n), yy], b_recv.at[yy])
        t = part_b[x, yy]
        for k in range(n):
            t = t + in_b[k, yy]
        sum_b[yy] = t

    def b2_copy(yy, src):
        return rcopy(sum_b.at[yy], in_b2.at[src], b2_send.at[0], b2_recv.at[0], (dp_of(yy, x), j))

    def b_next(k):
        yy = row_at(k)
        b_sum(yy, 2)
        b2_copy(yy, y).start()

    each(0, NY - 1, b_next)
    each(0, HX, a_sum)
    b_sum(y, 3)
    gp_own = pltpu.make_async_copy(gp_all.at[w_rows], gp_ref.at[:, my_cols], own_sem.at[1])
    gp_own.start()

    take(plane_loss.at[pl.ds(0, NP - 1)], l_recv.at[0])
    loss_part = plane_loss[0]
    for q in range(1, NP):
        loss_part = loss_part + plane_loss[q]

    loss_row = jnp.sum(loss_part, axis=0, keepdims=True)

    su, sinv = unit_cols(feats[1, y, x])
    for q in range(NJ):
        msg[q, DB + 1:DB + 2, :] = sinv
        msg[q, DB + 2:DB + 3, :] = loss_row
        msg[q, DB + 3:, :] = jnp.zeros((5, SH), F32)
    take(in_a2.at[pl.ds(0, NX - 1)], a2_recv.at[0])
    take(in_b2.at[pl.ds(0, NY - 1)], b2_recv.at[0])
    ga, gb = sum_a[x], sum_b[y]
    for k in range(1, NX):
        ga = ga + in_a2[nxt(x, k, NX)]
        gb = gb + in_b2[nxt(y, k, NY)]
    dots = jnp.sum(su[:DH] * ga, axis=0, keepdims=True) + jnp.sum(su[DH:] * gb, axis=0, keepdims=True)

    for q in range(NJ):
        lo = q * DB
        msg[q, :DB, :] = ga[lo:lo + DB] if lo < DH else gb[lo - DH:lo - DH + DB]
        msg[q, DB:DB + 1, :] = dots

    def m_copy(q, src):
        return rcopy(msg.at[q], msg_in.at[src], m_send.at[0], m_recv.at[0], (p, q))

    for q in proto_peers():
        m_copy(q, j).start()
    each(1, NP, lambda k: gp_copy(k).start())
    msg_in[j] = msg[j]

    take(msg_in.at[pl.ds(0, NJ - 1)], m_recv.at[0])
    loss_sum = jnp.zeros((1, SH), F32)
    for h in range(2):
        t = msg_in[h]
        for q in range(1, NZ):
            t = t + msg_in[2 * q + h]
        loss_sum = loss_sum + t[DB + 2:DB + 3]
        dsum = t[DB:DB + 1]
        inv = msg_in[h, DB + 1:DB + 2, :]
        own = s_ref[:, h * SH:(h + 1) * SH].astype(F32) * inv
        gs_ref[:, h * SH:(h + 1) * SH] = inv * (t[:DB] - own * dsum)
    loss_ref[0, 0] = -inv_rows * jnp.sum(loss_sum)

    take(gp_all.at[pl.ds(0, D - DB)], gp_recv.at[0])
    gp_own.wait()

    w_core.wait_send()
    gw_copy.wait_send()
    for r in range(ITERS + 1):
        if r < ITERS:
            take(core_col.at[r, 0], cc_send.at[r])
        take(plane_row.at[r, pl.ds(0, NP - 1)], pr_send.at[r])
        take(z_row.at[r, pl.ds(0, NZ - 1)], zr_send.at[r])
    for arr in range(2):
        take(feats.at[arr, 0, 0, pl.ds(0, D - DB)], f_send.at[arr])
        for h in range(2):
            take(base.at[0, pl.ds(0, ag_rows)], ag_send.at[arr, h])
    take(wraw.at[0, pl.ds(0, D - DB)], w_send.at[0])
    take(gp_all.at[pl.ds(0, D - DB)], gp_send.at[0])
    take(plane_loss.at[pl.ds(0, NP - 1)], l_send.at[0])
    take(msg_in.at[pl.ds(0, NJ - 1)], m_send.at[0])
    take(in_a2.at[pl.ds(0, NX - 1)], a2_send.at[0])
    take(in_b2.at[pl.ds(0, NY - 1)], b2_send.at[0])
    take(in_a.at[pl.ds(0, NY - 1)], a_send.at[0])
    take(in_b.at[pl.ds(0, NX - 1)], b_send.at[0])

def body(cfg, teacher_feats, student_feats, prototypes):
    NP, NJ, NY, NX, _, _ = cfg
    NZ = NJ // 2
    SB, DB = teacher_feats.shape
    SH = SB // 2
    D = DB * NJ
    DH = D // 2
    WC = prototypes.shape[1]
    CB = WC // NP
    PC = 2 * CB
    NB = NP // 2
    V, S = pltpu.VMEM, pltpu.SemaphoreType.DMA
    scratch = [
        V((DB, SB), BF16), V((DB, SB), BF16),
        V((2, NY, NX, D, SH), BF16), V((2, D, CB), BF16), V((2, D, CB), BF16), V((2, CB, D), BF16),
        V((NB, D, SB), BF16), V((NB, PC, SB), F32), V((NB, PC, SB), F32), V((PC, SH), F32),
        V((PC, SH), F32), V((NP, SH), F32), V((NP, SH), F32), V((PC, SB), BF16), V((8, SH), F32),
        V((ITERS, 2, 1, PC), F32), V((ITERS + 1, NP, NP, SH), F32), V((ITERS + 1, NZ, NP, SH), F32),
        V((2, D, CB), F32), V((D, CB), F32), V((D, CB), F32),
        V((NY, NX, DH, SH), F32), V((NX, NY, DH, SH), F32), V((2, 2, DH, SH), F32), V((NY, DH, SH), F32),
        V((NY, NX, DH, SH), F32), V((NX, NY, DH, SH), F32),
        V((NX, DH, SH), F32), V((NY, DH, SH), F32), V((NX, DH, SH), F32), V((NY, DH, SH), F32),
        V((NJ, DB + 8, SH), F32), V((NJ, DB + 8, SH), F32), V((NP, 8, SH), F32),
        S((2,)), S((2,)), S((1,)), S((1,)), S((2,)), S((2, 2)), S((2, NY, NX)), S((2, 2)), S((4,)),
        S((ITERS,)), S((ITERS,)), S((ITERS + 1,)), S((ITERS + 1,)), S((ITERS + 1,)), S((ITERS + 1,)),
        S((2,)), S((1,)), S((1,)),
        S((2,)), S((NY,)), S((1,)), S((NX // 2,)), S((1,)), S((NY,)), S((1,)), S((1,)), S((1,)), S((1,)),
        S((1,)), S((1,)), S((1,)), S((1,)),
    ]
    vmem = pl.BlockSpec(memory_space=pltpu.VMEM)
    hbm = pl.BlockSpec(memory_space=pl.ANY)
    loss, gp, gs = pl.pallas_call(
        functools.partial(kernel, cfg),
        out_shape=(
            jax.ShapeDtypeStruct((1, 1), F32),
            pltpu.VMEM((DB, WC), F32),
            pltpu.VMEM((DB, SB), F32),
        ),
        in_specs=[hbm, hbm, hbm],
        out_specs=(pl.BlockSpec(memory_space=pltpu.SMEM), vmem, vmem),
        scratch_shapes=scratch,
        compiler_params=pltpu.CompilerParams(
            collective_id=0, has_side_effects=True, vmem_limit_bytes=56 * 1024 * 1024
        ),
    )(teacher_feats.T, student_feats.T, prototypes)
    return loss[0, 0], gp, gs.T


def solution(mesh):
    NP, NJ = mesh.shape["dp"], mesh.shape["proto"]
    NY = NX = int(round(NP ** 0.5))

    def run(teacher_feats, student_feats, prototypes):
        rows, protos = teacher_feats.shape[0], prototypes.shape[1]
        loss_scale = rows * protos // 256
        factor = float(loss_scale) / float(rows) / STUDENT_TEMP
        cfg = (NP, NJ, NY, NX, factor, 1.0 / rows)
        spec = P("dp", "proto")
        return jax.shard_map(
            functools.partial(body, cfg), mesh=mesh, in_specs=(spec,) * 3,
            out_specs=(P(), spec, spec), check_vma=False,
        )(teacher_feats, student_feats, prototypes)

    return run
```

```python
import functools

import jax
import jax.numpy as jnp
from jax import lax
from jax.experimental import pallas as pl
from jax.experimental.pallas import tpu as pltpu
from jax.sharding import PartitionSpec as P

ITERS = 3
EPS = 1e-06
TEACHER_TEMP = 0.07
STUDENT_TEMP = 0.1
MESH = pl.DeviceIdType.MESH
F32 = jnp.float32
BF16 = jnp.bfloat16


def rcopy(src, dst, send_sem, recv_sem, dev):
    return pltpu.make_async_remote_copy(
        src_ref=src, dst_ref=dst, send_sem=send_sem, recv_sem=recv_sem,
        device_id=dev, device_id_type=MESH,
    )


def take(ref, sem):
    pltpu.make_async_copy(ref, ref, sem).wait()


def each(lo, hi, fn):
    def step(k, carry):
        fn(k)
        return carry
    lax.fori_loop(lo, hi, step, 0)


def dot(a, b, dims=((1,), (0,))):
    return lax.dot_general(a, b, (dims, ((), ())), preferred_element_type=F32)


def kernel(
    cfg, t_hbm, s_hbm, w_ref, loss_ref, gp_ref, gs_ref,
    t_ref, s_ref,
    feats, wraw, wn, wtn, sn, base, logit, acc, colb, rscale, tots, gbuf, lossv,
    core_col, plane_row, z_row, gw, gw_in, gp_all,
    part_a, part_b, rel_a, rel_b, in_a, in_b, sum_a, sum_b, in_a2, in_b2, msg, msg_in, plane_loss,
    f_send, f_recv, w_send, w_recv, wc_sem, ag_send, ag_recv, ag_recv_s, own_sem,
    cc_send, cc_recv, pr_send, pr_recv, zr_send, zr_recv, gw_sem, gp_send, gp_recv,
    ra_recv, rb_recv, a_send, a_recv, b_send, b_recv, a2_send, a2_recv, b2_send, b2_recv,
    m_send, m_recv, l_send, l_recv,
):
    NP, NJ, NY, NX, factor, inv_rows = cfg
    NZ = NJ // 2
    DB = t_ref.shape[0]
    SH = t_ref.shape[1] // 2
    CB = wraw.shape[2]
    D = DB * NJ
    DH = D // 2
    PC = 2 * CB
    CH = min(256, CB)
    HX = NX // 2
    ag_rows = (NP - 1) * DH * SH // 2 // (2 * SH)
    p = lax.axis_index("dp")
    j = lax.axis_index("proto")
    y, x = p // NX, lax.rem(p, NX)
    z, c = j // 2, lax.rem(j, 2)
    oc = 1 - c
    peer = (p, 2 * z + oc)

    def dp_of(yy, xx):
        return yy * NX + xx

    def nxt(v, k, n):
        return lax.rem(v + k, n)

    def hops(k, n):
        return min(k, n - k)

    plane_off = sorted(
        ((dy, dx) for dy in range(NY) for dx in range(NX) if dy + dx > 0),
        key=lambda o: -hops(o[0], NY) - hops(o[1], NX))
    z_off = sorted(range(1, NZ), key=lambda k: -hops(k, NZ))

    def plane_peers():
        return [dp_of(nxt(y, dy, NY), nxt(x, dx, NX)) for dy, dx in plane_off]

    def proto_peers():
        return [2 * nxt(z, k, NZ) + cc for k in z_off for cc in (c, oc)] + [2 * z + oc]

    barrier = pltpu.get_barrier_semaphore()

    def greet_dp(k):
        pl.semaphore_signal(barrier, inc=1, device_id=(nxt(p, k, NP), j), device_id_type=MESH)

    def greet_proto(k):
        pl.semaphore_signal(barrier, inc=1, device_id=(p, nxt(j, k, NJ)), device_id_type=MESH)

    each(1, NP, greet_dp)
    each(1, NJ, greet_proto)
    t_in = pltpu.make_async_copy(t_hbm, t_ref, own_sem.at[2])
    s_in = pltpu.make_async_copy(s_hbm, s_ref, own_sem.at[3])
    t_in.start()
    s_in.start()
    pl.semaphore_wait(barrier, NP + NJ - 2)
    t_in.wait()
    s_in.wait()

    my_rows = pl.ds(pl.multiple_of(j * DB, DB), DB)
    my_half = pl.ds(pl.multiple_of(c * SH, SH), SH)

    def feat_copy(arr, q):
        lanes = pl.ds(pl.multiple_of(lax.rem(q, 2) * SH, SH), SH)
        src = (t_ref, s_ref)[arr].at[:, lanes]
        return rcopy(src, feats.at[arr, y, x, my_rows], f_send.at[arr], f_recv.at[arr], (p, q))

    for q in proto_peers():
        feat_copy(0, q).start()

    w_rows = pl.ds(pl.multiple_of(p * DB, DB), DB)

    def w_copy(k):
        q = nxt(p, k, NP)
        cols = pl.ds(pl.multiple_of(q * CB, CB), CB)
        return rcopy(w_ref.at[:, cols], wraw.at[c, w_rows], w_send.at[0], w_recv.at[0], (q, j))

    each(1, NP, lambda k: w_copy(k).start())
    each(1, NJ, lambda k: feat_copy(1, nxt(j, k, NJ)).start())
    feats[0, y, x, my_rows, :] = t_ref[:, my_half]
    feats[1, y, x, my_rows, :] = s_ref[:, my_half]
    w_own = pltpu.make_async_copy(
        w_ref.at[:, pl.ds(pl.multiple_of(p * CB, CB), CB)], wraw.at[c, w_rows], own_sem.at[0])
    w_own.start()

    def feat_wait(arr):
        take(feats.at[arr, y, x, pl.ds(0, D - DB)], f_recv.at[arr])

    near = sorted(range(1, NX), key=lambda k: min(k, NX - k))

    def ag_copy(arr, h, ys, xs, stage, dev):
        slot = feats.at[arr, ys, xs, pl.ds(h * DH, DH)]
        sem = ag_recv.at[h, ys, xs] if arr == 0 else ag_recv_s.at[h, stage]
        return rcopy(slot, slot, ag_send.at[arr, h], sem, dev)

    def ag_wait(arr, h, ys, xs):
        take(feats.at[arr, ys, xs, pl.ds(h * DH, DH)], ag_recv.at[h, ys, xs])

    def own_out(arr):
        for k in near:
            ag_copy(arr, 0, y, x, 0, (dp_of(y, nxt(x, k, NX)), j)).start()
            ag_copy(arr, 1, y, x, 0, (dp_of(nxt(y, k, NY), x), j)).start()
        for k in near:
            ag_copy(arr, 0, y, x, 1, (dp_of(nxt(y, k, NY), x), j)).start()
            ag_copy(arr, 1, y, x, 1, (dp_of(y, nxt(x, k, NX)), j)).start()

    def forward(arr):
        if arr == 1:
            for h in range(2):
                take(feats.at[1, 0, pl.ds(0, NX - 1), pl.ds(0, DH)], ag_recv_s.at[h, 0])
        for k in near:
            xs, ys = nxt(x, k, NX), nxt(y, k, NY)
            if arr == 0:
                ag_wait(0, 0, y, xs)
            each(1, NY, lambda m: ag_copy(arr, 0, y, xs, 1, (dp_of(nxt(y, m, NY), x), j)).start())
            if arr == 0:
                ag_wait(0, 1, ys, x)
            each(1, NX, lambda m: ag_copy(arr, 1, ys, x, 1, (dp_of(y, nxt(x, m, NX)), j)).start())

    def pair_wait(arr, yy, xp):
        def one(xx):
            @pl.when(yy != y)
            def _():
                @pl.when(xx != x)
                def _():
                    ag_wait(arr, 0, yy, xx)
                    ag_wait(arr, 1, yy, xx)

                @pl.when(xx == x)
                def _():
                    ag_wait(arr, 0, yy, xx)

            @pl.when(jnp.logical_and(yy == y, xx != x))
            def _():
                ag_wait(arr, 1, yy, xx)

        one(2 * xp)
        one(2 * xp + 1)

    feat_wait(0)
    own_out(0)

    take(wraw.at[c, pl.ds(0, D - DB)], w_recv.at[0])
    w_own.wait()
    w_core = rcopy(wraw.at[c], wraw.at[c], wc_sem.at[0], wc_sem.at[1], peer)
    w_core.start()
    forward(0)

    def unit_cols(v):
        v32 = v.astype(F32)
        inv = lax.rsqrt(jnp.sum(v32 * v32, axis=0, keepdims=True) + EPS)
        return v32 * inv, inv

    def w_norm(cc):
        for h in range(CB // CH):
            u, _ = unit_cols(wraw[cc, :, h * CH:(h + 1) * CH])
            wn[cc, :, h * CH:(h + 1) * CH] = u.astype(BF16)
            wtn[cc, h * CH:(h + 1) * CH, :] = u.T.astype(BF16)

    w_norm(c)
    w_core.wait_recv()
    w_norm(oc)

    chunks = [(cc, h) for cc in range(2) for h in range(CB // CH)]

    def two(a):
        return jnp.concatenate([a, a], axis=1)

    acc[...] = jnp.zeros_like(acc)

    def teacher_rows(k):
        yy = nxt(y, k + k // 2 - 2 * (k // 3), NY)

        def pair(xp):
            pair_wait(0, yy, xp)
            b = yy * HX + xp
            raw = jnp.concatenate([feats[0, yy, 2 * xp], feats[0, yy, 2 * xp + 1]], axis=1)
            u, _ = unit_cols(raw)
            tn = u.astype(BF16)
            for i, (cc, h) in enumerate(chunks):
                rows = slice(i * CH, (i + 1) * CH)
                e = jnp.exp(dot(wtn[cc, h * CH:(h + 1) * CH, :], tn) * (1.0 / TEACHER_TEMP))
                base[b, rows, :] = e
                acc[rows, :] += e[:, :SH] + e[:, SH:]

        each(0, HX, pair)

    each(0, NY, teacher_rows)
    feat_wait(1)
    own_out(1)

    def student_rows(yy):

        def pair(xp):
            b = yy * HX + xp

            raw = jnp.concatenate([feats[1, yy, 2 * xp], feats[1, yy, 2 * xp + 1]], axis=1)
            u, _ = unit_cols(raw)
            un = u.astype(BF16)
            sn[b] = un
            part = jnp.zeros((8, 2 * SH), F32)
            for i, (cc, h) in enumerate(chunks):
                rows = slice(i * CH, (i + 1) * CH)
                v = dot(wtn[cc, h * CH:(h + 1) * CH, :], un) * (1.0 / STUDENT_TEMP)
                logit[b, rows, :] = v
                part = part + jnp.sum(jnp.exp(v).reshape(CH // 8, 8, 2 * SH), axis=0)
            tot = jnp.sum(part, axis=0, keepdims=True)
            q = yy * NX + 2 * xp
            plane_row[ITERS, p, pl.ds(q, 1), :] = tot[:, :SH]
            plane_row[ITERS, p, pl.ds(q + 1, 1), :] = tot[:, SH:]

        each(0, HX, pair)

    def col_exchange(r):
        for i in range(PC // 128):
            core_col[r, c, :, i * 128:(i + 1) * 128] = jnp.sum(
                acc[i * 128:(i + 1) * 128, :].T, axis=0, keepdims=True)
        cp = rcopy(core_col.at[r, c], core_col.at[r, c], cc_send.at[r], cc_recv.at[r], peer)
        cp.start()
        cp.wait_recv()
        for i in range(PC // 128):
            s = slice(i * 128, (i + 1) * 128)
            v = 1.0 / (core_col[r, 0, :, s] + core_col[r, 1, :, s])
            colb[s, :] = jnp.broadcast_to(v, (128, 128)).T

    def col_pass():
        scale = rscale[...]

        def block(i):
            rows = pl.ds(pl.multiple_of(i * 64, 64), 64)
            a = jnp.zeros((64, SH), F32)
            for b in range(NP // 2):
                for h in range(2):
                    a = a + base[b, rows, h * SH:(h + 1) * SH] * scale[2 * b + h:2 * b + h + 1, :]
            acc[rows, :] = a

        each(0, PC // 64, block)

    def row_pass(r):
        def pair(b):
            for h in range(2):
                a = jnp.zeros((8, SH), F32)
                for i in range(PC // 64):
                    rows = slice(i * 64, (i + 1) * 64)
                    v = base[b, rows, h * SH:(h + 1) * SH] * colb[rows, :]
                    a = a + jnp.sum(v.reshape(8, 8, SH), axis=0)
                plane_row[r, p, pl.ds(2 * b + h, 1), :] = jnp.sum(a, axis=0, keepdims=True)

        each(0, NP // 2, pair)

    def plane_start(r):
        slot = plane_row.at[r, p]
        for q in plane_peers():
            rcopy(slot, slot, pr_send.at[r], pr_recv.at[r], (q, j)).start()

    def plane_end(r):
        take(plane_row.at[r, pl.ds(0, NP - 1)], pr_recv.at[r])
        total = plane_row[r, 0]
        for q in range(1, NP):
            total = total + plane_row[r, q]
        z_row[r, z] = total

    def z_start(r):
        slot = z_row.at[r, z]
        for k in z_off:
            rcopy(slot, slot, zr_send.at[r], zr_recv.at[r], (p, 2 * nxt(z, k, NZ) + c)).start()

    def z_end(r):
        take(z_row.at[r, pl.ds(0, NZ - 1)], zr_recv.at[r])
        total = z_row[r, 0]
        for q in range(1, NZ):
            total = total + z_row[r, q]
        return total

    for r in range(ITERS):
        if r > 0:
            col_pass()
        col_exchange(r)
        row_pass(r)
        plane_start(r)
        if r == 1:
            for h in range(2):
                take(feats.at[1, pl.ds(0, NY - 1), :, pl.ds(0, DH)], ag_recv_s.at[h, 1])
            each(0, NY, student_rows)
        if r == 2:
            plane_end(ITERS)
            z_start(ITERS)
        plane_end(r)
        z_start(r)
        if r == 0:
            forward(1)
        if r == 1:
            plane_start(ITERS)
        rscale[...] = 1.0 / z_end(r)
    tots[...] = z_end(ITERS)

    lossv[...] = jnp.zeros_like(lossv)
    gw[...] = jnp.zeros_like(gw)

    def row_of(ref, q):
        return jnp.concatenate([ref[pl.ds(q, 1), :], ref[pl.ds(q + 1, 1), :]], axis=1)

    def a_copy(yy, xp, slot):
        xs = pl.ds(2 * xp, 2)
        return rcopy(part_a.at[yy, xs], in_a.at[slot, xs], a_send.at[0], a_recv.at[xp], (dp_of(yy, x), j))

    def a_relay(yy, xp):
        dev = (dp_of(nxt(y, 1 + 2 * xp, NY), x), j)
        return rcopy(part_a.at[yy, pl.ds(2 * xp, 2)], rel_a.at[xp], a_send.at[0], ra_recv.at[xp], dev)

    def b_copy(xx, yy, slot):
        return rcopy(part_b.at[xx, yy], in_b.at[slot, yy], b_send.at[0], b_recv.at[yy], (dp_of(y, xx), j))

    def b_relay(xx, yy, e):
        dev = (dp_of(y, nxt(x, 1 + 2 * e, NX)), j)
        return rcopy(part_b.at[xx, yy], rel_b.at[yy], b_send.at[0], rb_recv.at[yy], dev)

    def row_at(k):
        n = NY - 1 - k
        return nxt(y, n + n // 2 - 2 * (n // 3), NY)

    def grad_rows(k):
        yy = row_at(k)
        e = lax.rem(yy, 2)

        def pair(xp):
            b = yy * HX + xp
            q = yy * NX + 2 * xp
            rs = row_of(rscale, q)
            tot = row_of(tots, q)
            inv_tot = 1.0 / tot
            log_tot = jnp.log(tot)
            lsum = jnp.zeros((8, 2 * SH), F32)
            for i in range(PC // CH):
                rows = slice(i * CH, (i + 1) * CH)
                lg = logit[b, rows, :]
                target = base[b, rows, :] * rs * two(colb[rows, :])
                lsum = lsum + jnp.sum((target * (lg - log_tot)).reshape(CH // 8, 8, 2 * SH), axis=0)
                gbuf[rows, :] = ((jnp.exp(lg) * inv_tot - target) * factor).astype(BF16)
            lossv[...] += lsum[:, :SH] + lsum[:, SH:]
            gs = dot(wn[0], gbuf[:CB, :]) + dot(wn[1], gbuf[CB:, :])
            part_a[yy, 2 * xp] = gs[:DH, :SH]
            part_a[yy, 2 * xp + 1] = gs[:DH, SH:]
            part_b[2 * xp, yy] = gs[DH:, :SH]
            part_b[2 * xp + 1, yy] = gs[DH:, SH:]

            @pl.when(k == 0)
            def _():
                a_relay(yy, xp).start()

            @pl.when(k == xp + 1)
            def _():
                a_copy(yy, xp, 1 - xp).start()

            for h in range(2):
                xx = 2 * xp + h
                d = lax.rem(xx - x + NX, NX)

                @pl.when(jnp.logical_and(k < NY - 1, d == 2))
                def _():
                    b_relay(xx, yy, e).start()

                @pl.when(jnp.logical_and(k == NY - 1, d == 2))
                def _():
                    b_copy(xx, yy, 2).start()

                @pl.when(d == 3 - 2 * e)
                def _():
                    b_copy(xx, yy, 1 - e).start()

                @pl.when(jnp.logical_and(k == NY - 1, d == 1 + 2 * e))
                def _():
                    b_copy(xx, yy, e).start()

            un = sn[b]
            for i, (cc, h) in enumerate(chunks):
                gw[cc, :, h * CH:(h + 1) * CH] += dot(un, gbuf[i * CH:(i + 1) * CH, :], ((1,), (1,)))

        each(0, HX, pair)

    each(0, NY, grad_rows)

    gw_copy = rcopy(gw.at[oc], gw_in, gw_sem.at[0], gw_sem.at[1], peer)
    gw_copy.start()
    for h in range(2):
        take(rel_a.at[h], ra_recv.at[h])
        dest = nxt(y, 1 + 2 * h, NY)
        for i in range(2):
            part_a[dest, 2 * h + i] += rel_a[h, i]
        a_copy(dest, h, h).start()

    def b_later(k):
        yy = row_at(k)
        e = lax.rem(yy, 2)
        xx = nxt(x, 1 + 2 * e, NX)
        take(rel_b.at[yy], rb_recv.at[yy])
        part_b[xx, yy] += rel_b[yy]
        b_copy(xx, yy, e).start()

    each(0, NY - 1, b_later)

    plane_loss[p] = lossv[...]

    def l_start(k):
        slot = plane_loss.at[p]
        rcopy(slot, slot, l_send.at[0], l_recv.at[0], (nxt(p, k, NP), j)).start()

    each(1, NP, l_start)

    gw_copy.wait_recv()
    for h in range(CB // CH):
        s = slice(h * CH, (h + 1) * CH)
        u, inv = unit_cols(wraw[c, :, s])
        g = gw[c, :, s] + gw_in[:, s]
        gp_all[:, s] = inv * (g - u * jnp.sum(u * g, axis=0, keepdims=True))

    my_cols = pl.ds(pl.multiple_of(p * CB, CB), CB)

    def gp_copy(k):
        q = nxt(p, k, NP)
        rows = pl.ds(pl.multiple_of(q * DB, DB), DB)
        return rcopy(gp_all.at[rows], gp_ref.at[:, my_cols], gp_send.at[0], gp_recv.at[0], (q, j))

    def a_sum(xp):
        take(in_a.at[pl.ds(0, 2), pl.ds(2 * xp, 2)], a_recv.at[xp])
        for h in range(2):
            xx = 2 * xp + h
            sum_a[xx] = part_a[y, xx] + in_a[0, xx] + in_a[1, xx]

            @pl.when(xx != x)
            def _():
                a2_copy(xx, x).start()

    def a2_copy(xx, src):
        return rcopy(sum_a.at[xx], in_a2.at[src], a2_send.at[0], a2_recv.at[0], (dp_of(y, xx), j))

    def b_sum(yy, n):
        take(in_b.at[pl.ds(0, n), yy], b_recv.at[yy])
        t = part_b[x, yy]
        for k in range(n):
            t = t + in_b[k, yy]
        sum_b[yy] = t

    def b2_copy(yy, src):
        return rcopy(sum_b.at[yy], in_b2.at[src], b2_send.at[0], b2_recv.at[0], (dp_of(yy, x), j))

    def b_next(k):
        yy = row_at(k)
        b_sum(yy, 2)
        b2_copy(yy, y).start()

    each(0, NY - 1, b_next)
    each(0, HX, a_sum)
    b_sum(y, 3)
    gp_own = pltpu.make_async_copy(gp_all.at[w_rows], gp_ref.at[:, my_cols], own_sem.at[1])
    gp_own.start()

    take(plane_loss.at[pl.ds(0, NP - 1)], l_recv.at[0])
    loss_part = plane_loss[0]
    for q in range(1, NP):
        loss_part = loss_part + plane_loss[q]

    loss_row = jnp.sum(loss_part, axis=0, keepdims=True)

    su, sinv = unit_cols(feats[1, y, x])
    for q in range(NJ):
        msg[q, DB + 1:DB + 2, :] = sinv
        msg[q, DB + 2:DB + 3, :] = loss_row
        msg[q, DB + 3:, :] = jnp.zeros((5, SH), F32)
    take(in_a2.at[pl.ds(0, NX - 1)], a2_recv.at[0])
    take(in_b2.at[pl.ds(0, NY - 1)], b2_recv.at[0])
    ga, gb = sum_a[x], sum_b[y]
    for k in range(1, NX):
        ga = ga + in_a2[nxt(x, k, NX)]
        gb = gb + in_b2[nxt(y, k, NY)]
    dots = jnp.sum(su[:DH] * ga, axis=0, keepdims=True) + jnp.sum(su[DH:] * gb, axis=0, keepdims=True)

    for q in range(NJ):
        lo = q * DB
        msg[q, :DB, :] = ga[lo:lo + DB] if lo < DH else gb[lo - DH:lo - DH + DB]
        msg[q, DB:DB + 1, :] = dots

    def m_copy(q, src):
        return rcopy(msg.at[q], msg_in.at[src], m_send.at[0], m_recv.at[0], (p, q))

    for q in proto_peers():
        m_copy(q, j).start()
    each(1, NP, lambda k: gp_copy(k).start())
    msg_in[j] = msg[j]

    take(msg_in.at[pl.ds(0, NJ - 1)], m_recv.at[0])
    loss_sum = jnp.zeros((1, SH), F32)
    for h in range(2):
        t = msg_in[h]
        for q in range(1, NZ):
            t = t + msg_in[2 * q + h]
        loss_sum = loss_sum + t[DB + 2:DB + 3]
        dsum = t[DB:DB + 1]
        inv = msg_in[h, DB + 1:DB + 2, :]
        own = s_ref[:, h * SH:(h + 1) * SH].astype(F32) * inv
        gs_ref[:, h * SH:(h + 1) * SH] = inv * (t[:DB] - own * dsum)
    loss_ref[0, 0] = -inv_rows * jnp.sum(loss_sum)

    take(gp_all.at[pl.ds(0, D - DB)], gp_recv.at[0])
    gp_own.wait()

    w_core.wait_send()
    gw_copy.wait_send()
    for r in range(ITERS + 1):
        if r < ITERS:
            take(core_col.at[r, 0], cc_send.at[r])
        take(plane_row.at[r, pl.ds(0, NP - 1)], pr_send.at[r])
        take(z_row.at[r, pl.ds(0, NZ - 1)], zr_send.at[r])
    for arr in range(2):
        take(feats.at[arr, 0, 0, pl.ds(0, D - DB)], f_send.at[arr])
        for h in range(2):
            take(base.at[0, pl.ds(0, ag_rows)], ag_send.at[arr, h])
    take(wraw.at[0, pl.ds(0, D - DB)], w_send.at[0])
    take(gp_all.at[pl.ds(0, D - DB)], gp_send.at[0])
    take(plane_loss.at[pl.ds(0, NP - 1)], l_send.at[0])
    take(msg_in.at[pl.ds(0, NJ - 1)], m_send.at[0])
    take(in_a2.at[pl.ds(0, NX - 1)], a2_send.at[0])
    take(in_b2.at[pl.ds(0, NY - 1)], b2_send.at[0])
    take(in_a.at[pl.ds(0, NY - 1)], a_send.at[0])
    take(in_b.at[pl.ds(0, NX - 1)], b_send.at[0])

def body(cfg, teacher_feats, student_feats, prototypes):
    NP, NJ, NY, NX, _, _ = cfg
    NZ = NJ // 2
    SB, DB = teacher_feats.shape
    SH = SB // 2
    D = DB * NJ
    DH = D // 2
    WC = prototypes.shape[1]
    CB = WC // NP
    PC = 2 * CB
    NB = NP // 2
    V, S = pltpu.VMEM, pltpu.SemaphoreType.DMA
    scratch = [
        V((DB, SB), BF16), V((DB, SB), BF16),
        V((2, NY, NX, D, SH), BF16), V((2, D, CB), BF16), V((2, D, CB), BF16), V((2, CB, D), BF16),
        V((NB, D, SB), BF16), V((NB, PC, SB), F32), V((NB, PC, SB), F32), V((PC, SH), F32),
        V((PC, SH), F32), V((NP, SH), F32), V((NP, SH), F32), V((PC, SB), BF16), V((8, SH), F32),
        V((ITERS, 2, 1, PC), F32), V((ITERS + 1, NP, NP, SH), F32), V((ITERS + 1, NZ, NP, SH), F32),
        V((2, D, CB), F32), V((D, CB), F32), V((D, CB), F32),
        V((NY, NX, DH, SH), F32), V((NX, NY, DH, SH), F32), V((2, 2, DH, SH), F32), V((NY, DH, SH), F32),
        V((NY, NX, DH, SH), F32), V((NX, NY, DH, SH), F32),
        V((NX, DH, SH), F32), V((NY, DH, SH), F32), V((NX, DH, SH), F32), V((NY, DH, SH), F32),
        V((NJ, DB + 8, SH), F32), V((NJ, DB + 8, SH), F32), V((NP, 8, SH), F32),
        S((2,)), S((2,)), S((1,)), S((1,)), S((2,)), S((2, 2)), S((2, NY, NX)), S((2, 2)), S((4,)),
        S((ITERS,)), S((ITERS,)), S((ITERS + 1,)), S((ITERS + 1,)), S((ITERS + 1,)), S((ITERS + 1,)),
        S((2,)), S((1,)), S((1,)),
        S((2,)), S((NY,)), S((1,)), S((NX // 2,)), S((1,)), S((NY,)), S((1,)), S((1,)), S((1,)), S((1,)),
        S((1,)), S((1,)), S((1,)), S((1,)),
    ]
    vmem = pl.BlockSpec(memory_space=pltpu.VMEM)
    hbm = pl.BlockSpec(memory_space=pl.ANY)
    loss, gp, gs = pl.pallas_call(
        functools.partial(kernel, cfg),
        out_shape=(
            jax.ShapeDtypeStruct((1, 1), F32),
            pltpu.VMEM((DB, WC), F32),
            pltpu.VMEM((DB, SB), F32),
        ),
        in_specs=[hbm, hbm, hbm],
        out_specs=(pl.BlockSpec(memory_space=pltpu.SMEM), vmem, vmem),
        scratch_shapes=scratch,
        compiler_params=pltpu.CompilerParams(
            collective_id=0, has_side_effects=True, vmem_limit_bytes=56 * 1024 * 1024
        ),
    )(teacher_feats.T, student_feats.T, prototypes)
    return loss[0, 0], gp, gs.T


def solution(mesh):
    NP, NJ = mesh.shape["dp"], mesh.shape["proto"]
    NY = NX = int(round(NP ** 0.5))

    def run(teacher_feats, student_feats, prototypes):
        rows, protos = teacher_feats.shape[0], prototypes.shape[1]
        loss_scale = rows * protos // 256
        factor = float(loss_scale) / float(rows) / STUDENT_TEMP
        cfg = (NP, NJ, NY, NX, factor, 1.0 / rows)
        spec = P("dp", "proto")
        return jax.shard_map(
            functools.partial(body, cfg), mesh=mesh, in_specs=(spec,) * 3,
            out_specs=(P(), spec, spec), check_vma=False,
        )(teacher_feats, student_feats, prototypes)

    return run
```

```python
import functools

import jax
import jax.numpy as jnp
from jax import lax
from jax.experimental import pallas as pl
from jax.experimental.pallas import tpu as pltpu
from jax.sharding import PartitionSpec as P

ITERS = 3
EPS = 1e-06
TEACHER_TEMP = 0.07
STUDENT_TEMP = 0.1
MESH = pl.DeviceIdType.MESH
F32 = jnp.float32
BF16 = jnp.bfloat16


def rcopy(src, dst, send_sem, recv_sem, dev):
    return pltpu.make_async_remote_copy(
        src_ref=src, dst_ref=dst, send_sem=send_sem, recv_sem=recv_sem,
        device_id=dev, device_id_type=MESH,
    )


def take(ref, sem):
    pltpu.make_async_copy(ref, ref, sem).wait()


def each(lo, hi, fn):
    def step(k, carry):
        fn(k)
        return carry
    lax.fori_loop(lo, hi, step, 0)


def dot(a, b, dims=((1,), (0,))):
    return lax.dot_general(a, b, (dims, ((), ())), preferred_element_type=F32)


def kernel(
    cfg, t_hbm, s_hbm, w_ref, loss_ref, gp_ref, gs_ref,
    t_ref, s_ref,
    feats, wraw, wn, wtn, sn, base, logit, acc, colb, rscale, tots, gbuf, lossv,
    core_col, plane_row, z_row, gw, gw_in, gp_all,
    part_a, part_b, rel_a, rel_b, in_a, in_b, sum_a, sum_b, in_a2, in_b2, msg, msg_in, plane_loss,
    f_send, f_recv, w_send, w_recv, wc_sem, ag_send, ag_recv, ag_recv_s, own_sem,
    cc_send, cc_recv, pr_send, pr_recv, zr_send, zr_recv, gw_sem, gp_send, gp_recv,
    ra_recv, rb_recv, a_send, a_recv, b_send, b_recv, a2_send, a2_recv, b2_send, b2_recv,
    m_send, m_recv, l_send, l_recv,
):
    NP, NJ, NY, NX, factor, inv_rows = cfg
    NZ = NJ // 2
    DB = t_ref.shape[0]
    SH = t_ref.shape[1] // 2
    CB = wraw.shape[2]
    D = DB * NJ
    DH = D // 2
    PC = 2 * CB
    CH = min(256, CB)
    HX = NX // 2
    ag_rows = (NP - 1) * DH * SH // 2 // (2 * SH)
    p = lax.axis_index("dp")
    j = lax.axis_index("proto")
    y, x = p // NX, lax.rem(p, NX)
    z, c = j // 2, lax.rem(j, 2)
    oc = 1 - c
    peer = (p, 2 * z + oc)

    def dp_of(yy, xx):
        return yy * NX + xx

    def nxt(v, k, n):
        return lax.rem(v + k, n)

    def hops(k, n):
        return min(k, n - k)

    plane_off = sorted(
        ((dy, dx) for dy in range(NY) for dx in range(NX) if dy + dx > 0),
        key=lambda o: -hops(o[0], NY) - hops(o[1], NX))
    z_off = sorted(range(1, NZ), key=lambda k: -hops(k, NZ))

    def plane_peers():
        return [dp_of(nxt(y, dy, NY), nxt(x, dx, NX)) for dy, dx in plane_off]

    def proto_peers():
        return [2 * nxt(z, k, NZ) + cc for k in z_off for cc in (c, oc)] + [2 * z + oc]

    barrier = pltpu.get_barrier_semaphore()

    def greet_dp(k):
        pl.semaphore_signal(barrier, inc=1, device_id=(nxt(p, k, NP), j), device_id_type=MESH)

    def greet_proto(k):
        pl.semaphore_signal(barrier, inc=1, device_id=(p, nxt(j, k, NJ)), device_id_type=MESH)

    each(1, NP, greet_dp)
    each(1, NJ, greet_proto)
    t_in = pltpu.make_async_copy(t_hbm, t_ref, own_sem.at[2])
    s_in = pltpu.make_async_copy(s_hbm, s_ref, own_sem.at[3])
    t_in.start()
    s_in.start()
    pl.semaphore_wait(barrier, NP + NJ - 2)
    t_in.wait()
    s_in.wait()

    my_rows = pl.ds(pl.multiple_of(j * DB, DB), DB)
    my_half = pl.ds(pl.multiple_of(c * SH, SH), SH)

    def feat_copy(arr, q):
        lanes = pl.ds(pl.multiple_of(lax.rem(q, 2) * SH, SH), SH)
        src = (t_ref, s_ref)[arr].at[:, lanes]
        return rcopy(src, feats.at[arr, y, x, my_rows], f_send.at[arr], f_recv.at[arr], (p, q))

    for q in proto_peers():
        feat_copy(0, q).start()

    w_rows = pl.ds(pl.multiple_of(p * DB, DB), DB)

    def w_copy(k):
        q = nxt(p, k, NP)
        cols = pl.ds(pl.multiple_of(q * CB, CB), CB)
        return rcopy(w_ref.at[:, cols], wraw.at[c, w_rows], w_send.at[0], w_recv.at[0], (q, j))

    each(1, NP, lambda k: w_copy(k).start())
    feats[0, y, x, my_rows, :] = t_ref[:, my_half]
    feats[1, y, x, my_rows, :] = s_ref[:, my_half]
    w_own = pltpu.make_async_copy(
        w_ref.at[:, pl.ds(pl.multiple_of(p * CB, CB), CB)], wraw.at[c, w_rows], own_sem.at[0])
    w_own.start()

    def feat_wait(arr):
        take(feats.at[arr, y, x, pl.ds(0, D - DB)], f_recv.at[arr])

    near = sorted(range(1, NX), key=lambda k: min(k, NX - k))

    def ag_copy(arr, h, ys, xs, stage, dev):
        slot = feats.at[arr, ys, xs, pl.ds(h * DH, DH)]
        sem = ag_recv.at[h, ys, xs] if arr == 0 else ag_recv_s.at[h, stage]
        return rcopy(slot, slot, ag_send.at[arr, h], sem, dev)

    def ag_wait(arr, h, ys, xs):
        take(feats.at[arr, ys, xs, pl.ds(h * DH, DH)], ag_recv.at[h, ys, xs])

    def own_out(arr):
        for k in near:
            ag_copy(arr, 0, y, x, 0, (dp_of(y, nxt(x, k, NX)), j)).start()
            ag_copy(arr, 1, y, x, 0, (dp_of(nxt(y, k, NY), x), j)).start()
        for k in near:
            ag_copy(arr, 0, y, x, 1, (dp_of(nxt(y, k, NY), x), j)).start()
            ag_copy(arr, 1, y, x, 1, (dp_of(y, nxt(x, k, NX)), j)).start()

    def forward(arr):
        if arr == 1:
            for h in range(2):
                take(feats.at[1, 0, pl.ds(0, NX - 1), pl.ds(0, DH)], ag_recv_s.at[h, 0])
        for k in near:
            xs, ys = nxt(x, k, NX), nxt(y, k, NY)
            if arr == 0:
                ag_wait(0, 0, y, xs)
            each(1, NY, lambda m: ag_copy(arr, 0, y, xs, 1, (dp_of(nxt(y, m, NY), x), j)).start())
            if arr == 0:
                ag_wait(0, 1, ys, x)
            each(1, NX, lambda m: ag_copy(arr, 1, ys, x, 1, (dp_of(y, nxt(x, m, NX)), j)).start())

    def pair_wait(arr, yy, xp):
        def one(xx):
            @pl.when(yy != y)
            def _():
                @pl.when(xx != x)
                def _():
                    ag_wait(arr, 0, yy, xx)
                    ag_wait(arr, 1, yy, xx)

                @pl.when(xx == x)
                def _():
                    ag_wait(arr, 0, yy, xx)

            @pl.when(jnp.logical_and(yy == y, xx != x))
            def _():
                ag_wait(arr, 1, yy, xx)

        one(2 * xp)
        one(2 * xp + 1)

    feat_wait(0)
    own_out(0)
    each(1, NJ, lambda k: feat_copy(1, nxt(j, k, NJ)).start())

    take(wraw.at[c, pl.ds(0, D - DB)], w_recv.at[0])
    w_own.wait()
    w_core = rcopy(wraw.at[c], wraw.at[c], wc_sem.at[0], wc_sem.at[1], peer)
    w_core.start()
    forward(0)

    def unit_cols(v):
        v32 = v.astype(F32)
        inv = lax.rsqrt(jnp.sum(v32 * v32, axis=0, keepdims=True) + EPS)
        return v32 * inv, inv

    def w_norm(cc):
        for h in range(CB // CH):
            u, _ = unit_cols(wraw[cc, :, h * CH:(h + 1) * CH])
            wn[cc, :, h * CH:(h + 1) * CH] = u.astype(BF16)
            wtn[cc, h * CH:(h + 1) * CH, :] = u.T.astype(BF16)

    w_norm(c)
    w_core.wait_recv()
    w_norm(oc)

    chunks = [(cc, h) for cc in range(2) for h in range(CB // CH)]

    def two(a):
        return jnp.concatenate([a, a], axis=1)

    acc[...] = jnp.zeros_like(acc)

    def teacher_rows(k):
        yy = nxt(y, k + k // 2 - 2 * (k // 3), NY)

        def pair(xp):
            pair_wait(0, yy, xp)
            b = yy * HX + xp
            raw = jnp.concatenate([feats[0, yy, 2 * xp], feats[0, yy, 2 * xp + 1]], axis=1)
            u, _ = unit_cols(raw)
            tn = u.astype(BF16)
            for i, (cc, h) in enumerate(chunks):
                rows = slice(i * CH, (i + 1) * CH)
                e = jnp.exp(dot(wtn[cc, h * CH:(h + 1) * CH, :], tn) * (1.0 / TEACHER_TEMP))
                base[b, rows, :] = e
                acc[rows, :] += e[:, :SH] + e[:, SH:]

        each(0, HX, pair)

    each(0, NY, teacher_rows)
    feat_wait(1)
    own_out(1)

    def student_rows(yy):

        def pair(xp):
            b = yy * HX + xp

            raw = jnp.concatenate([feats[1, yy, 2 * xp], feats[1, yy, 2 * xp + 1]], axis=1)
            u, _ = unit_cols(raw)
            un = u.astype(BF16)
            sn[b] = un
            part = jnp.zeros((8, 2 * SH), F32)
            for i, (cc, h) in enumerate(chunks):
                rows = slice(i * CH, (i + 1) * CH)
                v = dot(wtn[cc, h * CH:(h + 1) * CH, :], un) * (1.0 / STUDENT_TEMP)
                logit[b, rows, :] = v
                part = part + jnp.sum(jnp.exp(v).reshape(CH // 8, 8, 2 * SH), axis=0)
            tot = jnp.sum(part, axis=0, keepdims=True)
            q = yy * NX + 2 * xp
            plane_row[ITERS, p, pl.ds(q, 1), :] = tot[:, :SH]
            plane_row[ITERS, p, pl.ds(q + 1, 1), :] = tot[:, SH:]

        each(0, HX, pair)

    def col_exchange(r):
        for i in range(PC // 128):
            core_col[r, c, :, i * 128:(i + 1) * 128] = jnp.sum(
                acc[i * 128:(i + 1) * 128, :].T, axis=0, keepdims=True)
        cp = rcopy(core_col.at[r, c], core_col.at[r, c], cc_send.at[r], cc_recv.at[r], peer)
        cp.start()
        cp.wait_recv()
        for i in range(PC // 128):
            s = slice(i * 128, (i + 1) * 128)
            v = 1.0 / (core_col[r, 0, :, s] + core_col[r, 1, :, s])
            colb[s, :] = jnp.broadcast_to(v, (128, 128)).T

    def col_pass():
        scale = rscale[...]

        def block(i):
            rows = pl.ds(pl.multiple_of(i * 64, 64), 64)
            a = jnp.zeros((64, SH), F32)
            for b in range(NP // 2):
                for h in range(2):
                    a = a + base[b, rows, h * SH:(h + 1) * SH] * scale[2 * b + h:2 * b + h + 1, :]
            acc[rows, :] = a

        each(0, PC // 64, block)

    def row_pass(r):
        def pair(b):
            for h in range(2):
                a = jnp.zeros((8, SH), F32)
                for i in range(PC // 64):
                    rows = slice(i * 64, (i + 1) * 64)
                    v = base[b, rows, h * SH:(h + 1) * SH] * colb[rows, :]
                    a = a + jnp.sum(v.reshape(8, 8, SH), axis=0)
                plane_row[r, p, pl.ds(2 * b + h, 1), :] = jnp.sum(a, axis=0, keepdims=True)

        each(0, NP // 2, pair)

    def plane_start(r):
        slot = plane_row.at[r, p]
        for q in plane_peers():
            rcopy(slot, slot, pr_send.at[r], pr_recv.at[r], (q, j)).start()

    def plane_end(r):
        take(plane_row.at[r, pl.ds(0, NP - 1)], pr_recv.at[r])
        total = plane_row[r, 0]
        for q in range(1, NP):
            total = total + plane_row[r, q]
        z_row[r, z] = total

    def z_start(r):
        slot = z_row.at[r, z]
        for k in z_off:
            rcopy(slot, slot, zr_send.at[r], zr_recv.at[r], (p, 2 * nxt(z, k, NZ) + c)).start()

    def z_end(r):
        take(z_row.at[r, pl.ds(0, NZ - 1)], zr_recv.at[r])
        total = z_row[r, 0]
        for q in range(1, NZ):
            total = total + z_row[r, q]
        return total

    for r in range(ITERS):
        if r > 0:
            col_pass()
        col_exchange(r)
        row_pass(r)
        plane_start(r)
        if r == 1:
            for h in range(2):
                take(feats.at[1, pl.ds(0, NY - 1), :, pl.ds(0, DH)], ag_recv_s.at[h, 1])
            each(0, NY, student_rows)
        if r == 2:
            plane_end(ITERS)
            z_start(ITERS)
        plane_end(r)
        z_start(r)
        if r == 0:
            forward(1)
        if r == 1:
            plane_start(ITERS)
        rscale[...] = 1.0 / z_end(r)
    tots[...] = z_end(ITERS)

    lossv[...] = jnp.zeros_like(lossv)
    gw[...] = jnp.zeros_like(gw)

    def row_of(ref, q):
        return jnp.concatenate([ref[pl.ds(q, 1), :], ref[pl.ds(q + 1, 1), :]], axis=1)

    def a_copy(yy, xp, slot):
        xs = pl.ds(2 * xp, 2)
        return rcopy(part_a.at[yy, xs], in_a.at[slot, xs], a_send.at[0], a_recv.at[xp], (dp_of(yy, x), j))

    def a_relay(yy, xp):
        dev = (dp_of(nxt(y, 1 + 2 * xp, NY), x), j)
        return rcopy(part_a.at[yy, pl.ds(2 * xp, 2)], rel_a.at[xp], a_send.at[0], ra_recv.at[xp], dev)

    def b_copy(xx, yy, slot):
        return rcopy(part_b.at[xx, yy], in_b.at[slot, yy], b_send.at[0], b_recv.at[yy], (dp_of(y, xx), j))

    def b_relay(xx, yy, e):
        dev = (dp_of(y, nxt(x, 1 + 2 * e, NX)), j)
        return rcopy(part_b.at[xx, yy], rel_b.at[yy], b_send.at[0], rb_recv.at[yy], dev)

    def row_at(k):
        n = NY - 1 - k
        return nxt(y, n + n // 2 - 2 * (n // 3), NY)

    def grad_rows(k):
        yy = row_at(k)
        e = lax.rem(yy, 2)

        def pair(xp):
            b = yy * HX + xp
            q = yy * NX + 2 * xp
            rs = row_of(rscale, q)
            tot = row_of(tots, q)
            inv_tot = 1.0 / tot
            log_tot = jnp.log(tot)
            lsum = jnp.zeros((8, 2 * SH), F32)
            for i in range(PC // CH):
                rows = slice(i * CH, (i + 1) * CH)
                lg = logit[b, rows, :]
                target = base[b, rows, :] * rs * two(colb[rows, :])
                lsum = lsum + jnp.sum((target * (lg - log_tot)).reshape(CH // 8, 8, 2 * SH), axis=0)
                gbuf[rows, :] = ((jnp.exp(lg) * inv_tot - target) * factor).astype(BF16)
            lossv[...] += lsum[:, :SH] + lsum[:, SH:]
            gs = dot(wn[0], gbuf[:CB, :]) + dot(wn[1], gbuf[CB:, :])
            part_a[yy, 2 * xp] = gs[:DH, :SH]
            part_a[yy, 2 * xp + 1] = gs[:DH, SH:]
            part_b[2 * xp, yy] = gs[DH:, :SH]
            part_b[2 * xp + 1, yy] = gs[DH:, SH:]

            @pl.when(k == 0)
            def _():
                a_relay(yy, xp).start()

            @pl.when(k == xp + 1)
            def _():
                a_copy(yy, xp, 1 - xp).start()

            for h in range(2):
                xx = 2 * xp + h
                d = lax.rem(xx - x + NX, NX)

                @pl.when(jnp.logical_and(k < NY - 1, d == 2))
                def _():
                    b_relay(xx, yy, e).start()

                @pl.when(jnp.logical_and(k == NY - 1, d == 2))
                def _():
                    b_copy(xx, yy, 2).start()

                @pl.when(d == 3 - 2 * e)
                def _():
                    b_copy(xx, yy, 1 - e).start()

                @pl.when(jnp.logical_and(k == NY - 1, d == 1 + 2 * e))
                def _():
                    b_copy(xx, yy, e).start()

            un = sn[b]
            for i, (cc, h) in enumerate(chunks):
                gw[cc, :, h * CH:(h + 1) * CH] += dot(un, gbuf[i * CH:(i + 1) * CH, :], ((1,), (1,)))

        each(0, HX, pair)

    each(0, NY, grad_rows)

    gw_copy = rcopy(gw.at[oc], gw_in, gw_sem.at[0], gw_sem.at[1], peer)
    gw_copy.start()
    for h in range(2):
        take(rel_a.at[h], ra_recv.at[h])
        dest = nxt(y, 1 + 2 * h, NY)
        for i in range(2):
            part_a[dest, 2 * h + i] += rel_a[h, i]
        a_copy(dest, h, h).start()

    def b_later(k):
        yy = row_at(k)
        e = lax.rem(yy, 2)
        xx = nxt(x, 1 + 2 * e, NX)
        take(rel_b.at[yy], rb_recv.at[yy])
        part_b[xx, yy] += rel_b[yy]
        b_copy(xx, yy, e).start()

    each(0, NY - 1, b_later)

    plane_loss[p] = lossv[...]

    def l_start(k):
        slot = plane_loss.at[p]
        rcopy(slot, slot, l_send.at[0], l_recv.at[0], (nxt(p, k, NP), j)).start()

    each(1, NP, l_start)

    gw_copy.wait_recv()
    for h in range(CB // CH):
        s = slice(h * CH, (h + 1) * CH)
        u, inv = unit_cols(wraw[c, :, s])
        g = gw[c, :, s] + gw_in[:, s]
        gp_all[:, s] = inv * (g - u * jnp.sum(u * g, axis=0, keepdims=True))

    my_cols = pl.ds(pl.multiple_of(p * CB, CB), CB)

    def gp_copy(k):
        q = nxt(p, k, NP)
        rows = pl.ds(pl.multiple_of(q * DB, DB), DB)
        return rcopy(gp_all.at[rows], gp_ref.at[:, my_cols], gp_send.at[0], gp_recv.at[0], (q, j))

    def a_sum(xp):
        take(in_a.at[pl.ds(0, 2), pl.ds(2 * xp, 2)], a_recv.at[xp])
        for h in range(2):
            xx = 2 * xp + h
            sum_a[xx] = part_a[y, xx] + in_a[0, xx] + in_a[1, xx]

            @pl.when(xx != x)
            def _():
                a2_copy(xx, x).start()

    def a2_copy(xx, src):
        return rcopy(sum_a.at[xx], in_a2.at[src], a2_send.at[0], a2_recv.at[0], (dp_of(y, xx), j))

    def b_sum(yy, n):
        take(in_b.at[pl.ds(0, n), yy], b_recv.at[yy])
        t = part_b[x, yy]
        for k in range(n):
            t = t + in_b[k, yy]
        sum_b[yy] = t

    def b2_copy(yy, src):
        return rcopy(sum_b.at[yy], in_b2.at[src], b2_send.at[0], b2_recv.at[0], (dp_of(yy, x), j))

    def b_next(k):
        yy = row_at(k)
        b_sum(yy, 2)
        b2_copy(yy, y).start()

    each(0, NY - 1, b_next)
    each(0, HX, a_sum)
    b_sum(y, 3)
    gp_own = pltpu.make_async_copy(gp_all.at[w_rows], gp_ref.at[:, my_cols], own_sem.at[1])
    gp_own.start()

    take(plane_loss.at[pl.ds(0, NP - 1)], l_recv.at[0])
    loss_part = plane_loss[0]
    for q in range(1, NP):
        loss_part = loss_part + plane_loss[q]

    loss_row = jnp.sum(loss_part, axis=0, keepdims=True)

    su, sinv = unit_cols(feats[1, y, x])
    for q in range(NJ):
        msg[q, DB + 1:DB + 2, :] = sinv
        msg[q, DB + 2:DB + 3, :] = loss_row
        msg[q, DB + 3:, :] = jnp.zeros((5, SH), F32)
    take(in_a2.at[pl.ds(0, NX - 1)], a2_recv.at[0])
    take(in_b2.at[pl.ds(0, NY - 1)], b2_recv.at[0])
    ga, gb = sum_a[x], sum_b[y]
    for k in range(1, NX):
        ga = ga + in_a2[nxt(x, k, NX)]
        gb = gb + in_b2[nxt(y, k, NY)]
    dots = jnp.sum(su[:DH] * ga, axis=0, keepdims=True) + jnp.sum(su[DH:] * gb, axis=0, keepdims=True)

    for q in range(NJ):
        lo = q * DB
        msg[q, :DB, :] = ga[lo:lo + DB] if lo < DH else gb[lo - DH:lo - DH + DB]
        msg[q, DB:DB + 1, :] = dots

    def m_copy(q, src):
        return rcopy(msg.at[q], msg_in.at[src], m_send.at[0], m_recv.at[0], (p, q))

    for q in proto_peers():
        m_copy(q, j).start()
    each(1, NP, lambda k: gp_copy(k).start())
    msg_in[j] = msg[j]

    take(msg_in.at[pl.ds(0, NJ - 1)], m_recv.at[0])
    loss_sum = jnp.zeros((1, SH), F32)
    for h in range(2):
        t = msg_in[h]
        for q in range(1, NZ):
            t = t + msg_in[2 * q + h]
        loss_sum = loss_sum + t[DB + 2:DB + 3]
        dsum = t[DB:DB + 1]
        inv = msg_in[h, DB + 1:DB + 2, :]
        own = s_ref[:, h * SH:(h + 1) * SH].astype(F32) * inv
        gs_ref[:, h * SH:(h + 1) * SH] = inv * (t[:DB] - own * dsum)
    loss_ref[0, 0] = -inv_rows * jnp.sum(loss_sum)

    take(gp_all.at[pl.ds(0, D - DB)], gp_recv.at[0])
    gp_own.wait()

    w_core.wait_send()
    gw_copy.wait_send()
    for r in range(ITERS + 1):
        if r < ITERS:
            take(core_col.at[r, 0], cc_send.at[r])
        take(plane_row.at[r, pl.ds(0, NP - 1)], pr_send.at[r])
        take(z_row.at[r, pl.ds(0, NZ - 1)], zr_send.at[r])
    for arr in range(2):
        take(feats.at[arr, 0, 0, pl.ds(0, D - DB)], f_send.at[arr])
        for h in range(2):
            take(base.at[0, pl.ds(0, ag_rows)], ag_send.at[arr, h])
    take(wraw.at[0, pl.ds(0, D - DB)], w_send.at[0])
    take(gp_all.at[pl.ds(0, D - DB)], gp_send.at[0])
    take(plane_loss.at[pl.ds(0, NP - 1)], l_send.at[0])
    take(msg_in.at[pl.ds(0, NJ - 1)], m_send.at[0])
    take(in_a2.at[pl.ds(0, NX - 1)], a2_send.at[0])
    take(in_b2.at[pl.ds(0, NY - 1)], b2_send.at[0])
    take(in_a.at[pl.ds(0, NY - 1)], a_send.at[0])
    take(in_b.at[pl.ds(0, NX - 1)], b_send.at[0])

def body(cfg, teacher_feats, student_feats, prototypes):
    NP, NJ, NY, NX, _, _ = cfg
    NZ = NJ // 2
    SB, DB = teacher_feats.shape
    SH = SB // 2
    D = DB * NJ
    DH = D // 2
    WC = prototypes.shape[1]
    CB = WC // NP
    PC = 2 * CB
    NB = NP // 2
    V, S = pltpu.VMEM, pltpu.SemaphoreType.DMA
    scratch = [
        V((DB, SB), BF16), V((DB, SB), BF16),
        V((2, NY, NX, D, SH), BF16), V((2, D, CB), BF16), V((2, D, CB), BF16), V((2, CB, D), BF16),
        V((NB, D, SB), BF16), V((NB, PC, SB), F32), V((NB, PC, SB), F32), V((PC, SH), F32),
        V((PC, SH), F32), V((NP, SH), F32), V((NP, SH), F32), V((PC, SB), BF16), V((8, SH), F32),
        V((ITERS, 2, 1, PC), F32), V((ITERS + 1, NP, NP, SH), F32), V((ITERS + 1, NZ, NP, SH), F32),
        V((2, D, CB), F32), V((D, CB), F32), V((D, CB), F32),
        V((NY, NX, DH, SH), F32), V((NX, NY, DH, SH), F32), V((2, 2, DH, SH), F32), V((NY, DH, SH), F32),
        V((NY, NX, DH, SH), F32), V((NX, NY, DH, SH), F32),
        V((NX, DH, SH), F32), V((NY, DH, SH), F32), V((NX, DH, SH), F32), V((NY, DH, SH), F32),
        V((NJ, DB + 8, SH), F32), V((NJ, DB + 8, SH), F32), V((NP, 8, SH), F32),
        S((2,)), S((2,)), S((1,)), S((1,)), S((2,)), S((2, 2)), S((2, NY, NX)), S((2, 2)), S((4,)),
        S((ITERS,)), S((ITERS,)), S((ITERS + 1,)), S((ITERS + 1,)), S((ITERS + 1,)), S((ITERS + 1,)),
        S((2,)), S((1,)), S((1,)),
        S((2,)), S((NY,)), S((1,)), S((NX // 2,)), S((1,)), S((NY,)), S((1,)), S((1,)), S((1,)), S((1,)),
        S((1,)), S((1,)), S((1,)), S((1,)),
    ]
    vmem = pl.BlockSpec(memory_space=pltpu.VMEM)
    hbm = pl.BlockSpec(memory_space=pl.ANY)
    loss, gp, gs = pl.pallas_call(
        functools.partial(kernel, cfg),
        out_shape=(
            jax.ShapeDtypeStruct((1, 1), F32),
            pltpu.VMEM((DB, WC), F32),
            pltpu.VMEM((DB, SB), F32),
        ),
        in_specs=[hbm, hbm, hbm],
        out_specs=(pl.BlockSpec(memory_space=pltpu.SMEM), vmem, vmem),
        scratch_shapes=scratch,
        compiler_params=pltpu.CompilerParams(
            collective_id=0, has_side_effects=True, vmem_limit_bytes=56 * 1024 * 1024
        ),
    )(teacher_feats.T, student_feats.T, prototypes)
    return loss[0, 0], gp, gs.T


def solution(mesh):
    NP, NJ = mesh.shape["dp"], mesh.shape["proto"]
    NY = NX = int(round(NP ** 0.5))

    def run(teacher_feats, student_feats, prototypes):
        rows, protos = teacher_feats.shape[0], prototypes.shape[1]
        loss_scale = rows * protos // 256
        factor = float(loss_scale) / float(rows) / STUDENT_TEMP
        cfg = (NP, NJ, NY, NX, factor, 1.0 / rows)
        spec = P("dp", "proto")
        return jax.shard_map(
            functools.partial(body, cfg), mesh=mesh, in_specs=(spec,) * 3,
            out_specs=(P(), spec, spec), check_vma=False,
        )(teacher_feats, student_feats, prototypes)

    return run
```

```python
import functools

import jax
import jax.numpy as jnp
from jax import lax
from jax.experimental import pallas as pl
from jax.experimental.pallas import tpu as pltpu
from jax.sharding import PartitionSpec as P

ITERS = 3
EPS = 1e-06
TEACHER_TEMP = 0.07
STUDENT_TEMP = 0.1
MESH = pl.DeviceIdType.MESH
F32 = jnp.float32
BF16 = jnp.bfloat16


def rcopy(src, dst, send_sem, recv_sem, dev):
    return pltpu.make_async_remote_copy(
        src_ref=src, dst_ref=dst, send_sem=send_sem, recv_sem=recv_sem,
        device_id=dev, device_id_type=MESH,
    )


def take(ref, sem):
    pltpu.make_async_copy(ref, ref, sem).wait()


def each(lo, hi, fn):
    def step(k, carry):
        fn(k)
        return carry
    lax.fori_loop(lo, hi, step, 0)


def dot(a, b, dims=((1,), (0,))):
    return lax.dot_general(a, b, (dims, ((), ())), preferred_element_type=F32)


def kernel(
    cfg, t_hbm, s_hbm, w_ref, loss_ref, gp_ref, gs_ref,
    t_ref, s_ref,
    feats, wraw, wn, wtn, sn, base, logit, acc, colb, rscale, tots, gbuf, lossv,
    core_col, plane_row, z_row, gw, gw_in, gp_all,
    part_a, part_b, rel_a, rel_b, in_a, in_b, sum_a, sum_b, in_a2, in_b2, msg, msg_in, plane_loss,
    f_send, f_recv, w_send, w_recv, wc_sem, ag_send, ag_recv, ag_recv_s, own_sem,
    cc_send, cc_recv, pr_send, pr_recv, zr_send, zr_recv, gw_sem, gp_send, gp_recv,
    ra_recv, rb_recv, a_send, a_recv, b_send, b_recv, a2_send, a2_recv, b2_send, b2_recv,
    m_send, m_recv, l_send, l_recv,
):
    NP, NJ, NY, NX, factor, inv_rows = cfg
    NZ = NJ // 2
    DB = t_ref.shape[0]
    SH = t_ref.shape[1] // 2
    CB = wraw.shape[2]
    D = DB * NJ
    DH = D // 2
    PC = 2 * CB
    CH = min(256, CB)
    HX = NX // 2
    ag_rows = (NP - 1) * DH * SH // 2 // (2 * SH)
    p = lax.axis_index("dp")
    j = lax.axis_index("proto")
    y, x = p // NX, lax.rem(p, NX)
    z, c = j // 2, lax.rem(j, 2)
    oc = 1 - c
    peer = (p, 2 * z + oc)

    def dp_of(yy, xx):
        return yy * NX + xx

    def nxt(v, k, n):
        return lax.rem(v + k, n)

    def hops(k, n):
        return min(k, n - k)

    plane_off = sorted(
        ((dy, dx) for dy in range(NY) for dx in range(NX) if dy + dx > 0),
        key=lambda o: -hops(o[0], NY) - hops(o[1], NX))
    z_off = sorted(range(1, NZ), key=lambda k: -hops(k, NZ))

    def plane_peers():
        return [dp_of(nxt(y, dy, NY), nxt(x, dx, NX)) for dy, dx in plane_off]

    def proto_peers():
        return [2 * nxt(z, k, NZ) + cc for k in z_off for cc in (c, oc)] + [2 * z + oc]

    barrier = pltpu.get_barrier_semaphore()

    def greet_dp(k):
        pl.semaphore_signal(barrier, inc=1, device_id=(nxt(p, k, NP), j), device_id_type=MESH)

    def greet_proto(k):
        pl.semaphore_signal(barrier, inc=1, device_id=(p, nxt(j, k, NJ)), device_id_type=MESH)

    each(1, NP, greet_dp)
    each(1, NJ, greet_proto)
    t_in = pltpu.make_async_copy(t_hbm, t_ref, own_sem.at[2])
    s_in = pltpu.make_async_copy(s_hbm, s_ref, own_sem.at[3])
    t_in.start()
    s_in.start()
    pl.semaphore_wait(barrier, NP + NJ - 2)
    t_in.wait()
    s_in.wait()

    my_rows = pl.ds(pl.multiple_of(j * DB, DB), DB)
    my_half = pl.ds(pl.multiple_of(c * SH, SH), SH)

    def feat_copy(arr, q):
        lanes = pl.ds(pl.multiple_of(lax.rem(q, 2) * SH, SH), SH)
        src = (t_ref, s_ref)[arr].at[:, lanes]
        return rcopy(src, feats.at[arr, y, x, my_rows], f_send.at[arr], f_recv.at[arr], (p, q))

    for q in proto_peers():
        feat_copy(0, q).start()

    w_rows = pl.ds(pl.multiple_of(p * DB, DB), DB)

    def w_copy(k):
        q = nxt(p, k, NP)
        cols = pl.ds(pl.multiple_of(q * CB, CB), CB)
        return rcopy(w_ref.at[:, cols], wraw.at[c, w_rows], w_send.at[0], w_recv.at[0], (q, j))

    each(1, NP, lambda k: w_copy(k).start())
    each(1, NJ, lambda k: feat_copy(1, nxt(j, k, NJ)).start())
    feats[0, y, x, my_rows, :] = t_ref[:, my_half]
    feats[1, y, x, my_rows, :] = s_ref[:, my_half]
    w_own = pltpu.make_async_copy(
        w_ref.at[:, pl.ds(pl.multiple_of(p * CB, CB), CB)], wraw.at[c, w_rows], own_sem.at[0])
    w_own.start()

    def feat_wait(arr):
        take(feats.at[arr, y, x, pl.ds(0, D - DB)], f_recv.at[arr])

    near = sorted(range(1, NX), key=lambda k: min(k, NX - k))

    def ag_copy(arr, h, ys, xs, stage, dev):
        slot = feats.at[arr, ys, xs, pl.ds(h * DH, DH)]
        sem = ag_recv.at[h, ys, xs] if arr == 0 else ag_recv_s.at[h, stage]
        return rcopy(slot, slot, ag_send.at[arr, h], sem, dev)

    def ag_wait(arr, h, ys, xs):
        take(feats.at[arr, ys, xs, pl.ds(h * DH, DH)], ag_recv.at[h, ys, xs])

    def own_out(arr):
        for k in near:
            ag_copy(arr, 0, y, x, 0, (dp_of(y, nxt(x, k, NX)), j)).start()
            ag_copy(arr, 1, y, x, 0, (dp_of(nxt(y, k, NY), x), j)).start()
        for k in near:
            ag_copy(arr, 0, y, x, 1, (dp_of(nxt(y, k, NY), x), j)).start()
            ag_copy(arr, 1, y, x, 1, (dp_of(y, nxt(x, k, NX)), j)).start()

    def forward(arr):
        if arr == 1:
            for h in range(2):
                take(feats.at[1, 0, pl.ds(0, NX - 1), pl.ds(0, DH)], ag_recv_s.at[h, 0])
        for k in near:
            xs, ys = nxt(x, k, NX), nxt(y, k, NY)
            if arr == 0:
                ag_wait(0, 0, y, xs)
            each(1, NY, lambda m: ag_copy(arr, 0, y, xs, 1, (dp_of(nxt(y, m, NY), x), j)).start())
            if arr == 0:
                ag_wait(0, 1, ys, x)
            each(1, NX, lambda m: ag_copy(arr, 1, ys, x, 1, (dp_of(y, nxt(x, m, NX)), j)).start())

    def pair_wait(arr, yy, xp):
        def one(xx):
            @pl.when(yy != y)
            def _():
                @pl.when(xx != x)
                def _():
                    ag_wait(arr, 0, yy, xx)
                    ag_wait(arr, 1, yy, xx)

                @pl.when(xx == x)
                def _():
                    ag_wait(arr, 0, yy, xx)

            @pl.when(jnp.logical_and(yy == y, xx != x))
            def _():
                ag_wait(arr, 1, yy, xx)

        one(2 * xp)
        one(2 * xp + 1)

    feat_wait(0)
    own_out(0)

    take(wraw.at[c, pl.ds(0, D - DB)], w_recv.at[0])
    w_own.wait()
    w_core = rcopy(wraw.at[c], wraw.at[c], wc_sem.at[0], wc_sem.at[1], peer)
    w_core.start()
    forward(0)

    def unit_cols(v):
        v32 = v.astype(F32)
        inv = lax.rsqrt(jnp.sum(v32 * v32, axis=0, keepdims=True) + EPS)
        return v32 * inv, inv

    def w_norm(cc):
        for h in range(CB // CH):
            u, _ = unit_cols(wraw[cc, :, h * CH:(h + 1) * CH])
            wn[cc, :, h * CH:(h + 1) * CH] = u.astype(BF16)
            wtn[cc, h * CH:(h + 1) * CH, :] = u.T.astype(BF16)

    w_norm(c)
    w_core.wait_recv()
    w_norm(oc)

    chunks = [(cc, h) for cc in range(2) for h in range(CB // CH)]

    def two(a):
        return jnp.concatenate([a, a], axis=1)

    acc[...] = jnp.zeros_like(acc)

    def teacher_rows(k):
        yy = nxt(y, k + k // 2 - 2 * (k // 3), NY)

        def pair(xp):
            pair_wait(0, yy, xp)
            b = yy * HX + xp
            raw = jnp.concatenate([feats[0, yy, 2 * xp], feats[0, yy, 2 * xp + 1]], axis=1)
            u, _ = unit_cols(raw)
            tn = u.astype(BF16)
            for i, (cc, h) in enumerate(chunks):
                rows = slice(i * CH, (i + 1) * CH)
                e = jnp.exp(dot(wtn[cc, h * CH:(h + 1) * CH, :], tn) * (1.0 / TEACHER_TEMP))
                base[b, rows, :] = e
                acc[rows, :] += e[:, :SH] + e[:, SH:]

        each(0, HX, pair)

    each(0, NY, teacher_rows)
    feat_wait(1)
    own_out(1)

    def student_rows(yy):

        def pair(xp):
            b = yy * HX + xp

            raw = jnp.concatenate([feats[1, yy, 2 * xp], feats[1, yy, 2 * xp + 1]], axis=1)
            u, _ = unit_cols(raw)
            un = u.astype(BF16)
            sn[b] = un
            part = jnp.zeros((8, 2 * SH), F32)
            for i, (cc, h) in enumerate(chunks):
                rows = slice(i * CH, (i + 1) * CH)
                v = dot(wtn[cc, h * CH:(h + 1) * CH, :], un) * (1.0 / STUDENT_TEMP)
                logit[b, rows, :] = v
                part = part + jnp.sum(jnp.exp(v).reshape(CH // 8, 8, 2 * SH), axis=0)
            tot = jnp.sum(part, axis=0, keepdims=True)
            q = yy * NX + 2 * xp
            plane_row[ITERS, p, pl.ds(q, 1), :] = tot[:, :SH]
            plane_row[ITERS, p, pl.ds(q + 1, 1), :] = tot[:, SH:]

        each(0, HX, pair)

    def col_exchange(r):
        for i in range(PC // 128):
            core_col[r, c, :, i * 128:(i + 1) * 128] = jnp.sum(
                acc[i * 128:(i + 1) * 128, :].T, axis=0, keepdims=True)
        cp = rcopy(core_col.at[r, c], core_col.at[r, c], cc_send.at[r], cc_recv.at[r], peer)
        cp.start()
        cp.wait_recv()
        for i in range(PC // 128):
            s = slice(i * 128, (i + 1) * 128)
            v = 1.0 / (core_col[r, 0, :, s] + core_col[r, 1, :, s])
            colb[s, :] = jnp.broadcast_to(v, (128, 128)).T

    def col_pass():
        scale = rscale[...]

        def block(i):
            rows = pl.ds(pl.multiple_of(i * 64, 64), 64)
            a = jnp.zeros((64, SH), F32)
            for b in range(NP // 2):
                for h in range(2):
                    a = a + base[b, rows, h * SH:(h + 1) * SH] * scale[2 * b + h:2 * b + h + 1, :]
            acc[rows, :] = a

        each(0, PC // 64, block)

    def row_pass(r):
        def pair(b):
            for h in range(2):
                a = jnp.zeros((8, SH), F32)
                for i in range(PC // 64):
                    rows = slice(i * 64, (i + 1) * 64)
                    v = base[b, rows, h * SH:(h + 1) * SH] * colb[rows, :]
                    a = a + jnp.sum(v.reshape(8, 8, SH), axis=0)
                plane_row[r, p, pl.ds(2 * b + h, 1), :] = jnp.sum(a, axis=0, keepdims=True)

        each(0, NP // 2, pair)

    def plane_start(r):
        slot = plane_row.at[r, p]
        for q in plane_peers():
            rcopy(slot, slot, pr_send.at[r], pr_recv.at[r], (q, j)).start()

    def plane_end(r):
        take(plane_row.at[r, pl.ds(0, NP - 1)], pr_recv.at[r])
        total = plane_row[r, 0]
        for q in range(1, NP):
            total = total + plane_row[r, q]
        z_row[r, z] = total

    def z_start(r):
        slot = z_row.at[r, z]
        for k in z_off:
            rcopy(slot, slot, zr_send.at[r], zr_recv.at[r], (p, 2 * nxt(z, k, NZ) + c)).start()

    def z_end(r):
        take(z_row.at[r, pl.ds(0, NZ - 1)], zr_recv.at[r])
        total = z_row[r, 0]
        for q in range(1, NZ):
            total = total + z_row[r, q]
        return total

    for r in range(ITERS):
        if r > 0:
            col_pass()
        col_exchange(r)
        row_pass(r)
        plane_start(r)
        if r == 1:
            for h in range(2):
                take(feats.at[1, pl.ds(0, NY - 1), :, pl.ds(0, DH)], ag_recv_s.at[h, 1])
            each(0, NY, student_rows)
        if r == 2:
            plane_end(ITERS)
            z_start(ITERS)
        plane_end(r)
        z_start(r)
        if r == 0:
            forward(1)
        if r == 1:
            plane_start(ITERS)
        rscale[...] = 1.0 / z_end(r)
    tots[...] = z_end(ITERS)

    lossv[...] = jnp.zeros_like(lossv)
    gw[...] = jnp.zeros_like(gw)

    def row_of(ref, q):
        return jnp.concatenate([ref[pl.ds(q, 1), :], ref[pl.ds(q + 1, 1), :]], axis=1)

    def a_copy(yy, xp, slot):
        xs = pl.ds(2 * xp, 2)
        return rcopy(part_a.at[yy, xs], in_a.at[slot, xs], a_send.at[0], a_recv.at[xp], (dp_of(yy, x), j))

    def a_relay(yy, xp):
        dev = (dp_of(nxt(y, 1 + 2 * xp, NY), x), j)
        return rcopy(part_a.at[yy, pl.ds(2 * xp, 2)], rel_a.at[xp], a_send.at[0], ra_recv.at[xp], dev)

    def b_copy(xx, yy, slot):
        return rcopy(part_b.at[xx, yy], in_b.at[slot, yy], b_send.at[0], b_recv.at[yy], (dp_of(y, xx), j))

    def b_relay(xx, yy, e):
        dev = (dp_of(y, nxt(x, 1 + 2 * e, NX)), j)
        return rcopy(part_b.at[xx, yy], rel_b.at[yy], b_send.at[0], rb_recv.at[yy], dev)

    def row_at(k):
        n = NY - 1 - k
        return nxt(y, n + n // 2 - 2 * (n // 3), NY)

    def grad_rows(k):
        yy = row_at(k)
        e = lax.rem(yy, 2)

        def pair(xp):
            b = yy * HX + xp
            q = yy * NX + 2 * xp
            rs = row_of(rscale, q)
            tot = row_of(tots, q)
            inv_tot = 1.0 / tot
            log_tot = jnp.log(tot)
            lsum = jnp.zeros((8, 2 * SH), F32)
            for i in range(PC // CH):
                rows = slice(i * CH, (i + 1) * CH)
                lg = logit[b, rows, :]
                target = base[b, rows, :] * rs * two(colb[rows, :])
                lsum = lsum + jnp.sum((target * (lg - log_tot)).reshape(CH // 8, 8, 2 * SH), axis=0)
                gbuf[rows, :] = ((jnp.exp(lg) * inv_tot - target) * factor).astype(BF16)
            lossv[...] += lsum[:, :SH] + lsum[:, SH:]
            gs = dot(wn[0], gbuf[:CB, :]) + dot(wn[1], gbuf[CB:, :])
            part_a[yy, 2 * xp] = gs[:DH, :SH]
            part_a[yy, 2 * xp + 1] = gs[:DH, SH:]
            part_b[2 * xp, yy] = gs[DH:, :SH]
            part_b[2 * xp + 1, yy] = gs[DH:, SH:]

            @pl.when(k == 0)
            def _():
                a_relay(yy, xp).start()

            @pl.when(k == xp + 1)
            def _():
                a_copy(yy, xp, 1 - xp).start()

            for h in range(2):
                xx = 2 * xp + h
                d = lax.rem(xx - x + NX, NX)

                @pl.when(jnp.logical_and(k < NY - 1, d == 2))
                def _():
                    b_relay(xx, yy, e).start()

                @pl.when(jnp.logical_and(k == NY - 1, d == 2))
                def _():
                    b_copy(xx, yy, 2).start()

                @pl.when(d == 3 - 2 * e)
                def _():
                    b_copy(xx, yy, 1 - e).start()

                @pl.when(jnp.logical_and(k == NY - 1, d == 1 + 2 * e))
                def _():
                    b_copy(xx, yy, e).start()

            un = sn[b]
            for i, (cc, h) in enumerate(chunks):
                gw[cc, :, h * CH:(h + 1) * CH] += dot(un, gbuf[i * CH:(i + 1) * CH, :], ((1,), (1,)))

        each(0, HX, pair)

    each(0, NY, grad_rows)

    gw_copy = rcopy(gw.at[oc], gw_in, gw_sem.at[0], gw_sem.at[1], peer)
    gw_copy.start()
    for h in range(2):
        take(rel_a.at[h], ra_recv.at[h])
        dest = nxt(y, 1 + 2 * h, NY)
        for i in range(2):
            part_a[dest, 2 * h + i] += rel_a[h, i]
        a_copy(dest, h, h).start()

    def b_later(k):
        yy = row_at(k)
        e = lax.rem(yy, 2)
        xx = nxt(x, 1 + 2 * e, NX)
        take(rel_b.at[yy], rb_recv.at[yy])
        part_b[xx, yy] += rel_b[yy]
        b_copy(xx, yy, e).start()

    for k in range(NY - 1):
        b_later(k)

    plane_loss[p] = lossv[...]

    def l_start(k):
        slot = plane_loss.at[p]
        rcopy(slot, slot, l_send.at[0], l_recv.at[0], (nxt(p, k, NP), j)).start()

    each(1, NP, l_start)

    gw_copy.wait_recv()
    for h in range(CB // CH):
        s = slice(h * CH, (h + 1) * CH)
        u, inv = unit_cols(wraw[c, :, s])
        g = gw[c, :, s] + gw_in[:, s]
        gp_all[:, s] = inv * (g - u * jnp.sum(u * g, axis=0, keepdims=True))

    my_cols = pl.ds(pl.multiple_of(p * CB, CB), CB)

    def gp_copy(k):
        q = nxt(p, k, NP)
        rows = pl.ds(pl.multiple_of(q * DB, DB), DB)
        return rcopy(gp_all.at[rows], gp_ref.at[:, my_cols], gp_send.at[0], gp_recv.at[0], (q, j))

    def a_sum(xp):
        take(in_a.at[pl.ds(0, 2), pl.ds(2 * xp, 2)], a_recv.at[xp])
        for h in range(2):
            xx = 2 * xp + h
            sum_a[xx] = part_a[y, xx] + in_a[0, xx] + in_a[1, xx]

            @pl.when(xx != x)
            def _():
                a2_copy(xx, x).start()

    def a2_copy(xx, src):
        return rcopy(sum_a.at[xx], in_a2.at[src], a2_send.at[0], a2_recv.at[0], (dp_of(y, xx), j))

    def b_sum(yy, n):
        take(in_b.at[pl.ds(0, n), yy], b_recv.at[yy])
        t = part_b[x, yy]
        for k in range(n):
            t = t + in_b[k, yy]
        sum_b[yy] = t

    def b2_copy(yy, src):
        return rcopy(sum_b.at[yy], in_b2.at[src], b2_send.at[0], b2_recv.at[0], (dp_of(yy, x), j))

    def b_next(k):
        yy = row_at(k)
        b_sum(yy, 2)
        b2_copy(yy, y).start()

    for k in range(NY - 1):
        b_next(k)
    for xp in range(HX):
        a_sum(xp)
    b_sum(y, 3)
    gp_own = pltpu.make_async_copy(gp_all.at[w_rows], gp_ref.at[:, my_cols], own_sem.at[1])
    gp_own.start()

    take(plane_loss.at[pl.ds(0, NP - 1)], l_recv.at[0])
    loss_part = plane_loss[0]
    for q in range(1, NP):
        loss_part = loss_part + plane_loss[q]

    loss_row = jnp.sum(loss_part, axis=0, keepdims=True)

    su, sinv = unit_cols(feats[1, y, x])
    for q in range(NJ):
        msg[q, DB + 1:DB + 2, :] = sinv
        msg[q, DB + 2:DB + 3, :] = loss_row
        msg[q, DB + 3:, :] = jnp.zeros((5, SH), F32)
    take(in_a2.at[pl.ds(0, NX - 1)], a2_recv.at[0])
    take(in_b2.at[pl.ds(0, NY - 1)], b2_recv.at[0])
    ga, gb = sum_a[x], sum_b[y]
    for k in range(1, NX):
        ga = ga + in_a2[nxt(x, k, NX)]
        gb = gb + in_b2[nxt(y, k, NY)]
    dots = jnp.sum(su[:DH] * ga, axis=0, keepdims=True) + jnp.sum(su[DH:] * gb, axis=0, keepdims=True)

    for q in range(NJ):
        lo = q * DB
        msg[q, :DB, :] = ga[lo:lo + DB] if lo < DH else gb[lo - DH:lo - DH + DB]
        msg[q, DB:DB + 1, :] = dots

    def m_copy(q, src):
        return rcopy(msg.at[q], msg_in.at[src], m_send.at[0], m_recv.at[0], (p, q))

    for q in proto_peers():
        m_copy(q, j).start()
    each(1, NP, lambda k: gp_copy(k).start())
    msg_in[j] = msg[j]

    take(msg_in.at[pl.ds(0, NJ - 1)], m_recv.at[0])
    loss_sum = jnp.zeros((1, SH), F32)
    for h in range(2):
        t = msg_in[h]
        for q in range(1, NZ):
            t = t + msg_in[2 * q + h]
        loss_sum = loss_sum + t[DB + 2:DB + 3]
        dsum = t[DB:DB + 1]
        inv = msg_in[h, DB + 1:DB + 2, :]
        own = s_ref[:, h * SH:(h + 1) * SH].astype(F32) * inv
        gs_ref[:, h * SH:(h + 1) * SH] = inv * (t[:DB] - own * dsum)
    loss_ref[0, 0] = -inv_rows * jnp.sum(loss_sum)

    take(gp_all.at[pl.ds(0, D - DB)], gp_recv.at[0])
    gp_own.wait()

    w_core.wait_send()
    gw_copy.wait_send()
    for r in range(ITERS + 1):
        if r < ITERS:
            take(core_col.at[r, 0], cc_send.at[r])
        take(plane_row.at[r, pl.ds(0, NP - 1)], pr_send.at[r])
        take(z_row.at[r, pl.ds(0, NZ - 1)], zr_send.at[r])
    for arr in range(2):
        take(feats.at[arr, 0, 0, pl.ds(0, D - DB)], f_send.at[arr])
        for h in range(2):
            take(base.at[0, pl.ds(0, ag_rows)], ag_send.at[arr, h])
    take(wraw.at[0, pl.ds(0, D - DB)], w_send.at[0])
    take(gp_all.at[pl.ds(0, D - DB)], gp_send.at[0])
    take(plane_loss.at[pl.ds(0, NP - 1)], l_send.at[0])
    take(msg_in.at[pl.ds(0, NJ - 1)], m_send.at[0])
    take(in_a2.at[pl.ds(0, NX - 1)], a2_send.at[0])
    take(in_b2.at[pl.ds(0, NY - 1)], b2_send.at[0])
    take(in_a.at[pl.ds(0, NY - 1)], a_send.at[0])
    take(in_b.at[pl.ds(0, NX - 1)], b_send.at[0])

def body(cfg, teacher_feats, student_feats, prototypes):
    NP, NJ, NY, NX, _, _ = cfg
    NZ = NJ // 2
    SB, DB = teacher_feats.shape
    SH = SB // 2
    D = DB * NJ
    DH = D // 2
    WC = prototypes.shape[1]
    CB = WC // NP
    PC = 2 * CB
    NB = NP // 2
    V, S = pltpu.VMEM, pltpu.SemaphoreType.DMA
    scratch = [
        V((DB, SB), BF16), V((DB, SB), BF16),
        V((2, NY, NX, D, SH), BF16), V((2, D, CB), BF16), V((2, D, CB), BF16), V((2, CB, D), BF16),
        V((NB, D, SB), BF16), V((NB, PC, SB), F32), V((NB, PC, SB), F32), V((PC, SH), F32),
        V((PC, SH), F32), V((NP, SH), F32), V((NP, SH), F32), V((PC, SB), BF16), V((8, SH), F32),
        V((ITERS, 2, 1, PC), F32), V((ITERS + 1, NP, NP, SH), F32), V((ITERS + 1, NZ, NP, SH), F32),
        V((2, D, CB), F32), V((D, CB), F32), V((D, CB), F32),
        V((NY, NX, DH, SH), F32), V((NX, NY, DH, SH), F32), V((2, 2, DH, SH), F32), V((NY, DH, SH), F32),
        V((NY, NX, DH, SH), F32), V((NX, NY, DH, SH), F32),
        V((NX, DH, SH), F32), V((NY, DH, SH), F32), V((NX, DH, SH), F32), V((NY, DH, SH), F32),
        V((NJ, DB + 8, SH), F32), V((NJ, DB + 8, SH), F32), V((NP, 8, SH), F32),
        S((2,)), S((2,)), S((1,)), S((1,)), S((2,)), S((2, 2)), S((2, NY, NX)), S((2, 2)), S((4,)),
        S((ITERS,)), S((ITERS,)), S((ITERS + 1,)), S((ITERS + 1,)), S((ITERS + 1,)), S((ITERS + 1,)),
        S((2,)), S((1,)), S((1,)),
        S((2,)), S((NY,)), S((1,)), S((NX // 2,)), S((1,)), S((NY,)), S((1,)), S((1,)), S((1,)), S((1,)),
        S((1,)), S((1,)), S((1,)), S((1,)),
    ]
    vmem = pl.BlockSpec(memory_space=pltpu.VMEM)
    hbm = pl.BlockSpec(memory_space=pl.ANY)
    loss, gp, gs = pl.pallas_call(
        functools.partial(kernel, cfg),
        out_shape=(
            jax.ShapeDtypeStruct((1, 1), F32),
            pltpu.VMEM((DB, WC), F32),
            pltpu.VMEM((DB, SB), F32),
        ),
        in_specs=[hbm, hbm, hbm],
        out_specs=(pl.BlockSpec(memory_space=pltpu.SMEM), vmem, vmem),
        scratch_shapes=scratch,
        compiler_params=pltpu.CompilerParams(
            collective_id=0, has_side_effects=True, vmem_limit_bytes=56 * 1024 * 1024
        ),
    )(teacher_feats.T, student_feats.T, prototypes)
    return loss[0, 0], gp, gs.T


def solution(mesh):
    NP, NJ = mesh.shape["dp"], mesh.shape["proto"]
    NY = NX = int(round(NP ** 0.5))

    def run(teacher_feats, student_feats, prototypes):
        rows, protos = teacher_feats.shape[0], prototypes.shape[1]
        loss_scale = rows * protos // 256
        factor = float(loss_scale) / float(rows) / STUDENT_TEMP
        cfg = (NP, NJ, NY, NX, factor, 1.0 / rows)
        spec = P("dp", "proto")
        return jax.shard_map(
            functools.partial(body, cfg), mesh=mesh, in_specs=(spec,) * 3,
            out_specs=(P(), spec, spec), check_vma=False,
        )(teacher_feats, student_feats, prototypes)

    return run
```
